32 devices in a mesh: prompt: 1, seq: 32 (over z, y, x, core).
Axes of the slice: x: 2, y: 2, z: 4, core: 2. Of those that a mesh axis runs over, the one named last changes fastest.
Arguments:
- queries: bfloat16 [8192, 32, 128], P(('prompt', 'seq')), may hold values from -12 to 12
- key_value: bfloat16 [2, 8192, 16, 128], P(None, ('prompt', 'seq')), may hold values from -6 to 6
- damping: bfloat16 [8192], P('prompt'), may hold values from 0.0099487305 to 1
- span_start: int32 [1], P('prompt'), may hold values from 0 to 3584
- steered_heads: int32 [8], replicated, may hold values from 0 to 31, as said below
Outputs:
- attention: bfloat16 [8192, 32, 128], P(('prompt', 'seq'))
The draws below stay inside these ranges and needn't reach their ends.
Inputs may be any that keep to these rules, and one draw needn't show every extreme that they name: The emphasized tokens are span_start to span_start + 511. `steered_heads`: 8 distinct head numbers in any order; head 31 is always one of them.
All inputs are finite; a program needn't handle non-finite values.
Results may differ from the reference program's by a relative error of at most 0.0085.
Values may be sent and summed in bfloat16 or wider, within the bound.
No kernel may reach another device: no remote copies, remote signals or barrier semaphores. Data moves between devices by JAX's collectives and lax.ppermute only.
A program may use at most 64 MiB of HBM per device.

```python
import math
import jax
import jax.numpy as jnp
from jax import lax

HEADS = 32
KV_HEADS = 16
HEAD_DIM = 128
WINDOW = 4096
SPAN = 512
STEERED = 8
TOKENS = 8192


def draw_steered_heads(key, part):
    others = jax.random.permutation(jax.random.fold_in(key, 11), HEADS - 1)[:STEERED - 1].astype(jnp.int32)
    chosen = jnp.concatenate([others, jnp.full((1,), HEADS - 1, jnp.int32)])
    order = jax.random.permutation(jax.random.fold_in(key, 23), STEERED)
    return chosen[order].astype(jnp.int32)


def shard_levels(own_key, shape, shards, least, high):
    loudness = 1.0
    for axis_at, blocks in shards:
        heights = jax.random.uniform(jax.random.fold_in(jax.random.fold_in(own_key, 6), axis_at), (blocks,), jnp.float32, least / len(shards), high / len(shards))
        loudness = loudness * jnp.repeat(jnp.exp(heights), shape[axis_at] // blocks).reshape((-1,) + (1,) * (len(shape) - 1 - axis_at))
    return loudness


def centred(rng, dims, spread, bound, split=(), held_as=jnp.bfloat16):
    factor_of = shard_levels(rng, dims, split, -0.22, 0.18) if split else 1.0
    values = jax.random.normal(rng, dims, jnp.float32) * spread * factor_of
    return jnp.minimum(jnp.maximum(values, -bound), bound).astype(held_as)


def setup_inputs(seed: int = 0, part: int = 0) -> dict:
    seeds = jax.random.split(jax.random.key(seed), 6)
    part_keys = jax.random.split(jax.random.fold_in(seeds[5], part), 6)
    queries = centred(part_keys[0], (TOKENS, HEADS, HEAD_DIM), 3.0, 12.0, ((0, 32),))
    key_value = centred(part_keys[1], (2, TOKENS, KV_HEADS, HEAD_DIM), 1.0, 6.0, ((1, 32),))
    damping = jnp.clip(jnp.exp(jax.random.uniform(part_keys[2], (TOKENS,), jnp.float32, math.log(0.0099487305), math.log(1.0))), 0.0099487305, 1.0).astype(jnp.bfloat16)
    span_start = jax.random.randint(part_keys[3], (1,), 0, max(TOKENS - WINDOW - SPAN, 0) + 1).astype(jnp.int32)
    steered_heads = draw_steered_heads(jax.random.fold_in(seeds[5], 71), part)
    return dict(queries=queries, key_value=key_value, damping=damping, span_start=span_start, steered_heads=steered_heads)


SCORE_SCALE = 144.0 ** -0.5
SOFTCAP = 50.0


def piece_terms(query_groups, key_piece, value_piece, key_bias, visible):
    raw_score = jnp.einsum("qkgd,skd->kgqs", query_groups.astype(jnp.float32), key_piece.astype(jnp.float32))
    scores = SOFTCAP * jnp.tanh(raw_score * SCORE_SCALE / SOFTCAP) + key_bias
    weight = jnp.where(visible, jnp.exp(scores), jnp.float32(0.0))
    weight_sum = jnp.sum(weight, axis=-1)
    rounded = weight.astype(jnp.bfloat16)
    weighted = jnp.einsum("kgqs,skd->kgqd", rounded.astype(jnp.float32), value_piece.astype(jnp.float32))
    return weighted, weight_sum


def reference(queries, key_value, damping, span_start, steered_heads):
    total_rows, head_count, head_width = queries.shape
    key_heads = key_value.shape[2]
    group_size = head_count // key_heads
    block_rows = min(512, total_rows)
    span_first = span_start[0].astype(jnp.int32)
    head_index = jnp.arange(head_count, dtype=jnp.int32)
    steered = jnp.any(steered_heads[:, None] == head_index[None, :], axis=0)
    steer_grid = steered.reshape(key_heads, group_size)[:, :, None, None]
    log_damping = jnp.log(damping.astype(jnp.float32))
    padded_states = jnp.pad(key_value, ((0, 0), (WINDOW, 0), (0, 0), (0, 0)))
    padded_log = jnp.pad(log_damping, (WINDOW, 0))
    span_states = lax.dynamic_slice_in_dim(key_value, span_first, SPAN, 1)
    span_index = span_first + jnp.arange(SPAN, dtype=jnp.int32)

    def one_block(block_index):
        first_row = (block_index * block_rows).astype(jnp.int32)
        query_index = first_row + jnp.arange(block_rows, dtype=jnp.int32)
        query_groups = lax.dynamic_slice_in_dim(queries, first_row, block_rows, 0).reshape(block_rows, key_heads, group_size, head_width)
        window_states = lax.dynamic_slice_in_dim(padded_states, first_row, WINDOW + block_rows, 1)
        window_log = lax.dynamic_slice_in_dim(padded_log, first_row, WINDOW + block_rows, 0)
        key_index = first_row - WINDOW + jnp.arange(WINDOW + block_rows, dtype=jnp.int32)
        emphasis = (key_index >= span_first) & (key_index < span_first + SPAN)
        distance = query_index[:, None] - key_index[None, :]
        visible = (key_index[None, :] >= 0) & (distance >= 0) & (distance < WINDOW)
        key_bias = jnp.where(steer_grid & ~emphasis[None, None, None, :], window_log[None, None, None, :], jnp.float32(0.0))
        weighted, weight_sum = piece_terms(query_groups, window_states[0], window_states[1], key_bias, visible[None, None])
        span_distance = query_index[:, None] - span_index[None, :]
        span_visible = steer_grid & (span_distance >= WINDOW)[None, None]
        more_weighted, more_sum = piece_terms(query_groups, span_states[0], span_states[1], jnp.float32(0.0), span_visible)
        result = (weighted + more_weighted) / (weight_sum + more_sum)[..., None]
        result = result.astype(jnp.bfloat16)
        return result.transpose(2, 0, 1, 3).reshape(block_rows, head_count, head_width)

    outputs = lax.map(one_block, jnp.arange(total_rows // block_rows, dtype=jnp.int32))
    return outputs.reshape(total_rows, head_count, head_width)
```

```python
import functools
import math

import jax
import jax.numpy as jnp
from jax import lax
from jax.experimental import pallas as pl
from jax.experimental.pallas import tpu as pltpu
from jax.sharding import PartitionSpec as P

WINDOW = 4096
SPAN = 512

SCORE_SCALE = 144.0 ** (-0.5)
SOFTCAP = 50.0
LOG2_E = math.log2(math.e)

GROUP = 8
VMEM_BYTES = 48 * 1024 * 1024

FIRST_SCALAR = 32
PLANE, SPAN_FIRST, STEERED_0, STEERED_1 = range(FIRST_SCALAR, FIRST_SCALAR + 4)
SCALARS = FIRST_SCALAR + 4


def smem():
    return pl.BlockSpec(memory_space=pltpu.SMEM)


def vmem():
    return pl.BlockSpec(memory_space=pltpu.VMEM)


def params():
    return pltpu.CompilerParams(vmem_limit_bytes=VMEM_BYTES)


def pack_kernel(
    index_ref, span_ref, steered_ref, queries_ref, states_ref,
    states_a, states_b, queries_a, queries_b, scalars, query_heads, state_heads,
):
    key_heads = states_ref.shape[2]
    steered_count = steered_ref.shape[0]
    steered_keys = [lax.div(steered_ref[n], 2) for n in range(steered_count)]
    flags = []
    for head in range(key_heads):
        hit = steered_keys[0] == head
        for n in range(1, steered_count):
            hit = hit | (steered_keys[n] == head)
        flags.append(hit.astype(jnp.int32))
    total = sum(flags[1:], flags[0])
    before = jnp.int32(0)
    for head in range(key_heads):
        rank = jnp.where(flags[head] == 1, before, total + head - before)
        scalars[rank] = jnp.int32(head)
        before = before + flags[head]
    place = lax.rem(index_ref[0], GROUP)
    scalars[PLANE] = lax.div(index_ref[0], GROUP)
    scalars[SPAN_FIRST] = span_ref[0]
    own_head = scalars[place]
    for group_head in range(2):
        hit = steered_ref[0] == 2 * own_head + group_head
        for n in range(1, steered_count):
            hit = hit | (steered_ref[n] == 2 * own_head + group_head)
        scalars[STEERED_0 + group_head] = hit.astype(jnp.int32)

    for part in range(2):
        state_heads[part] = jnp.transpose(states_ref[part], (1, 0, 2))
    for n in range(GROUP):
        for part in range(2):
            states_a[n, part] = state_heads[part, scalars[n]]
    for n in range(GROUP):
        for part in range(2):
            states_b[n, part] = state_heads[part, scalars[GROUP + n]]
    query_heads[...] = jnp.transpose(queries_ref[...], (1, 0, 2))
    for n in range(GROUP):
        for group_head in range(2):
            queries_a[n, group_head] = query_heads[2 * scalars[n] + group_head]
            queries_b[n, group_head] = query_heads[2 * scalars[GROUP + n] + group_head]


def pack(index, span_start, steered_heads, queries, states):
    rows, heads, width = queries.shape
    key_heads = states.shape[2]
    part = jax.ShapeDtypeStruct((GROUP, 2, rows, width), queries.dtype)
    return pl.pallas_call(
        pack_kernel,
        in_specs=[smem()] * 3 + [vmem()] * 2,
        out_specs=[vmem()] * 4 + [smem()],
        out_shape=[part] * 4 + [jax.ShapeDtypeStruct((SCALARS,), jnp.int32)],
        scratch_shapes=[
            pltpu.VMEM((heads, rows, width), queries.dtype),
            pltpu.VMEM((2, key_heads, rows, width), queries.dtype),
        ],
        compiler_params=params(),
    )(index, span_start, steered_heads, queries, states)


def tile(query, key, value, bias=None, visible=None):
    raw_score = lax.dot_general(
        query, key, (((1,), (1,)), ((), ())), preferred_element_type=jnp.float32
    )
    score = jnp.tanh(raw_score * (SCORE_SCALE / SOFTCAP)) * (SOFTCAP * LOG2_E)
    pair = (2, score.shape[0] // 2, score.shape[1])
    if bias is not None:
        score = (score.reshape(pair) + bias).reshape(score.shape)
    weight = jnp.exp2(score)
    if visible is not None:
        weight = jnp.where(visible, weight.reshape(pair), 0.0).reshape(score.shape)
    lanes = query.shape[1]
    sums = weight[:, :lanes]
    for first in range(lanes, weight.shape[1], lanes):
        sums = sums + weight[:, first : first + lanes]
    weighted = jnp.dot(
        weight.astype(jnp.bfloat16), value, preferred_element_type=jnp.float32
    )
    return weighted, sums


def attend_kernel(*refs, step, steerable, last):
    refs = list(refs)
    scalars = refs.pop(0)
    bias_ref = refs.pop(0) if steerable else None
    query_ref, states_ref = refs.pop(0), refs.pop(0)
    if step:
        old_weighted, old_sums = refs.pop(0), refs.pop(0)
    if last:
        out_ref, weighted_ref, sums_ref = refs
    else:
        weighted_ref, sums_ref = refs
    block = pl.program_id(0)
    blocks, _, rows, width = states_ref.shape
    plane = scalars[PLANE]
    first_block = (plane - step) * blocks
    query = query_ref[0].reshape(2 * rows, width)
    shape = weighted_ref.shape
    if step:
        weighted_ref[...] = old_weighted[...]
        sums_ref[...] = old_sums[...]
    else:
        weighted_ref[...] = jnp.zeros(shape, jnp.float32)
        sums_ref[...] = jnp.zeros(shape, jnp.float32)

    def head_flags():
        return [scalars[STEERED_0 + n] for n in range(2)]

    def add(key_block, visible=None):
        bias = None
        if steerable:
            row = bias_ref[pl.ds(first_block + key_block, 1), :]
            bias = jnp.stack([row * flag.astype(jnp.float32) for flag in head_flags()])
        weighted, sums = tile(
            query, states_ref[key_block, 0], states_ref[key_block, 1], bias, visible
        )
        weighted_ref[...] += weighted.reshape(shape)
        sums_ref[...] += sums.reshape(shape)

    def emphasized(key_block):
        index = (first_block + key_block) * rows + lax.broadcasted_iota(jnp.int32, (1, rows), 1)
        first = scalars[SPAN_FIRST]
        inside = (index >= first) & (index < first + SPAN)
        return jnp.stack([inside & (flag == 1) for flag in head_flags()])

    def order():
        row = lax.broadcasted_iota(jnp.int32, (rows, rows), 0)
        column = lax.broadcasted_iota(jnp.int32, (rows, rows), 1)
        return row, column

    def compute():
        if step == 0:
            lax.fori_loop(0, block, lambda n, c: (add(n), c)[1], 0)
            row, column = order()
            add(block, (row >= column)[None])
        elif step == 1:
            for n in range(blocks):
                add(n)
        else:
            lax.fori_loop(block + 1, blocks, lambda n, c: (add(n), c)[1], 0)
            row, column = order()
            if not steerable:
                add(block, (row < column)[None])
                return
            add(block, (row < column)[None] | emphasized(block))
            first = scalars[SPAN_FIRST] - first_block * rows
            low = jnp.maximum(first, 0) // rows
            high = jnp.minimum(lax.div(first + SPAN + rows - 1, rows), block)
            flags = head_flags()
            high = jnp.where(flags[0] + flags[1] > 0, high, low)
            lax.fori_loop(low, high, lambda n, c: (add(n, emphasized(n)), c)[1], 0)

    if step:
        pl.when(plane >= step)(compute)
    else:
        compute()
    if last:
        total = jnp.sum(sums_ref[...], axis=-1, keepdims=True)
        out_ref[...] = (weighted_ref[...] / total).astype(out_ref.dtype).reshape(out_ref.shape)


def attend(step, scalars, bias, queries, states, carried=None, last=False):
    blocks, pair, rows, width = queries.shape
    held = jax.ShapeDtypeStruct((blocks, pair * rows, width), jnp.float32)
    one = pl.BlockSpec((1, pair, rows, width), lambda n: (n, 0, 0, 0))
    held_spec = pl.BlockSpec((1, pair * rows, width), lambda n: (n, 0, 0))
    operands, in_specs = [scalars], [smem()]
    if bias is not None:
        operands.append(bias)
        in_specs.append(pl.BlockSpec(bias.shape, lambda n: (0, 0)))
    operands += [queries, states]
    in_specs += [one, pl.BlockSpec(states.shape, lambda n: (0, 0, 0, 0))]
    if carried is not None:
        operands += list(carried)
        in_specs += [held_spec] * 2
    scratch = []
    if last:
        out_shape, out_specs = jax.ShapeDtypeStruct(queries.shape, queries.dtype), one
        scratch = [pltpu.VMEM((1, pair * rows, width), jnp.float32)] * 2
    else:
        out_shape, out_specs = [held, held], [held_spec] * 2
    return pl.pallas_call(
        functools.partial(attend_kernel, step=step, steerable=bias is not None, last=last),
        grid=(blocks,),
        in_specs=in_specs,
        out_specs=out_specs,
        out_shape=out_shape,
        scratch_shapes=scratch,
        compiler_params=params(),
    )(*operands)


def span_kernel(scalars, query_ref, states_ref, old_weighted, old_sums, out_ref, weighted_ref, sums_ref, *, step, length):
    _, pair, rows, width = query_ref.shape
    plane = scalars[PLANE]
    weighted_ref[...] = old_weighted[0]
    sums_ref[...] = old_sums[0]
    first = scalars[SPAN_FIRST]
    flags = [scalars[STEERED_0 + n] for n in range(2)]
    wanted = (plane >= step) & (first < (plane - step + 1) * length) & (flags[0] + flags[1] > 0)

    @pl.when(wanted)
    def _():
        query = query_ref[0].reshape(pair * rows, width)
        index = (plane - step) * length + jnp.minimum(first, length - SPAN)
        index = index + lax.broadcasted_iota(jnp.int32, (1, SPAN), 1)
        inside = (index >= first) & (index < first + SPAN)
        visible = jnp.stack([inside & (flag == 1) for flag in flags])
        weighted, sums = tile(query, states_ref[0], states_ref[1], None, visible)
        weighted_ref[...] += weighted
        sums_ref[...] += sums

    total = jnp.sum(sums_ref[...], axis=-1, keepdims=True)
    out_ref[...] = (weighted_ref[...] / total).astype(out_ref.dtype).reshape(out_ref.shape)


def attend_span(step, scalars, queries, states, carried):
    blocks, pair, rows, width = queries.shape
    one = pl.BlockSpec((1, pair, rows, width), lambda n: (n, 0, 0, 0))
    held_spec = pl.BlockSpec((1, pair * rows, width), lambda n: (n, 0, 0))
    return pl.pallas_call(
        functools.partial(span_kernel, step=step, length=blocks * rows),
        grid=(blocks,),
        in_specs=[smem(), one, pl.BlockSpec(states.shape, lambda n: (0, 0, 0))] + [held_spec] * 2,
        out_specs=one,
        out_shape=jax.ShapeDtypeStruct(queries.shape, queries.dtype),
        scratch_shapes=[pltpu.VMEM((pair * rows, width), jnp.float32)] * 2,
        compiler_params=params(),
    )(scalars, queries, states, *carried)


def unpack_kernel(scalars, out_a, out_b, attention, heads_ref):
    for n in range(GROUP):
        for group_head in range(2):
            heads_ref[2 * scalars[n] + group_head] = out_a[n, group_head]
            heads_ref[2 * scalars[GROUP + n] + group_head] = out_b[n, group_head]
    attention[...] = jnp.transpose(heads_ref[...], (1, 0, 2))


def unpack(scalars, out_a, out_b):
    blocks, pair, rows, width = out_a.shape
    heads = 2 * blocks * pair
    return pl.pallas_call(
        unpack_kernel,
        in_specs=[smem()] + [vmem()] * 2,
        out_specs=vmem(),
        out_shape=jax.ShapeDtypeStruct((rows, heads, width), out_a.dtype),
        scratch_shapes=[pltpu.VMEM((heads, rows, width), out_a.dtype)],
        compiler_params=params(),
    )(scalars, out_a, out_b)


def per_device(queries, key_value, damping, span_start, steered_heads):
    rows = queries.shape[0]
    device_count = lax.axis_size("seq")
    assert WINDOW == 2 * GROUP * rows and device_count == 4 * GROUP
    assert key_value.shape[2] == 2 * GROUP and queries.shape[1] == 4 * GROUP
    assert steered_heads.shape[0] <= GROUP
    groups = [
        list(range(first, first + GROUP)) for first in range(0, device_count, GROUP)
    ]

    def exchange(blocks):
        return lax.all_to_all(
            blocks, "seq", split_axis=0, concat_axis=0, axis_index_groups=groups, tiled=True
        )

    def onward(blocks):
        pairs = [(n, n + GROUP) for n in range(device_count - GROUP)]
        return lax.ppermute(blocks, "seq", pairs)

    index = lax.axis_index("seq").astype(jnp.int32).reshape(1)
    states_a, states_b, queries_a, queries_b, scalars = pack(
        index, span_start, steered_heads, queries, key_value
    )
    position = jnp.arange(damping.shape[0], dtype=jnp.int32)
    emphasized = (position >= span_start[0]) & (position < span_start[0] + SPAN)
    bias = jnp.where(emphasized, 0.0, jnp.log2(damping.astype(jnp.float32)))
    bias = bias.reshape(-1, rows)

    states_a = exchange(states_a)
    back_a = onward(states_a)
    states_b = exchange(states_b)
    queries_a = exchange(queries_a)
    queries_b = exchange(queries_b)
    back_b = onward(states_b)
    far_a = onward(back_a)
    far_b = onward(back_b)
    length = GROUP * rows
    span_states = lax.dynamic_slice_in_dim(
        far_a.transpose(1, 0, 2, 3).reshape(2, length, -1),
        jnp.minimum(span_start[0], length - SPAN),
        SPAN,
        1,
    )
    span_states = onward(span_states)

    held_a = attend(0, scalars, bias, queries_a, states_a)
    held_b = attend(0, scalars, None, queries_b, states_b)
    held_a = attend(1, scalars, bias, queries_a, back_a, held_a)
    held_b = attend(1, scalars, None, queries_b, back_b, held_b)
    held_a = attend(2, scalars, bias, queries_a, far_a, held_a)
    out_a = attend_span(3, scalars, queries_a, span_states, held_a)
    out_a = exchange(out_a)
    out_b = attend(2, scalars, None, queries_b, far_b, held_b, last=True)
    out_b = exchange(out_b)
    return unpack(scalars, out_a, out_b)


def solution(mesh):
    in_specs = (
        P(("prompt", "seq"), None, None),
        P(None, ("prompt", "seq"), None, None),
        P("prompt"),
        P("prompt"),
        P(),
    )
    out_specs = P(("prompt", "seq"), None, None)
    return jax.shard_map(
        per_device, mesh=mesh, in_specs=in_specs, out_specs=out_specs, check_vma=False
    )
```

```python
import functools
import math

import jax
import jax.numpy as jnp
from jax import lax
from jax.experimental import pallas as pl
from jax.experimental.pallas import tpu as pltpu
from jax.sharding import PartitionSpec as P

WINDOW = 4096
SPAN = 512

SCORE_SCALE = 144.0 ** (-0.5)
SOFTCAP = 50.0
LOG2_E = math.log2(math.e)

GROUP = 8
PAIR_FLOPS = 1536
VMEM_BYTES = 48 * 1024 * 1024

FIRST_SCALAR = 32
PLANE, SPAN_FIRST, STEERED_0, STEERED_1 = range(FIRST_SCALAR, FIRST_SCALAR + 4)
SCALARS = FIRST_SCALAR + 4


def smem():
    return pl.BlockSpec(memory_space=pltpu.SMEM)


def vmem():
    return pl.BlockSpec(memory_space=pltpu.VMEM)


def params():
    return pltpu.CompilerParams(vmem_limit_bytes=VMEM_BYTES)


def cost(pairs, moved):
    return pl.CostEstimate(
        flops=int(pairs * PAIR_FLOPS), bytes_accessed=int(moved), transcendentals=int(2 * pairs)
    )


def pack_states_kernel(
    index_ref, span_ref, steered_ref, states_ref, states_a, states_b, scalars, state_heads
):
    key_heads = states_ref.shape[2]
    steered_count = steered_ref.shape[0]
    steered_keys = [lax.div(steered_ref[n], 2) for n in range(steered_count)]
    flags = []
    for head in range(key_heads):
        hit = steered_keys[0] == head
        for n in range(1, steered_count):
            hit = hit | (steered_keys[n] == head)
        flags.append(hit.astype(jnp.int32))
    total = sum(flags[1:], flags[0])
    before = jnp.int32(0)
    for head in range(key_heads):
        rank = jnp.where(flags[head] == 1, before, total + head - before)
        scalars[rank] = jnp.int32(head)
        before = before + flags[head]
    place = lax.rem(index_ref[0], GROUP)
    scalars[PLANE] = lax.div(index_ref[0], GROUP)
    scalars[SPAN_FIRST] = span_ref[0]
    own_head = scalars[place]
    for group_head in range(2):
        hit = steered_ref[0] == 2 * own_head + group_head
        for n in range(1, steered_count):
            hit = hit | (steered_ref[n] == 2 * own_head + group_head)
        scalars[STEERED_0 + group_head] = hit.astype(jnp.int32)

    for part in range(2):
        state_heads[part] = jnp.transpose(states_ref[part], (1, 0, 2))
        for n in range(GROUP):
            states_a[n, part] = state_heads[part, scalars[n]]
            states_b[n, part] = state_heads[part, scalars[GROUP + n]]


def pack_states(index, span_start, steered_heads, states):
    _, rows, key_heads, width = states.shape
    part = jax.ShapeDtypeStruct((GROUP, 2, rows, width), states.dtype)
    return pl.pallas_call(
        pack_states_kernel,
        in_specs=[smem()] * 3 + [vmem()],
        out_specs=[vmem()] * 2 + [smem()],
        out_shape=[part] * 2 + [jax.ShapeDtypeStruct((SCALARS,), jnp.int32)],
        scratch_shapes=[pltpu.VMEM((2, key_heads, rows, width), states.dtype)],
        compiler_params=params(),
        cost_estimate=cost(0, 8 * states.size),
    )(index, span_start, steered_heads, states)


def pack_queries_kernel(scalars, queries_ref, states_b, queries_a, both_b, query_heads):
    query_heads[...] = jnp.transpose(queries_ref[...], (1, 0, 2))
    for n in range(GROUP):
        for group_head in range(2):
            queries_a[n, group_head] = query_heads[2 * scalars[n] + group_head]
            both_b[n, 2 + group_head] = query_heads[2 * scalars[GROUP + n] + group_head]
            both_b[n, group_head] = states_b[n, group_head]


def pack_queries(scalars, queries, states_b):
    rows, heads, width = queries.shape
    return pl.pallas_call(
        pack_queries_kernel,
        in_specs=[smem()] + [vmem()] * 2,
        out_specs=[vmem()] * 2,
        out_shape=[
            jax.ShapeDtypeStruct((GROUP, 2, rows, width), queries.dtype),
            jax.ShapeDtypeStruct((GROUP, 4, rows, width), queries.dtype),
        ],
        scratch_shapes=[pltpu.VMEM((heads, rows, width), queries.dtype)],
        compiler_params=params(),
        cost_estimate=cost(0, 8 * queries.size),
    )(scalars, queries, states_b)


def raw_scores(query, key):
    return lax.dot_general(
        query, key, (((1,), (1,)), ((), ())), preferred_element_type=jnp.float32
    )


def weights(raw_score, bias=None, visible=None):
    score = jnp.tanh(raw_score * (SCORE_SCALE / SOFTCAP)) * (SOFTCAP * LOG2_E)
    pair = (2, score.shape[0] // 2, score.shape[1])
    if bias is not None:
        score = (score.reshape(pair) + bias).reshape(score.shape)
    weight = jnp.exp2(score)
    if visible is not None:
        weight = jnp.where(visible, weight.reshape(pair), 0.0).reshape(score.shape)
    return weight


def lane_sums(weight, lanes):
    sums = weight[:, :lanes]
    for first in range(lanes, weight.shape[1], lanes):
        sums = sums + weight[:, first : first + lanes]
    return sums


def tile(query, key, value, bias=None, visible=None):
    weight = weights(raw_scores(query, key), bias, visible)
    weighted = jnp.dot(
        weight.astype(jnp.bfloat16), value, preferred_element_type=jnp.float32
    )
    return weighted, lane_sums(weight, query.shape[1])


def attend_kernel(*refs, step, steerable, last):
    refs = list(refs)
    scalars = refs.pop(0)
    bias_ref = refs.pop(0) if steerable else None
    low_ref, high_ref, states_ref = refs.pop(0), refs.pop(0), refs.pop(0)
    if step:
        old_weighted, old_sums = refs.pop(0), refs.pop(0)
    if last:
        out_ref = refs.pop(0)
    weighted_ref, sums_ref, query_ref = refs
    low = pl.program_id(0)
    blocks, _, rows, width = states_ref.shape
    high = blocks - 1 - low
    plane = scalars[PLANE]
    first_block = (plane - step) * blocks
    query_ref[0] = low_ref[0].reshape(2 * rows, width)
    query_ref[1] = high_ref[0].reshape(2 * rows, width)
    if step:
        weighted_ref[...] = old_weighted[...]
        sums_ref[...] = old_sums[...]
    else:
        weighted_ref[...] = jnp.zeros(weighted_ref.shape, jnp.float32)
        sums_ref[...] = jnp.zeros(sums_ref.shape, jnp.float32)
    flags = [scalars[STEERED_0 + n] for n in range(2)]
    flag_values = [flag.astype(jnp.float32) for flag in flags]

    def states(part, key_block, count):
        if count == 1:
            return states_ref[key_block, part]
        return states_ref[pl.ds(key_block, count), part].reshape(count * rows, width)

    def bias(key_block, count):
        if not steerable:
            return None
        parts = [bias_ref[pl.ds(first_block + key_block + n, 1), :] for n in range(count)]
        row = parts[0] if count == 1 else jnp.concatenate(parts, axis=1)
        return jnp.stack([row * value for value in flag_values])

    def add(tiles):
        ahead = raw_scores(query_ref[tiles[0][0]], states(0, *tiles[0][1:3]))
        for n, (which, key_block, count, visible) in enumerate(tiles):
            raw_score = ahead
            if n + 1 < len(tiles):
                ahead = raw_scores(query_ref[tiles[n + 1][0]], states(0, *tiles[n + 1][1:3]))
            weight = weights(raw_score, bias(key_block, count), visible)
            sums_ref[0, which] += lane_sums(weight, width)
            weighted_ref[0, which] += jnp.dot(
                weight.astype(jnp.bfloat16),
                states(1, key_block, count),
                preferred_element_type=jnp.float32,
            )

    def emphasized(key_block):
        index = (first_block + key_block) * rows + lax.broadcasted_iota(jnp.int32, (1, rows), 1)
        first = scalars[SPAN_FIRST]
        inside = (index >= first) & (index < first + SPAN)
        return jnp.stack([inside & (flag == 1) for flag in flags])

    def compute():
        row = lax.broadcasted_iota(jnp.int32, (rows, rows), 0)
        column = lax.broadcasted_iota(jnp.int32, (rows, rows), 1)
        tiles = []
        if step == 0:
            for n in range(blocks - 1):
                is_low = n < low
                tiles.append((jnp.where(is_low, 0, 1), jnp.where(is_low, n, n - low), 1, None))
            visible = (row >= column)[None]
            tiles += [(0, low, 1, visible), (1, high, 1, visible)]
        elif step == 1:
            tiles = [(which, n, 2, None) for which in range(2) for n in range(0, blocks, 2)]
        else:
            for n in range(blocks - 1):
                is_high = n < low
                tiles.append(
                    (jnp.where(is_high, 1, 0), jnp.where(is_high, high + 1 + n, n + 1), 1, None)
                )
            visible = (row < column)[None]
            for which, block in ((0, low), (1, high)):
                seen = visible | emphasized(block) if steerable else visible
                tiles.append((which, block, 1, seen))
        add(tiles)
        if step == 2 and steerable:
            first = scalars[SPAN_FIRST] - first_block * rows
            span_low = lax.div(jnp.maximum(first, 0), rows)
            span_high = lax.div(jnp.maximum(first + SPAN + rows - 1, 0), rows)
            span_high = jnp.where(flags[0] + flags[1] > 0, span_high, 0)
            for which, block in ((0, low), (1, high)):
                lax.fori_loop(
                    span_low,
                    jnp.minimum(span_high, block),
                    lambda n, c: (add([(which, n, 1, emphasized(n))]), c)[1],
                    0,
                )

    if step:
        pl.when(plane >= step)(compute)
    else:
        compute()
    if last:
        write_result(out_ref, weighted_ref, sums_ref, low, high)


def write_result(out_ref, weighted_ref, sums_ref, low, high):
    for which, block in ((0, low), (1, high)):
        total = jnp.sum(sums_ref[0, which], axis=-1, keepdims=True)
        result = (weighted_ref[0, which] / total).astype(out_ref.dtype)
        out_ref[block] = result.reshape(out_ref.shape[1:])


def query_specs(queries):
    blocks, pair, rows, width = queries.shape
    one = (1, pair, rows, width)
    return [
        pl.BlockSpec(one, lambda n: (n, 0, 0, 0)),
        pl.BlockSpec(one, lambda n: (blocks - 1 - n, 0, 0, 0)),
    ]


def held_spec(queries):
    _, pair, rows, width = queries.shape
    return pl.BlockSpec((1, 2, pair * rows, width), lambda n: (n, 0, 0, 0))


def attend(step, scalars, bias, queries, states, carried=None, last=False):
    blocks, pair, rows, width = queries.shape
    assert blocks % 2 == 0 and pair == 2
    held = jax.ShapeDtypeStruct((blocks // 2, 2, pair * rows, width), jnp.float32)
    whole = pl.BlockSpec(states.shape, lambda n: (0, 0, 0, 0))
    operands, in_specs = [scalars], [smem()]
    if bias is not None:
        operands.append(bias)
        in_specs.append(pl.BlockSpec(bias.shape, lambda n: (0, 0)))
    operands += [queries, queries, states]
    in_specs += query_specs(queries) + [whole]
    if carried is not None:
        operands += list(carried)
        in_specs += [held_spec(queries)] * 2
    scratch = [pltpu.VMEM((2, pair * rows, width), queries.dtype)]
    if last:
        out_shape = jax.ShapeDtypeStruct(queries.shape, queries.dtype)
        out_specs = pl.BlockSpec(queries.shape, lambda n: (0, 0, 0, 0))
        scratch = [pltpu.VMEM((1, 2, pair * rows, width), jnp.float32)] * 2 + scratch
    else:
        out_shape, out_specs = [held, held], [held_spec(queries)] * 2
    return pl.pallas_call(
        functools.partial(attend_kernel, step=step, steerable=bias is not None, last=last),
        grid=(blocks // 2,),
        in_specs=in_specs,
        out_specs=out_specs,
        out_shape=out_shape,
        scratch_shapes=scratch,
        compiler_params=params(),
        cost_estimate=cost(
            pair * (blocks * rows) ** 2 / (1 if step == 1 else 2),
            8 * queries.size + 8 * pair * blocks * rows * width,
        ),
    )(*operands)


def span_kernel(
    scalars, low_ref, high_ref, states_ref, old_weighted, old_sums,
    out_ref, weighted_ref, sums_ref, *, step, length,
):
    _, pair, rows, width = low_ref.shape
    low = pl.program_id(0)
    high = 2 * pl.num_programs(0) - 1 - low
    plane = scalars[PLANE]
    weighted_ref[...] = old_weighted[...]
    sums_ref[...] = old_sums[...]
    first = scalars[SPAN_FIRST]
    flags = [scalars[STEERED_0 + n] for n in range(2)]
    wanted = (plane >= step) & (first < (plane - step + 1) * length) & (flags[0] + flags[1] > 0)

    @pl.when(wanted)
    def _():
        index = (plane - step) * length + jnp.minimum(first, length - SPAN)
        index = index + lax.broadcasted_iota(jnp.int32, (1, SPAN), 1)
        inside = (index >= first) & (index < first + SPAN)
        visible = jnp.stack([inside & (flag == 1) for flag in flags])
        for which, query_ref in enumerate((low_ref, high_ref)):
            query = query_ref[0].reshape(pair * rows, width)
            weighted, sums = tile(query, states_ref[0], states_ref[1], None, visible)
            weighted_ref[0, which] += weighted
            sums_ref[0, which] += sums

    write_result(out_ref, weighted_ref, sums_ref, low, high)


def attend_span(step, scalars, queries, states, carried):
    blocks, pair, rows, width = queries.shape
    return pl.pallas_call(
        functools.partial(span_kernel, step=step, length=blocks * rows),
        grid=(blocks // 2,),
        in_specs=[smem()]
        + query_specs(queries)
        + [pl.BlockSpec(states.shape, lambda n: (0, 0, 0))]
        + [held_spec(queries)] * 2,
        out_specs=pl.BlockSpec(queries.shape, lambda n: (0, 0, 0, 0)),
        out_shape=jax.ShapeDtypeStruct(queries.shape, queries.dtype),
        scratch_shapes=[pltpu.VMEM((1, 2, pair * rows, width), jnp.float32)] * 2,
        compiler_params=params(),
        cost_estimate=cost(pair * blocks * rows * SPAN, 8 * queries.size),
    )(scalars, queries, queries, states, *carried)


def unpack_kernel(scalars, out_a, out_b, attention, heads_ref):
    for n in range(GROUP):
        for group_head in range(2):
            heads_ref[2 * scalars[n] + group_head] = out_a[n, group_head]
            heads_ref[2 * scalars[GROUP + n] + group_head] = out_b[n, group_head]
    attention[...] = jnp.transpose(heads_ref[...], (1, 0, 2))


def unpack(scalars, out_a, out_b):
    blocks, pair, rows, width = out_a.shape
    heads = 2 * blocks * pair
    return pl.pallas_call(
        unpack_kernel,
        in_specs=[smem()] + [vmem()] * 2,
        out_specs=vmem(),
        out_shape=jax.ShapeDtypeStruct((rows, heads, width), out_a.dtype),
        scratch_shapes=[pltpu.VMEM((heads, rows, width), out_a.dtype)],
        compiler_params=params(),
    )(scalars, out_a, out_b)


def per_device(queries, key_value, damping, span_start, steered_heads):
    rows = queries.shape[0]
    device_count = lax.axis_size("seq")
    assert WINDOW == 2 * GROUP * rows and device_count == 4 * GROUP
    assert key_value.shape[2] == 2 * GROUP and queries.shape[1] == 4 * GROUP
    assert steered_heads.shape[0] <= GROUP
    groups = [
        list(range(first, first + GROUP)) for first in range(0, device_count, GROUP)
    ]

    def exchange(blocks):
        return lax.all_to_all(
            blocks, "seq", split_axis=0, concat_axis=0, axis_index_groups=groups, tiled=True
        )

    def onward(blocks):
        pairs = [(n, n + GROUP) for n in range(device_count - GROUP)]
        return lax.ppermute(blocks, "seq", pairs)

    def after(value, earlier):
        return lax.optimization_barrier((value, earlier))[0]

    index = lax.axis_index("seq").astype(jnp.int32).reshape(1)
    states_a, states_b, scalars = pack_states(index, span_start, steered_heads, key_value)
    queries_a, both_b = pack_queries(scalars, queries, states_b)
    position = jnp.arange(damping.shape[0], dtype=jnp.int32)
    emphasized = (position >= span_start[0]) & (position < span_start[0] + SPAN)
    bias = jnp.where(emphasized, 0.0, jnp.log2(damping.astype(jnp.float32)))
    bias = bias.reshape(-1, rows)

    states_a = exchange(states_a)
    back_a = onward(states_a)
    queries_a = exchange(after(queries_a, states_a))
    both_b = exchange(after(both_b, queries_a))
    states_b, queries_b = both_b[:, :2], both_b[:, 2:]
    far_a = onward(back_a)
    back_b = onward(after(states_b, back_a))
    far_b = onward(after(back_b, far_a))
    length = GROUP * rows
    span_states = lax.dynamic_slice_in_dim(
        far_a.transpose(1, 0, 2, 3).reshape(2, length, -1),
        jnp.minimum(span_start[0], length - SPAN),
        SPAN,
        1,
    )
    span_states = onward(span_states)

    held_a = attend(0, scalars, bias, queries_a, states_a)
    held_a = attend(1, scalars, bias, queries_a, back_a, held_a)
    held_b = attend(0, scalars, None, queries_b, states_b)
    held_a = attend(2, scalars, bias, queries_a, far_a, held_a)
    out_a = attend_span(3, scalars, queries_a, span_states, held_a)
    out_a = exchange(out_a)
    held_b = attend(1, scalars, None, queries_b, back_b, held_b)
    out_b = attend(2, scalars, None, queries_b, far_b, held_b, last=True)
    out_b = exchange(out_b)
    return unpack(scalars, out_a, out_b)


def solution(mesh):
    in_specs = (
        P(("prompt", "seq"), None, None),
        P(None, ("prompt", "seq"), None, None),
        P("prompt"),
        P("prompt"),
        P(),
    )
    out_specs = P(("prompt", "seq"), None, None)
    return jax.shard_map(
        per_device, mesh=mesh, in_specs=in_specs, out_specs=out_specs, check_vma=False
    )
```

```python
import functools
import math

import jax
import jax.numpy as jnp
from jax import lax
from jax.experimental import pallas as pl
from jax.experimental.pallas import tpu as pltpu
from jax.sharding import PartitionSpec as P

WINDOW = 4096
SPAN = 512

SCORE_SCALE = 144.0 ** (-0.5)
SOFTCAP = 50.0
LOG2_E = math.log2(math.e)

GROUP = 8
PAIR_FLOPS = 1536
VMEM_BYTES = 60 * 1024 * 1024

FIRST_SCALAR = 32
PLANE, SPAN_FIRST, STEERED_0, STEERED_1 = range(FIRST_SCALAR, FIRST_SCALAR + 4)
SCALARS = FIRST_SCALAR + 4


def smem():
    return pl.BlockSpec(memory_space=pltpu.SMEM)


def vmem():
    return pl.BlockSpec(memory_space=pltpu.VMEM)


def params():
    return pltpu.CompilerParams(vmem_limit_bytes=VMEM_BYTES)


def cost(pairs, moved):
    return pl.CostEstimate(
        flops=int(pairs * PAIR_FLOPS), bytes_accessed=int(moved), transcendentals=int(2 * pairs)
    )


def pack_states_kernel(
    index_ref, span_ref, steered_ref, states_ref, states_a, states_b, scalars, state_heads
):
    key_heads = states_ref.shape[2]
    steered_count = steered_ref.shape[0]
    steered_keys = [lax.div(steered_ref[n], 2) for n in range(steered_count)]
    flags = []
    for head in range(key_heads):
        hit = steered_keys[0] == head
        for n in range(1, steered_count):
            hit = hit | (steered_keys[n] == head)
        flags.append(hit.astype(jnp.int32))
    total = sum(flags[1:], flags[0])
    before = jnp.int32(0)
    for head in range(key_heads):
        rank = jnp.where(flags[head] == 1, before, total + head - before)
        scalars[rank] = jnp.int32(head)
        before = before + flags[head]
    place = lax.rem(index_ref[0], GROUP)
    scalars[PLANE] = lax.div(index_ref[0], GROUP)
    scalars[SPAN_FIRST] = span_ref[0]
    own_head = scalars[place]
    for group_head in range(2):
        hit = steered_ref[0] == 2 * own_head + group_head
        for n in range(1, steered_count):
            hit = hit | (steered_ref[n] == 2 * own_head + group_head)
        scalars[STEERED_0 + group_head] = hit.astype(jnp.int32)

    for part in range(2):
        state_heads[part] = jnp.transpose(states_ref[part], (1, 0, 2))
        for n in range(GROUP):
            states_a[n, part] = state_heads[part, scalars[n]]
            states_b[n, part] = state_heads[part, scalars[GROUP + n]]


def pack_states(index, span_start, steered_heads, states):
    _, rows, key_heads, width = states.shape
    part = jax.ShapeDtypeStruct((GROUP, 2, rows, width), states.dtype)
    return pl.pallas_call(
        pack_states_kernel,
        in_specs=[smem()] * 3 + [vmem()],
        out_specs=[vmem()] * 2 + [smem()],
        out_shape=[part] * 2 + [jax.ShapeDtypeStruct((SCALARS,), jnp.int32)],
        scratch_shapes=[pltpu.VMEM((2, key_heads, rows, width), states.dtype)],
        compiler_params=params(),
        cost_estimate=cost(0, 8 * states.size),
    )(index, span_start, steered_heads, states)


def pack_queries_kernel(scalars, queries_ref, queries_a, queries_b, query_heads):
    query_heads[...] = jnp.transpose(queries_ref[...], (1, 0, 2))
    for n in range(GROUP):
        for group_head in range(2):
            queries_a[n, group_head] = query_heads[2 * scalars[n] + group_head]
            queries_b[n, group_head] = query_heads[2 * scalars[GROUP + n] + group_head]


def pack_queries(scalars, queries):
    rows, heads, width = queries.shape
    part = jax.ShapeDtypeStruct((GROUP, 2, rows, width), queries.dtype)
    return pl.pallas_call(
        pack_queries_kernel,
        in_specs=[smem(), vmem()],
        out_specs=[vmem()] * 2,
        out_shape=[part] * 2,
        scratch_shapes=[pltpu.VMEM((heads, rows, width), queries.dtype)],
        compiler_params=params(),
        cost_estimate=cost(0, 8 * queries.size),
    )(scalars, queries)


def raw_scores(query, key):
    return lax.dot_general(
        query, key, (((1,), (1,)), ((), ())), preferred_element_type=jnp.float32
    )


def rounded_weights(raw_score, bias=None, visible=None):
    score = jnp.tanh(raw_score * (SCORE_SCALE / SOFTCAP)) * (SOFTCAP * LOG2_E)
    if bias is not None:
        score = score + bias
    weight = jnp.exp2(score)
    if visible is not None:
        weight = jnp.where(visible, weight, 0.0)
    return weight.astype(jnp.bfloat16)


def product(weight, extended):
    return jnp.dot(weight, extended, preferred_element_type=jnp.float32)


def attend_kernel(*refs, step, steerable, last):
    refs = list(refs)
    scalars = refs.pop(0)
    bias_ref = refs.pop(0) if steerable else None
    low_ref, high_ref, states_ref = refs.pop(0), refs.pop(0), refs.pop(0)
    span_ref = refs.pop(0) if steerable and last else None
    old_ref = refs.pop(0) if step else None
    out_ref = refs.pop(0) if last else None
    held_ref, query_ref, extended_ref, weight_ref = refs
    low = pl.program_id(0)
    blocks, _, rows, width = states_ref.shape
    high = blocks - 1 - low
    plane = scalars[PLANE]
    first_block = (plane - step) * blocks
    query_ref[0] = low_ref[0]
    query_ref[1] = high_ref[0]
    flags = [scalars[STEERED_0 + n] for n in range(2)]
    flag_values = [flag.astype(jnp.float32) for flag in flags]
    ones = jnp.ones((rows, width), jnp.bfloat16)

    @pl.when(low == 0)
    def _():
        for n in range(blocks):
            extended_ref[n, :, :width] = states_ref[n, 1]
            extended_ref[n, :, width:] = ones

    def bias(head, key_block):
        if not steerable:
            return None
        return bias_ref[pl.ds(first_block + key_block, 1), :] * flag_values[head]

    def emphasized(head, key_block):
        index = (first_block + key_block) * rows + lax.broadcasted_iota(jnp.int32, (1, rows), 1)
        first = scalars[SPAN_FIRST]
        return (index >= first) & (index < first + SPAN) & (flags[head] == 1)

    def add(tiles):
        ahead = raw_scores(query_ref[tiles[0][0], tiles[0][1]], states_ref[tiles[0][2], 0])
        late = None
        for n, (which, head, key_block, visible) in enumerate(tiles):
            raw_score = ahead
            if n + 1 < len(tiles):
                other, other_head, other_block, _ = tiles[n + 1]
                ahead = raw_scores(query_ref[other, other_head], states_ref[other_block, 0])
            weight = rounded_weights(raw_score, bias(head, key_block), visible)
            if late is not None:
                held_ref[0, late[0], late[1]] += product(late[2], extended_ref[late[3]])
            late = (which, head, weight, key_block)
        held_ref[0, late[0], late[1]] += product(late[2], extended_ref[late[3]])

    def add_all():
        chunks = [(which, head) for which in range(2) for head in range(2)]
        tiles = [(chunk, n) for chunk in chunks for n in range(blocks)]
        ahead = raw_scores(query_ref[0, 0], states_ref[0, 0])
        late = None

        def finish(chunk):
            weight = weight_ref[chunk[1]]
            extended = extended_ref[...].reshape(blocks * rows, 2 * width)
            held_ref[0, chunk[0], chunk[1]] += product(weight, extended)

        for at, (chunk, n) in enumerate(tiles):
            raw_score = ahead
            if at + 1 < len(tiles):
                (which, head), other = tiles[at + 1]
                ahead = raw_scores(query_ref[which, head], states_ref[other, 0])
            weight = rounded_weights(raw_score, bias(chunk[1], n))
            weight_ref[chunk[1], :, n * rows : (n + 1) * rows] = weight
            if n == 0 and late is not None:
                finish(late)
            late = chunk
        finish(late)

    def compute():
        row = lax.broadcasted_iota(jnp.int32, (rows, rows), 0)
        column = lax.broadcasted_iota(jnp.int32, (rows, rows), 1)
        if step == 1:
            add_all()
            return
        tiles = []
        for n in range(blocks - 1):
            if step == 0:
                is_low = n < low
                which, key_block = jnp.where(is_low, 0, 1), jnp.where(is_low, n, n - low)
            else:
                is_high = n < low
                which, key_block = jnp.where(is_high, 1, 0), jnp.where(is_high, high + 1 + n, n + 1)
            tiles += [(which, head, key_block, None) for head in range(2)]
        in_order = row >= column if step == 0 else row < column
        for which, block in ((0, low), (1, high)):
            for head in range(2):
                visible = in_order
                if step and steerable:
                    visible = visible | emphasized(head, block)
                tiles.append((which, head, block, visible))
        add(tiles)

    def add_span():
        first = scalars[SPAN_FIRST] - first_block * rows
        span_low = lax.div(jnp.maximum(first, 0), rows)
        span_high = lax.div(jnp.maximum(first + SPAN + rows - 1, 0), rows)
        span_high = jnp.where(flags[0] + flags[1] > 0, span_high, 0)
        for which, block in ((0, low), (1, high)):
            lax.fori_loop(
                span_low,
                jnp.minimum(span_high, block),
                lambda n, c: (add([(which, head, n, emphasized(head, n)) for head in range(2)]), c)[1],
                0,
            )

    def add_far_span():
        first = scalars[SPAN_FIRST]
        length = blocks * rows
        index = (plane - step - 1) * length + jnp.minimum(first, length - SPAN)
        index = index + lax.broadcasted_iota(jnp.int32, (1, SPAN), 1)
        inside = (index >= first) & (index < first + SPAN)
        extended = jnp.concatenate([span_ref[1], jnp.ones((SPAN, width), jnp.bfloat16)], axis=1)
        for which in range(2):
            for head in range(2):
                raw_score = raw_scores(query_ref[which, head], span_ref[0])
                weight = rounded_weights(raw_score, None, inside & (flags[head] == 1))
                held_ref[0, which, head] += product(weight, extended)

    if step:
        held_ref[...] = old_ref[...]
        pl.when(plane >= step)(compute)
    else:
        held_ref[...] = jnp.zeros(held_ref.shape, jnp.float32)
        compute()
    if last and steerable:
        pl.when(plane >= step)(add_span)
        far_end = (plane - step) * blocks * rows
        wanted = (plane > step) & (scalars[SPAN_FIRST] < far_end) & (flags[0] + flags[1] > 0)
        pl.when(wanted)(add_far_span)
    if last:
        for which, block in ((0, low), (1, high)):
            held = held_ref[0, which]
            out_ref[block] = (held[:, :, :width] / held[:, :, width:]).astype(out_ref.dtype)


def attend(step, scalars, bias, queries, states, held=None, span_states=None, last=False):
    blocks, pair, rows, width = queries.shape
    assert blocks % 2 == 0 and pair == 2
    one = (1, pair, rows, width)
    held_shape = (blocks // 2, 2, pair, rows, 2 * width)
    held_spec = pl.BlockSpec((1,) + held_shape[1:], lambda n: (n, 0, 0, 0, 0))
    operands, in_specs = [scalars], [smem()]
    if bias is not None:
        operands.append(bias)
        in_specs.append(pl.BlockSpec(bias.shape, lambda n: (0, 0)))
    operands += [queries, queries, states]
    in_specs += [
        pl.BlockSpec(one, lambda n: (n, 0, 0, 0)),
        pl.BlockSpec(one, lambda n: (blocks - 1 - n, 0, 0, 0)),
        pl.BlockSpec(states.shape, lambda n: (0, 0, 0, 0)),
    ]
    if span_states is not None:
        operands.append(span_states)
        in_specs.append(pl.BlockSpec(span_states.shape, lambda n: (0, 0, 0)))
    if held is not None:
        operands.append(held)
        in_specs.append(held_spec)
    scratch = [
        pltpu.VMEM((2, pair, rows, width), queries.dtype),
        pltpu.VMEM((blocks, rows, 2 * width), queries.dtype),
        pltpu.VMEM((2, rows, blocks * rows if step == 1 else width), queries.dtype),
    ]
    if last:
        out_shape = jax.ShapeDtypeStruct(queries.shape, queries.dtype)
        out_specs = pl.BlockSpec(queries.shape, lambda n: (0, 0, 0, 0))
        scratch = [pltpu.VMEM((1,) + held_shape[1:], jnp.float32)] + scratch
    else:
        out_shape, out_specs = jax.ShapeDtypeStruct(held_shape, jnp.float32), held_spec
    return pl.pallas_call(
        functools.partial(attend_kernel, step=step, steerable=bias is not None, last=last),
        grid=(blocks // 2,),
        in_specs=in_specs,
        out_specs=out_specs,
        out_shape=out_shape,
        scratch_shapes=scratch,
        compiler_params=params(),
        cost_estimate=cost(
            pair * (blocks * rows) ** 2 / (1 if step == 1 else 2),
            8 * queries.size + 8 * pair * blocks * rows * width,
        ),
    )(*operands)


def unpack_kernel(scalars, out_a, out_b, attention, heads_ref):
    for n in range(GROUP):
        for group_head in range(2):
            heads_ref[2 * scalars[n] + group_head] = out_a[n, group_head]
            heads_ref[2 * scalars[GROUP + n] + group_head] = out_b[n, group_head]
    attention[...] = jnp.transpose(heads_ref[...], (1, 0, 2))


def unpack(scalars, out_a, out_b):
    blocks, pair, rows, width = out_a.shape
    heads = 2 * blocks * pair
    return pl.pallas_call(
        unpack_kernel,
        in_specs=[smem()] + [vmem()] * 2,
        out_specs=vmem(),
        out_shape=jax.ShapeDtypeStruct((rows, heads, width), out_a.dtype),
        scratch_shapes=[pltpu.VMEM((heads, rows, width), out_a.dtype)],
        compiler_params=params(),
    )(scalars, out_a, out_b)


def per_device(queries, key_value, damping, span_start, steered_heads):
    rows = queries.shape[0]
    device_count = lax.axis_size("seq")
    assert WINDOW == 2 * GROUP * rows and device_count == 4 * GROUP
    assert key_value.shape[2] == 2 * GROUP and queries.shape[1] == 4 * GROUP
    assert steered_heads.shape[0] <= GROUP
    groups = [
        list(range(first, first + GROUP)) for first in range(0, device_count, GROUP)
    ]

    def exchange(blocks):
        return lax.all_to_all(
            blocks, "seq", split_axis=0, concat_axis=0, axis_index_groups=groups, tiled=True
        )

    def onward(blocks):
        pairs = [(n, n + GROUP) for n in range(device_count - GROUP)]
        return lax.ppermute(blocks, "seq", pairs)

    def after(value, earlier):
        return lax.optimization_barrier((value, earlier))[0]

    index = lax.axis_index("seq").astype(jnp.int32).reshape(1)
    states_a, states_b, scalars = pack_states(index, span_start, steered_heads, key_value)
    queries_a, queries_b = pack_queries(scalars, queries)
    position = jnp.arange(damping.shape[0], dtype=jnp.int32)
    emphasized = (position >= span_start[0]) & (position < span_start[0] + SPAN)
    bias = jnp.where(emphasized, 0.0, jnp.log2(damping.astype(jnp.float32)))
    bias = bias.reshape(-1, rows)

    states_a = exchange(states_a)
    back_a = onward(states_a)
    queries_a = exchange(after(queries_a, states_a))
    states_b = exchange(after(states_b, queries_a))
    queries_b = exchange(after(queries_b, states_b))
    far_a = onward(back_a)
    back_b = onward(states_b)
    far_b = onward(back_b)
    length = GROUP * rows
    span_states = lax.dynamic_slice_in_dim(
        far_a.transpose(1, 0, 2, 3).reshape(2, length, -1),
        jnp.minimum(span_start[0], length - SPAN),
        SPAN,
        1,
    )
    span_states = onward(span_states)

    held_a = attend(0, scalars, bias, queries_a, states_a)
    held_a = attend(1, scalars, bias, after(queries_a, states_b), back_a, held_a)
    held_b = attend(0, scalars, None, after(queries_b, held_a), states_b)
    out_a = attend(2, scalars, bias, queries_a, far_a, after(held_a, held_b), span_states, last=True)
    held_b = attend(1, scalars, None, queries_b, back_b, after(held_b, out_a))
    out_a = exchange(out_a)
    out_b = attend(2, scalars, None, queries_b, far_b, held_b, last=True)
    out_b = exchange(out_b)
    return unpack(scalars, out_a, out_b)


def solution(mesh):
    in_specs = (
        P(("prompt", "seq"), None, None),
        P(None, ("prompt", "seq"), None, None),
        P("prompt"),
        P("prompt"),
        P(),
    )
    out_specs = P(("prompt", "seq"), None, None)
    return jax.shard_map(
        per_device, mesh=mesh, in_specs=in_specs, out_specs=out_specs, check_vma=False
    )
```

```python
import functools
import math

import jax
import jax.numpy as jnp
from jax import lax
from jax.experimental import pallas as pl
from jax.experimental.pallas import tpu as pltpu
from jax.sharding import PartitionSpec as P

WINDOW = 4096
SPAN = 512

SCORE_SCALE = 144.0 ** (-0.5)
SOFTCAP = 50.0
LOG2_E = math.log2(math.e)

GROUP = 8
PAIR_FLOPS = 256
VMEM_BYTES = 24 * 1024 * 1024

FIRST_SCALAR = 32
PLANE, SPAN_FIRST, STEERED_0, STEERED_1 = range(FIRST_SCALAR, FIRST_SCALAR + 4)
SCALARS = FIRST_SCALAR + 4


def smem():
    return pl.BlockSpec(memory_space=pltpu.SMEM)


def vmem():
    return pl.BlockSpec(memory_space=pltpu.VMEM)


def params():
    return pltpu.CompilerParams(vmem_limit_bytes=VMEM_BYTES)


def cost(pairs, moved):
    return pl.CostEstimate(
        flops=int(pairs * PAIR_FLOPS), bytes_accessed=int(moved), transcendentals=int(2 * pairs)
    )


def pack_states_kernel(
    index_ref, span_ref, steered_ref, states_ref, states_a, states_b, scalars, state_heads
):
    key_heads = states_ref.shape[2]
    steered_count = steered_ref.shape[0]
    steered_keys = [lax.div(steered_ref[n], 2) for n in range(steered_count)]
    flags = []
    for head in range(key_heads):
        hit = steered_keys[0] == head
        for n in range(1, steered_count):
            hit = hit | (steered_keys[n] == head)
        flags.append(hit.astype(jnp.int32))
    total = sum(flags[1:], flags[0])
    before = jnp.int32(0)
    for head in range(key_heads):
        rank = jnp.where(flags[head] == 1, before, total + head - before)
        scalars[rank] = jnp.int32(head)
        before = before + flags[head]
    place = lax.rem(index_ref[0], GROUP)
    scalars[PLANE] = lax.div(index_ref[0], GROUP)
    scalars[SPAN_FIRST] = span_ref[0]
    own_head = scalars[place]
    for group_head in range(2):
        hit = steered_ref[0] == 2 * own_head + group_head
        for n in range(1, steered_count):
            hit = hit | (steered_ref[n] == 2 * own_head + group_head)
        scalars[STEERED_0 + group_head] = hit.astype(jnp.int32)

    for part in range(2):
        state_heads[part] = jnp.transpose(states_ref[part], (1, 0, 2))
        for n in range(GROUP):
            states_a[n, part] = state_heads[part, scalars[n]]
            states_b[n, part] = state_heads[part, scalars[GROUP + n]]


def pack_states(index, span_start, steered_heads, states):
    _, rows, key_heads, width = states.shape
    part = jax.ShapeDtypeStruct((GROUP, 2, rows, width), states.dtype)
    return pl.pallas_call(
        pack_states_kernel,
        in_specs=[smem()] * 3 + [vmem()],
        out_specs=[vmem()] * 2 + [smem()],
        out_shape=[part] * 2 + [jax.ShapeDtypeStruct((SCALARS,), jnp.int32)],
        scratch_shapes=[pltpu.VMEM((2, key_heads, rows, width), states.dtype)],
        compiler_params=params(),
        cost_estimate=cost(0, 8 * states.size),
    )(index, span_start, steered_heads, states)


def pack_queries_kernel(scalars, queries_ref, queries_a, queries_b, query_heads):
    query_heads[...] = jnp.transpose(queries_ref[...], (1, 0, 2))
    for n in range(GROUP):
        for group_head in range(2):
            queries_a[n, group_head] = query_heads[2 * scalars[n] + group_head]
            queries_b[n, group_head] = query_heads[2 * scalars[GROUP + n] + group_head]


def pack_queries(scalars, queries):
    rows, heads, width = queries.shape
    part = jax.ShapeDtypeStruct((GROUP, 2, rows, width), queries.dtype)
    return pl.pallas_call(
        pack_queries_kernel,
        in_specs=[smem(), vmem()],
        out_specs=[vmem()] * 2,
        out_shape=[part] * 2,
        scratch_shapes=[pltpu.VMEM((heads, rows, width), queries.dtype)],
        compiler_params=params(),
        cost_estimate=cost(0, 8 * queries.size),
    )(scalars, queries)


def raw_scores(query, key):
    return lax.dot_general(
        query, key, (((1,), (1,)), ((), ())), preferred_element_type=jnp.float32
    )


def weights(raw_score, bias=None, visible=None):
    score = jnp.tanh(raw_score * (SCORE_SCALE / SOFTCAP)) * (SOFTCAP * LOG2_E)
    if bias is not None:
        score = score + bias
    weight = jnp.exp2(score)
    if visible is not None:
        weight = jnp.where(visible, weight, 0.0)
    return weight


def lane_sums(weight, lanes):
    sums = weight[:, :lanes]
    for first in range(lanes, weight.shape[1], lanes):
        sums = sums + weight[:, first : first + lanes]
    return sums


def attend_kernel(*refs, step, steerable, last, chunk):
    refs = list(refs)
    scalars = refs.pop(0)
    bias_ref = refs.pop(0) if steerable else None
    low_ref, high_ref, states_ref = refs.pop(0), refs.pop(0), refs.pop(0)
    span_ref = refs.pop(0) if steerable and last else None
    old_ref = refs.pop(0) if step else None
    out_ref = refs.pop(0) if last else None
    held_ref, query_ref = refs
    low = pl.program_id(0)
    blocks, _, rows, width = states_ref.shape
    high = blocks - 1 - low
    plane = scalars[PLANE]
    first_block = (plane - step) * blocks
    query_ref[0] = low_ref[0]
    query_ref[1] = high_ref[0]
    flags = [scalars[STEERED_0 + n] for n in range(2)]
    flag_values = [flag.astype(jnp.float32) for flag in flags]
    chunks = [pl.ds(first, chunk) for first in range(0, rows, chunk)]

    def bias(head, key_block, columns):
        if not steerable:
            return None
        row = bias_ref[pl.ds(first_block + key_block, 1), :] * flag_values[head]
        return row[:, columns.start : columns.start + columns.size]

    def emphasized(head, key_block, columns):
        index = (first_block + key_block) * rows + columns.start
        index = index + lax.broadcasted_iota(jnp.int32, (1, columns.size), 1)
        first = scalars[SPAN_FIRST]
        return (index >= first) & (index < first + SPAN) & (flags[head] == 1)

    def score(unit):
        which, head, some, key_block, columns, _ = unit
        return raw_scores(query_ref[which, head, some, :], states_ref[key_block, 0, columns, :])

    def add(units):
        ahead = score(units[0])
        late = None

        def finish(unit, weight, sums):
            which, head, some, key_block, columns, _ = unit
            held_ref[0, 1, which, head, some, :] += sums
            held_ref[0, 0, which, head, some, :] += jnp.dot(
                weight, states_ref[key_block, 1, columns, :], preferred_element_type=jnp.float32
            )

        for n, unit in enumerate(units):
            raw_score = ahead
            if n + 1 < len(units):
                ahead = score(units[n + 1])
            _, head, _, key_block, columns, visible = unit
            weight = weights(raw_score, bias(head, key_block, columns), visible)
            if late is not None:
                finish(*late)
            late = (unit, weight.astype(jnp.bfloat16), lane_sums(weight, width))
        finish(*late)

    whole = pl.ds(0, rows)

    def add_all():
        units = [
            (which, head, some, n, whole, None)
            for which in range(2)
            for head in range(2)
            for some in chunks
            for n in range(blocks)
        ]
        ahead = score(units[0])
        late = None
        weighted = sums = None

        def finish(weighted, unit, weight):
            which, head, some, n, columns, _ = unit
            more = jnp.dot(weight, states_ref[n, 1], preferred_element_type=jnp.float32)
            weighted = more if n == 0 else weighted + more
            if n == blocks - 1:
                held_ref[0, 0, which, head, some, :] += weighted
            return weighted

        for at, unit in enumerate(units):
            raw_score = ahead
            if at + 1 < len(units):
                ahead = score(units[at + 1])
            which, head, some, n, columns, _ = unit
            weight = weights(raw_score, bias(head, n, columns))
            if late is not None:
                weighted = finish(weighted, *late)
            late = (unit, weight.astype(jnp.bfloat16))
            more = lane_sums(weight, width)
            sums = more if n == 0 else sums + more
            if n == blocks - 1:
                held_ref[0, 1, which, head, some, :] += sums
        finish(weighted, *late)

    def compute():
        if step == 1:
            add_all()
            return
        units = []
        for n in range(blocks - 1):
            if step == 0:
                is_low = n < low
                which, key_block = jnp.where(is_low, 0, 1), jnp.where(is_low, n, n - low)
            else:
                is_high = n < low
                which, key_block = jnp.where(is_high, 1, 0), jnp.where(is_high, high + 1 + n, n + 1)
            units += [
                (which, head, some, key_block, whole, None) for head in range(2) for some in chunks
            ]
        for which, block in ((0, low), (1, high)):
            for head in range(2):
                for first in range(0, rows, chunk):
                    if step == 0:
                        columns = pl.ds(0, -(-(first + chunk) // width) * width)
                    else:
                        start = 0 if steerable else first // width * width
                        columns = pl.ds(start, rows - start)
                    shape = (chunk, columns.size)
                    row = first + lax.broadcasted_iota(jnp.int32, shape, 0)
                    column = columns.start + lax.broadcasted_iota(jnp.int32, shape, 1)
                    visible = row >= column if step == 0 else row < column
                    if step and steerable:
                        visible = visible | emphasized(head, block, columns)
                    units.append((which, head, pl.ds(first, chunk), block, columns, visible))
        add(units)

    def add_span():
        first = scalars[SPAN_FIRST] - first_block * rows
        span_low = lax.div(jnp.maximum(first, 0), rows)
        span_high = lax.div(jnp.maximum(first + SPAN + rows - 1, 0), rows)
        span_high = jnp.where(flags[0] + flags[1] > 0, span_high, 0)

        def body(which, n):
            add(
                [
                    (which, head, some, n, whole, emphasized(head, n, whole))
                    for head in range(2)
                    for some in chunks
                ]
            )

        for which, block in ((0, low), (1, high)):
            lax.fori_loop(
                span_low,
                jnp.minimum(span_high, block),
                lambda n, c, which=which: (body(which, n), c)[1],
                0,
            )

    def add_far_span():
        first = scalars[SPAN_FIRST]
        length = blocks * rows
        index = (plane - step - 1) * length + jnp.minimum(first, length - SPAN)
        index = index + lax.broadcasted_iota(jnp.int32, (1, SPAN), 1)
        inside = (index >= first) & (index < first + SPAN)
        for which in range(2):
            for head in range(2):
                visible = inside & (flags[head] == 1)
                for some in chunks:
                    raw_score = raw_scores(query_ref[which, head, some, :], span_ref[0])
                    weight = weights(raw_score, None, visible)
                    held_ref[0, 1, which, head, some, :] += lane_sums(weight, width)
                    held_ref[0, 0, which, head, some, :] += jnp.dot(
                        weight.astype(jnp.bfloat16), span_ref[1], preferred_element_type=jnp.float32
                    )

    if step:
        held_ref[...] = old_ref[...]
        pl.when(plane >= step)(compute)
    else:
        held_ref[...] = jnp.zeros(held_ref.shape, jnp.float32)
        compute()
    if last and steerable:
        pl.when(plane >= step)(add_span)
        far_end = (plane - step) * blocks * rows
        wanted = (plane > step) & (scalars[SPAN_FIRST] < far_end) & (flags[0] + flags[1] > 0)
        pl.when(wanted)(add_far_span)
    if last:
        for which, block in ((0, low), (1, high)):
            total = jnp.sum(held_ref[0, 1, which], axis=-1, keepdims=True)
            out_ref[block] = (held_ref[0, 0, which] / total).astype(out_ref.dtype)


def attend(step, scalars, bias, queries, states, held=None, span_states=None, last=False):
    blocks, pair, rows, width = queries.shape
    assert blocks % 2 == 0 and pair == 2
    one = (1, pair, rows, width)
    held_shape = (blocks // 2, 2, 2, pair, rows, width)
    held_spec = pl.BlockSpec((1,) + held_shape[1:], lambda n: (n, 0, 0, 0, 0, 0))
    operands, in_specs = [scalars], [smem()]
    if bias is not None:
        operands.append(bias)
        in_specs.append(pl.BlockSpec(bias.shape, lambda n: (0, 0)))
    operands += [queries, queries, states]
    in_specs += [
        pl.BlockSpec(one, lambda n: (n, 0, 0, 0)),
        pl.BlockSpec(one, lambda n: (blocks - 1 - n, 0, 0, 0)),
        pl.BlockSpec(states.shape, lambda n: (0, 0, 0, 0)),
    ]
    if span_states is not None:
        operands.append(span_states)
        in_specs.append(pl.BlockSpec(span_states.shape, lambda n: (0, 0, 0)))
    if held is not None:
        operands.append(held)
        in_specs.append(held_spec)
    scratch = [pltpu.VMEM((2, pair, rows, width), queries.dtype)]
    if last:
        out_shape = jax.ShapeDtypeStruct(queries.shape, queries.dtype)
        out_specs = pl.BlockSpec(queries.shape, lambda n: (0, 0, 0, 0))
        scratch = [pltpu.VMEM((1,) + held_shape[1:], jnp.float32)] + scratch
    else:
        out_shape, out_specs = jax.ShapeDtypeStruct(held_shape, jnp.float32), held_spec
    kernel = functools.partial(
        attend_kernel,
        step=step,
        steerable=bias is not None,
        last=last,
        chunk=min(rows, 128 if bias is not None else 64),
    )
    return pl.pallas_call(
        kernel,
        grid=(blocks // 2,),
        in_specs=in_specs,
        out_specs=out_specs,
        out_shape=out_shape,
        scratch_shapes=scratch,
        compiler_params=params(),
        cost_estimate=cost(
            pair * (blocks * rows) ** 2 / (1 if step == 1 else 2),
            8 * queries.size + 8 * pair * blocks * rows * width,
        ),
    )(*operands)


def unpack_kernel(scalars, out_a, out_b, attention, heads_ref):
    for n in range(GROUP):
        for group_head in range(2):
            heads_ref[2 * scalars[n] + group_head] = out_a[n, group_head]
            heads_ref[2 * scalars[GROUP + n] + group_head] = out_b[n, group_head]
    attention[...] = jnp.transpose(heads_ref[...], (1, 0, 2))


def unpack(scalars, out_a, out_b):
    blocks, pair, rows, width = out_a.shape
    heads = 2 * blocks * pair
    return pl.pallas_call(
        unpack_kernel,
        in_specs=[smem()] + [vmem()] * 2,
        out_specs=vmem(),
        out_shape=jax.ShapeDtypeStruct((rows, heads, width), out_a.dtype),
        scratch_shapes=[pltpu.VMEM((heads, rows, width), out_a.dtype)],
        compiler_params=params(),
    )(scalars, out_a, out_b)


def per_device(queries, key_value, damping, span_start, steered_heads):
    rows = queries.shape[0]
    device_count = lax.axis_size("seq")
    assert WINDOW == 2 * GROUP * rows and device_count == 4 * GROUP
    assert key_value.shape[2] == 2 * GROUP and queries.shape[1] == 4 * GROUP
    assert steered_heads.shape[0] <= GROUP
    groups = [
        list(range(first, first + GROUP)) for first in range(0, device_count, GROUP)
    ]

    def exchange(blocks):
        return lax.all_to_all(
            blocks, "seq", split_axis=0, concat_axis=0, axis_index_groups=groups, tiled=True
        )

    def onward(blocks, planes=1):
        shift = planes * GROUP
        pairs = [(n, n + shift) for n in range(device_count - shift)]
        return lax.ppermute(blocks, "seq", pairs)

    def after(value, earlier):
        return lax.optimization_barrier((value, earlier))[0]

    index = lax.axis_index("seq").astype(jnp.int32).reshape(1)
    states_a, states_b, scalars = pack_states(index, span_start, steered_heads, key_value)
    queries_a, queries_b = pack_queries(scalars, queries)
    states_a = exchange(states_a)
    back_a = onward(states_a)
    length = GROUP * rows
    span_states = lax.dynamic_slice_in_dim(
        states_a.transpose(1, 0, 2, 3).reshape(2, length, -1),
        jnp.minimum(span_start[0], length - SPAN),
        SPAN,
        1,
    )
    span_states = onward(span_states, 3)
    damping = after(damping, states_a)
    position = jnp.arange(damping.shape[0], dtype=jnp.int32)
    emphasized = (position >= span_start[0]) & (position < span_start[0] + SPAN)
    bias = jnp.where(emphasized, 0.0, jnp.log2(damping.astype(jnp.float32)))
    bias = bias.reshape(-1, rows)
    states_b = exchange(after(states_b, bias))
    back_b = onward(states_b)
    queries_a = exchange(after(queries_a, states_b))
    queries_b = exchange(after(queries_b, queries_a))
    far_a = onward(back_a)
    far_b = onward(back_b)

    held_a = attend(0, scalars, bias, queries_a, states_a)
    held_a = attend(1, scalars, bias, queries_a, back_a, held_a)
    held_b = attend(0, scalars, None, after(queries_b, held_a), states_b)
    held_b = attend(1, scalars, None, queries_b, back_b, held_b)
    out_a = attend(2, scalars, bias, queries_a, far_a, after(held_a, held_b), span_states, last=True)
    out_a = exchange(out_a)
    out_b = attend(2, scalars, None, queries_b, far_b, held_b, last=True)
    out_b = exchange(out_b)
    return unpack(scalars, out_a, out_b)


def solution(mesh):
    in_specs = (
        P(("prompt", "seq"), None, None),
        P(None, ("prompt", "seq"), None, None),
        P("prompt"),
        P("prompt"),
        P(),
    )
    out_specs = P(("prompt", "seq"), None, None)
    return jax.shard_map(
        per_device, mesh=mesh, in_specs=in_specs, out_specs=out_specs, check_vma=False
    )
```

```python
import functools
import math

import jax
import jax.numpy as jnp
from jax import lax
from jax.experimental import pallas as pl
from jax.experimental.pallas import tpu as pltpu
from jax.sharding import PartitionSpec as P

WINDOW = 4096
SPAN = 512

SCORE_SCALE = 144.0 ** (-0.5)
SOFTCAP = 50.0
LOG2_E = math.log2(math.e)

GROUP = 8
PAIR_FLOPS = 512
VMEM_BYTES = 60 * 1024 * 1024

FIRST_SCALAR = 32
PLANE, SPAN_FIRST, STEERED_0, STEERED_1 = range(FIRST_SCALAR, FIRST_SCALAR + 4)
SCALARS = FIRST_SCALAR + 4


def smem():
    return pl.BlockSpec(memory_space=pltpu.SMEM)


def vmem():
    return pl.BlockSpec(memory_space=pltpu.VMEM)


def params():
    return pltpu.CompilerParams(vmem_limit_bytes=VMEM_BYTES)


def cost(pairs, moved):
    return pl.CostEstimate(
        flops=int(pairs * PAIR_FLOPS), bytes_accessed=int(moved), transcendentals=int(2 * pairs)
    )


def pack_states_kernel(
    index_ref, span_ref, steered_ref, states_ref, states_a, states_b, scalars, state_heads
):
    key_heads = states_ref.shape[2]
    steered_count = steered_ref.shape[0]
    steered_keys = [lax.div(steered_ref[n], 2) for n in range(steered_count)]
    flags = []
    for head in range(key_heads):
        hit = steered_keys[0] == head
        for n in range(1, steered_count):
            hit = hit | (steered_keys[n] == head)
        flags.append(hit.astype(jnp.int32))
    total = sum(flags[1:], flags[0])
    before = jnp.int32(0)
    for head in range(key_heads):
        rank = jnp.where(flags[head] == 1, before, total + head - before)
        scalars[rank] = jnp.int32(head)
        before = before + flags[head]
    place = lax.rem(index_ref[0], GROUP)
    scalars[PLANE] = lax.div(index_ref[0], GROUP)
    scalars[SPAN_FIRST] = span_ref[0]
    own_head = scalars[place]
    for group_head in range(2):
        hit = steered_ref[0] == 2 * own_head + group_head
        for n in range(1, steered_count):
            hit = hit | (steered_ref[n] == 2 * own_head + group_head)
        scalars[STEERED_0 + group_head] = hit.astype(jnp.int32)

    for part in range(2):
        state_heads[part] = jnp.transpose(states_ref[part], (1, 0, 2))
        for n in range(GROUP):
            states_a[n, part] = state_heads[part, scalars[n]]
            states_b[n, part] = state_heads[part, scalars[GROUP + n]]


def pack_states(index, span_start, steered_heads, states):
    _, rows, key_heads, width = states.shape
    part = jax.ShapeDtypeStruct((GROUP, 2, rows, width), states.dtype)
    return pl.pallas_call(
        pack_states_kernel,
        in_specs=[smem()] * 3 + [vmem()],
        out_specs=[vmem()] * 2 + [smem()],
        out_shape=[part] * 2 + [jax.ShapeDtypeStruct((SCALARS,), jnp.int32)],
        scratch_shapes=[pltpu.VMEM((2, key_heads, rows, width), states.dtype)],
        compiler_params=params(),
        cost_estimate=cost(0, 8 * states.size),
    )(index, span_start, steered_heads, states)


def pack_queries_kernel(scalars, queries_ref, queries_a, queries_b, query_heads):
    query_heads[...] = jnp.transpose(queries_ref[...], (1, 0, 2))
    for n in range(GROUP):
        for group_head in range(2):
            queries_a[n, group_head] = query_heads[2 * scalars[n] + group_head]
            queries_b[n, group_head] = query_heads[2 * scalars[GROUP + n] + group_head]


def pack_queries(scalars, queries):
    rows, heads, width = queries.shape
    part = jax.ShapeDtypeStruct((GROUP, 2, rows, width), queries.dtype)
    return pl.pallas_call(
        pack_queries_kernel,
        in_specs=[smem(), vmem()],
        out_specs=[vmem()] * 2,
        out_shape=[part] * 2,
        scratch_shapes=[pltpu.VMEM((heads, rows, width), queries.dtype)],
        compiler_params=params(),
        cost_estimate=cost(0, 8 * queries.size),
    )(scalars, queries)


def weights(raw_score, bias=None, visible=None):
    score = jnp.tanh(raw_score * (SCORE_SCALE / SOFTCAP)) * (SOFTCAP * LOG2_E)
    if bias is not None:
        score = score + bias
    weight = jnp.exp2(score)
    if visible is not None:
        weight = jnp.where(visible, weight, 0.0)
    return weight


def product(left, right):
    return jnp.dot(left, right, preferred_element_type=jnp.float32)


def lane_sums(weight, lanes):
    sums = weight[:, :lanes]
    for first in range(lanes, weight.shape[1], lanes):
        sums = sums + weight[:, first : first + lanes]
    return sums


def attend_kernel(*refs, step, steerable, last, chunk):
    refs = list(refs)
    scalars = refs.pop(0)
    bias_ref = refs.pop(0) if steerable else None
    low_ref, high_ref, states_ref = refs.pop(0), refs.pop(0), refs.pop(0)
    span_ref = refs.pop(0) if steerable and last else None
    old_ref = refs.pop(0) if step else None
    out_ref = refs.pop(0) if last else None
    held_ref, query_ref, keys_ref = refs
    low = pl.program_id(0)
    blocks, _, rows, width = states_ref.shape
    high = blocks - 1 - low
    plane = scalars[PLANE]
    first_block = (plane - step) * blocks
    query_ref[0] = low_ref[0].reshape(2 * rows, width)
    query_ref[1] = high_ref[0].reshape(2 * rows, width)
    flags = [scalars[STEERED_0 + n] for n in range(2)]
    flag_values = [flag.astype(jnp.float32) for flag in flags]
    firsts = range(0, 2 * rows, chunk)

    @pl.when(low == 0)
    def _():
        for n in range(blocks):
            keys_ref[n] = states_ref[n, 0].T

    def bias(first, key_block):
        if not steerable:
            return None
        return bias_ref[pl.ds(first_block + key_block, 1), :] * flag_values[first // rows]

    def emphasized(first, key_block):
        index = (first_block + key_block) * rows + lax.broadcasted_iota(jnp.int32, (1, rows), 1)
        start = scalars[SPAN_FIRST]
        return (index >= start) & (index < start + SPAN) & (flags[first // rows] == 1)

    def score(unit):
        which, first, key_block, _ = unit
        return product(query_ref[which, pl.ds(first, chunk), :], keys_ref[key_block])

    def add(units):
        ahead = score(units[0])
        late = None

        def finish(unit, weight, sums):
            which, first, key_block, _ = unit
            some = pl.ds(first, chunk)
            held_ref[0, 1, which, some, :] += sums
            held_ref[0, 0, which, some, :] += product(weight, states_ref[key_block, 1])

        for n, unit in enumerate(units):
            raw_score = ahead
            if n + 1 < len(units):
                ahead = score(units[n + 1])
            _, first, key_block, visible = unit
            weight = weights(raw_score, bias(first, key_block), visible)
            if late is not None:
                finish(*late)
            late = (unit, weight.astype(jnp.bfloat16), lane_sums(weight, width))
        finish(*late)

    def compute():
        units = []
        if step == 1:
            add(
                [
                    (which, first, n, None)
                    for which in range(2)
                    for first in firsts
                    for n in range(blocks)
                ]
            )
            return
        for n in range(blocks - 1):
            if step == 0:
                is_low = n < low
                which, key_block = jnp.where(is_low, 0, 1), jnp.where(is_low, n, n - low)
            else:
                is_high = n < low
                which, key_block = jnp.where(is_high, 1, 0), jnp.where(is_high, high + 1 + n, n + 1)
            units += [(which, first, key_block, None) for first in firsts]
        row = lax.rem(lax.broadcasted_iota(jnp.int32, (chunk, rows), 0), rows)
        column = lax.broadcasted_iota(jnp.int32, (chunk, rows), 1)
        in_order = row >= column if step == 0 else row < column
        for which, block in ((0, low), (1, high)):
            for first in firsts:
                visible = in_order
                if step and steerable:
                    visible = visible | emphasized(first, block)
                units.append((which, first, block, visible))
        add(units)

    def add_span():
        first = scalars[SPAN_FIRST] - first_block * rows
        span_low = lax.div(jnp.maximum(first, 0), rows)
        span_high = lax.div(jnp.maximum(first + SPAN + rows - 1, 0), rows)
        span_high = jnp.where(flags[0] + flags[1] > 0, span_high, 0)

        def body(which, n):
            add([(which, first, n, emphasized(first, n)) for first in firsts])

        for which, block in ((0, low), (1, high)):
            lax.fori_loop(
                span_low,
                jnp.minimum(span_high, block),
                lambda n, c, which=which: (body(which, n), c)[1],
                0,
            )

    def add_far_span():
        start = scalars[SPAN_FIRST]
        length = blocks * rows
        index = (plane - step - 1) * length + jnp.minimum(start, length - SPAN)
        index = index + lax.broadcasted_iota(jnp.int32, (1, SPAN), 1)
        inside = (index >= start) & (index < start + SPAN)
        keys = span_ref[0].T
        for which in range(2):
            for first in firsts:
                some = pl.ds(first, chunk)
                raw_score = product(query_ref[which, some, :], keys)
                weight = weights(raw_score, None, inside & (flags[first // rows] == 1))
                held_ref[0, 1, which, some, :] += lane_sums(weight, width)
                held_ref[0, 0, which, some, :] += product(weight.astype(jnp.bfloat16), span_ref[1])

    if step:
        held_ref[...] = old_ref[...]
        pl.when(plane >= step)(compute)
    else:
        held_ref[...] = jnp.zeros(held_ref.shape, jnp.float32)
        compute()
    if last and steerable:
        pl.when(plane >= step)(add_span)
        far_end = (plane - step) * blocks * rows
        wanted = (plane > step) & (scalars[SPAN_FIRST] < far_end) & (flags[0] + flags[1] > 0)
        pl.when(wanted)(add_far_span)
    if last:
        for which, block in ((0, low), (1, high)):
            total = jnp.sum(held_ref[0, 1, which], axis=-1, keepdims=True)
            result = (held_ref[0, 0, which] / total).astype(out_ref.dtype)
            out_ref[block] = result.reshape(2, rows, width)


def attend(step, scalars, bias, queries, states, held=None, span_states=None, last=False):
    blocks, pair, rows, width = queries.shape
    assert blocks % 2 == 0 and pair == 2
    one = (1, pair, rows, width)
    held_shape = (blocks // 2, 2, 2, pair * rows, width)
    held_spec = pl.BlockSpec((1,) + held_shape[1:], lambda n: (n, 0, 0, 0, 0))
    operands, in_specs = [scalars], [smem()]
    if bias is not None:
        operands.append(bias)
        in_specs.append(pl.BlockSpec(bias.shape, lambda n: (0, 0)))
    operands += [queries, queries, states]
    in_specs += [
        pl.BlockSpec(one, lambda n: (n, 0, 0, 0)),
        pl.BlockSpec(one, lambda n: (blocks - 1 - n, 0, 0, 0)),
        pl.BlockSpec(states.shape, lambda n: (0, 0, 0, 0)),
    ]
    if span_states is not None:
        operands.append(span_states)
        in_specs.append(pl.BlockSpec(span_states.shape, lambda n: (0, 0, 0)))
    if held is not None:
        operands.append(held)
        in_specs.append(held_spec)
    scratch = [
        pltpu.VMEM((2, pair * rows, width), queries.dtype),
        pltpu.VMEM((blocks, width, rows), queries.dtype),
    ]
    if last:
        out_shape = jax.ShapeDtypeStruct(queries.shape, queries.dtype)
        out_specs = pl.BlockSpec(queries.shape, lambda n: (0, 0, 0, 0))
        scratch = [pltpu.VMEM((1,) + held_shape[1:], jnp.float32)] + scratch
    else:
        out_shape, out_specs = jax.ShapeDtypeStruct(held_shape, jnp.float32), held_spec
    kernel = functools.partial(
        attend_kernel,
        step=step,
        steerable=bias is not None,
        last=last,
        chunk=rows if bias is not None else pair * rows,
    )
    return pl.pallas_call(
        kernel,
        grid=(blocks // 2,),
        in_specs=in_specs,
        out_specs=out_specs,
        out_shape=out_shape,
        scratch_shapes=scratch,
        compiler_params=params(),
        cost_estimate=cost(
            pair * (blocks * rows) ** 2 / (1 if step == 1 else 2),
            8 * queries.size + 8 * pair * blocks * rows * width,
        ),
    )(*operands)


def unpack_kernel(scalars, out_a, out_b, attention, heads_ref):
    for n in range(GROUP):
        for group_head in range(2):
            heads_ref[2 * scalars[n] + group_head] = out_a[n, group_head]
            heads_ref[2 * scalars[GROUP + n] + group_head] = out_b[n, group_head]
    attention[...] = jnp.transpose(heads_ref[...], (1, 0, 2))


def unpack(scalars, out_a, out_b):
    blocks, pair, rows, width = out_a.shape
    heads = 2 * blocks * pair
    return pl.pallas_call(
        unpack_kernel,
        in_specs=[smem()] + [vmem()] * 2,
        out_specs=vmem(),
        out_shape=jax.ShapeDtypeStruct((rows, heads, width), out_a.dtype),
        scratch_shapes=[pltpu.VMEM((heads, rows, width), out_a.dtype)],
        compiler_params=params(),
    )(scalars, out_a, out_b)


def per_device(queries, key_value, damping, span_start, steered_heads):
    rows = queries.shape[0]
    device_count = lax.axis_size("seq")
    assert WINDOW == 2 * GROUP * rows and device_count == 4 * GROUP
    assert key_value.shape[2] == 2 * GROUP and queries.shape[1] == 4 * GROUP
    assert steered_heads.shape[0] <= GROUP
    groups = [
        list(range(first, first + GROUP)) for first in range(0, device_count, GROUP)
    ]

    def exchange(blocks):
        return lax.all_to_all(
            blocks, "seq", split_axis=0, concat_axis=0, axis_index_groups=groups, tiled=True
        )

    def onward(blocks, planes=1):
        shift = planes * GROUP
        pairs = [(n, n + shift) for n in range(device_count - shift)]
        return lax.ppermute(blocks, "seq", pairs)

    def after(value, earlier):
        return lax.optimization_barrier((value, earlier))[0]

    index = lax.axis_index("seq").astype(jnp.int32).reshape(1)
    states_a, states_b, scalars = pack_states(index, span_start, steered_heads, key_value)
    queries_a, queries_b = pack_queries(scalars, queries)
    states_a = exchange(states_a)
    back_a = onward(states_a)
    length = GROUP * rows
    span_states = lax.dynamic_slice_in_dim(
        states_a.transpose(1, 0, 2, 3).reshape(2, length, -1),
        jnp.minimum(span_start[0], length - SPAN),
        SPAN,
        1,
    )
    span_states = onward(span_states, 3)
    position = jnp.arange(damping.shape[0], dtype=jnp.int32)
    emphasized = (position >= span_start[0]) & (position < span_start[0] + SPAN)
    bias = jnp.where(emphasized, 0.0, jnp.log2(damping.astype(jnp.float32)))
    bias = bias.reshape(-1, rows)
    queries_a = exchange(after(queries_a, states_a))
    states_b = exchange(after(states_b, queries_a))
    back_b = onward(states_b)
    queries_b = exchange(after(queries_b, states_b))
    far_a = onward(back_a)
    far_b = onward(after(back_b, far_a))

    held_a = attend(0, scalars, bias, queries_a, states_a)
    held_a = attend(1, scalars, bias, after(queries_a, states_b), back_a, held_a)
    out_a = attend(2, scalars, bias, queries_a, far_a, held_a, span_states, last=True)
    held_b = attend(0, scalars, None, after(queries_b, out_a), states_b)
    out_a = exchange(out_a)
    held_b = attend(1, scalars, None, queries_b, back_b, held_b)
    out_b = attend(2, scalars, None, queries_b, far_b, held_b, last=True)
    out_b = exchange(out_b)
    return unpack(scalars, out_a, out_b)


def solution(mesh):
    in_specs = (
        P(("prompt", "seq"), None, None),
        P(None, ("prompt", "seq"), None, None),
        P("prompt"),
        P("prompt"),
        P(),
    )
    out_specs = P(("prompt", "seq"), None, None)
    return jax.shard_map(
        per_device, mesh=mesh, in_specs=in_specs, out_specs=out_specs, check_vma=False
    )
```

```python
import functools
import math

import jax
import jax.numpy as jnp
from jax import lax
from jax.experimental import pallas as pl
from jax.experimental.pallas import tpu as pltpu
from jax.sharding import PartitionSpec as P

WINDOW = 4096
SPAN = 512

SCORE_SCALE = 144.0 ** (-0.5)
SOFTCAP = 50.0
LOG2_E = math.log2(math.e)

GROUP = 8
PAIR_FLOPS = 512
VMEM_BYTES = 60 * 1024 * 1024

FIRST_SCALAR = 32
PLANE, SPAN_FIRST, STEERED_0, STEERED_1 = range(FIRST_SCALAR, FIRST_SCALAR + 4)
SCALARS = FIRST_SCALAR + 4


def smem():
    return pl.BlockSpec(memory_space=pltpu.SMEM)


def vmem():
    return pl.BlockSpec(memory_space=pltpu.VMEM)


def params():
    return pltpu.CompilerParams(vmem_limit_bytes=VMEM_BYTES)


def cost(pairs, moved):
    return pl.CostEstimate(
        flops=int(pairs * PAIR_FLOPS), bytes_accessed=int(moved), transcendentals=int(2 * pairs)
    )


def pack_states_kernel(
    index_ref, span_ref, steered_ref, states_ref, states_a, states_b, scalars, state_heads
):
    key_heads = states_ref.shape[2]
    steered_count = steered_ref.shape[0]
    steered_keys = [lax.div(steered_ref[n], 2) for n in range(steered_count)]
    flags = []
    for head in range(key_heads):
        hit = steered_keys[0] == head
        for n in range(1, steered_count):
            hit = hit | (steered_keys[n] == head)
        flags.append(hit.astype(jnp.int32))
    total = sum(flags[1:], flags[0])
    before = jnp.int32(0)
    for head in range(key_heads):
        rank = jnp.where(flags[head] == 1, before, total + head - before)
        scalars[rank] = jnp.int32(head)
        before = before + flags[head]
    place = lax.rem(index_ref[0], GROUP)
    scalars[PLANE] = lax.div(index_ref[0], GROUP)
    scalars[SPAN_FIRST] = span_ref[0]
    own_head = scalars[place]
    for group_head in range(2):
        hit = steered_ref[0] == 2 * own_head + group_head
        for n in range(1, steered_count):
            hit = hit | (steered_ref[n] == 2 * own_head + group_head)
        scalars[STEERED_0 + group_head] = hit.astype(jnp.int32)

    for part in range(2):
        state_heads[part] = jnp.transpose(states_ref[part], (1, 0, 2))
        for n in range(GROUP):
            states_a[n, part] = state_heads[part, scalars[n]]
            states_b[n, part] = state_heads[part, scalars[GROUP + n]]


def pack_states(index, span_start, steered_heads, states):
    _, rows, key_heads, width = states.shape
    part = jax.ShapeDtypeStruct((GROUP, 2, rows, width), states.dtype)
    return pl.pallas_call(
        pack_states_kernel,
        in_specs=[smem()] * 3 + [vmem()],
        out_specs=[vmem()] * 2 + [smem()],
        out_shape=[part] * 2 + [jax.ShapeDtypeStruct((SCALARS,), jnp.int32)],
        scratch_shapes=[pltpu.VMEM((2, key_heads, rows, width), states.dtype)],
        compiler_params=params(),
        cost_estimate=cost(0, 8 * states.size),
    )(index, span_start, steered_heads, states)


def pack_queries_kernel(scalars, queries_ref, queries_a, queries_b, query_heads):
    query_heads[...] = jnp.transpose(queries_ref[...], (1, 0, 2))
    for n in range(GROUP):
        for group_head in range(2):
            queries_a[n, group_head] = query_heads[2 * scalars[n] + group_head]
            queries_b[n, group_head] = query_heads[2 * scalars[GROUP + n] + group_head]


def pack_queries(scalars, queries):
    rows, heads, width = queries.shape
    part = jax.ShapeDtypeStruct((GROUP, 2, rows, width), queries.dtype)
    return pl.pallas_call(
        pack_queries_kernel,
        in_specs=[smem(), vmem()],
        out_specs=[vmem()] * 2,
        out_shape=[part] * 2,
        scratch_shapes=[pltpu.VMEM((heads, rows, width), queries.dtype)],
        compiler_params=params(),
        cost_estimate=cost(0, 8 * queries.size),
    )(scalars, queries)


def raw_scores(query, key):
    return lax.dot_general(
        query, key, (((1,), (1,)), ((), ())), preferred_element_type=jnp.float32
    )


def weights(raw_score, bias=None, visible=None):
    score = jnp.tanh(raw_score * (SCORE_SCALE / SOFTCAP)) * (SOFTCAP * LOG2_E)
    pair = (2, score.shape[0] // 2, score.shape[1])
    if bias is not None:
        score = (score.reshape(pair) + bias).reshape(score.shape)
    weight = jnp.exp2(score)
    if visible is not None:
        weight = jnp.where(visible, weight.reshape(pair), 0.0).reshape(score.shape)
    return weight


def lane_sums(weight, lanes):
    sums = weight[:, :lanes]
    for first in range(lanes, weight.shape[1], lanes):
        sums = sums + weight[:, first : first + lanes]
    return sums


def tile(query, key, value, bias=None, visible=None):
    weight = weights(raw_scores(query, key), bias, visible)
    weighted = jnp.dot(
        weight.astype(jnp.bfloat16), value, preferred_element_type=jnp.float32
    )
    return weighted, lane_sums(weight, query.shape[1])


def attend_kernel(*refs, step, steerable, last):
    refs = list(refs)
    scalars = refs.pop(0)
    bias_ref = refs.pop(0) if steerable else None
    low_ref, high_ref, states_ref = refs.pop(0), refs.pop(0), refs.pop(0)
    span_ref = refs.pop(0) if steerable and last else None
    if step:
        old_weighted, old_sums = refs.pop(0), refs.pop(0)
    if last:
        out_ref = refs.pop(0)
    weighted_ref, sums_ref, query_ref = refs
    low = pl.program_id(0)
    blocks, _, rows, width = states_ref.shape
    high = blocks - 1 - low
    plane = scalars[PLANE]
    first_block = (plane - step) * blocks
    query_ref[0] = low_ref[0].reshape(2 * rows, width)
    query_ref[1] = high_ref[0].reshape(2 * rows, width)
    if step:
        weighted_ref[...] = old_weighted[...]
        sums_ref[...] = old_sums[...]
    else:
        weighted_ref[...] = jnp.zeros(weighted_ref.shape, jnp.float32)
        sums_ref[...] = jnp.zeros(sums_ref.shape, jnp.float32)
    flags = [scalars[STEERED_0 + n] for n in range(2)]
    flag_values = [flag.astype(jnp.float32) for flag in flags]

    def states(part, key_block, count):
        if count == 1:
            return states_ref[key_block, part]
        return states_ref[pl.ds(key_block, count), part].reshape(count * rows, width)

    def bias(key_block, count):
        if not steerable:
            return None
        parts = [bias_ref[pl.ds(first_block + key_block + n, 1), :] for n in range(count)]
        row = parts[0] if count == 1 else jnp.concatenate(parts, axis=1)
        return jnp.stack([row * value for value in flag_values])

    def add(tiles):
        ahead = raw_scores(query_ref[tiles[0][0]], states(0, *tiles[0][1:3]))
        for n, (which, key_block, count, visible) in enumerate(tiles):
            raw_score = ahead
            if n + 1 < len(tiles):
                ahead = raw_scores(query_ref[tiles[n + 1][0]], states(0, *tiles[n + 1][1:3]))
            weight = weights(raw_score, bias(key_block, count), visible)
            sums_ref[0, which] += lane_sums(weight, width)
            weighted_ref[0, which] += jnp.dot(
                weight.astype(jnp.bfloat16),
                states(1, key_block, count),
                preferred_element_type=jnp.float32,
            )

    def emphasized(key_block):
        index = (first_block + key_block) * rows + lax.broadcasted_iota(jnp.int32, (1, rows), 1)
        first = scalars[SPAN_FIRST]
        inside = (index >= first) & (index < first + SPAN)
        return jnp.stack([inside & (flag == 1) for flag in flags])

    def compute():
        row = lax.broadcasted_iota(jnp.int32, (rows, rows), 0)
        column = lax.broadcasted_iota(jnp.int32, (rows, rows), 1)
        half = blocks // 2
        if step == 1:
            wide = half if steerable else blocks
            add([(which, n, wide, None) for which in range(2) for n in range(0, blocks, wide)])
            return
        tiles = [(1, 0, half, None) if step == 0 else (0, half, half, None)]
        for n in range(half - 1):
            if step == 0:
                is_low = n < low
                tiles.append(
                    (jnp.where(is_low, 0, 1), jnp.where(is_low, n, half + n - low), 1, None)
                )
            else:
                is_high = n < low
                tiles.append(
                    (jnp.where(is_high, 1, 0), jnp.where(is_high, high + 1 + n, n + 1), 1, None)
                )
        visible = (row >= column if step == 0 else row < column)[None]
        for which, block in ((0, low), (1, high)):
            seen = visible | emphasized(block) if step and steerable else visible
            tiles.append((which, block, 1, seen))
        add(tiles)
        if step == 2 and steerable:
            first = scalars[SPAN_FIRST] - first_block * rows
            span_low = lax.div(jnp.maximum(first, 0), rows)
            span_high = lax.div(jnp.maximum(first + SPAN + rows - 1, 0), rows)
            span_high = jnp.where(flags[0] + flags[1] > 0, span_high, 0)
            for which, block in ((0, low), (1, high)):
                lax.fori_loop(
                    span_low,
                    jnp.minimum(span_high, block),
                    lambda n, c: (add([(which, n, 1, emphasized(n))]), c)[1],
                    0,
                )

    def add_far_span():
        start = scalars[SPAN_FIRST]
        length = blocks * rows
        index = (plane - step - 1) * length + jnp.minimum(start, length - SPAN)
        index = index + lax.broadcasted_iota(jnp.int32, (1, SPAN), 1)
        inside = (index >= start) & (index < start + SPAN)
        visible = jnp.stack([inside & (flag == 1) for flag in flags])
        for which in range(2):
            weighted, sums = tile(query_ref[which], span_ref[0], span_ref[1], None, visible)
            weighted_ref[0, which] += weighted
            sums_ref[0, which] += sums

    if step:
        pl.when(plane >= step)(compute)
    else:
        compute()
    if last and steerable:
        far_end = (plane - step) * blocks * rows
        wanted = (plane > step) & (scalars[SPAN_FIRST] < far_end) & (flags[0] + flags[1] > 0)
        pl.when(wanted)(add_far_span)
    if last:
        write_result(out_ref, weighted_ref, sums_ref, low, high)


def write_result(out_ref, weighted_ref, sums_ref, low, high):
    for which, block in ((0, low), (1, high)):
        total = jnp.sum(sums_ref[0, which], axis=-1, keepdims=True)
        result = (weighted_ref[0, which] / total).astype(out_ref.dtype)
        out_ref[block] = result.reshape(out_ref.shape[1:])


def query_specs(queries):
    blocks, pair, rows, width = queries.shape
    one = (1, pair, rows, width)
    return [
        pl.BlockSpec(one, lambda n: (n, 0, 0, 0)),
        pl.BlockSpec(one, lambda n: (blocks - 1 - n, 0, 0, 0)),
    ]


def held_spec(queries):
    _, pair, rows, width = queries.shape
    return pl.BlockSpec((1, 2, pair * rows, width), lambda n: (n, 0, 0, 0))


def attend(step, scalars, bias, queries, states, carried=None, span_states=None, last=False):
    blocks, pair, rows, width = queries.shape
    assert blocks % 2 == 0 and pair == 2
    held = jax.ShapeDtypeStruct((blocks // 2, 2, pair * rows, width), jnp.float32)
    whole = pl.BlockSpec(states.shape, lambda n: (0, 0, 0, 0))
    operands, in_specs = [scalars], [smem()]
    if bias is not None:
        operands.append(bias)
        in_specs.append(pl.BlockSpec(bias.shape, lambda n: (0, 0)))
    operands += [queries, queries, states]
    in_specs += query_specs(queries) + [whole]
    if span_states is not None:
        operands.append(span_states)
        in_specs.append(pl.BlockSpec(span_states.shape, lambda n: (0, 0, 0)))
    if carried is not None:
        operands += list(carried)
        in_specs += [held_spec(queries)] * 2
    scratch = [pltpu.VMEM((2, pair * rows, width), queries.dtype)]
    if last:
        out_shape = jax.ShapeDtypeStruct(queries.shape, queries.dtype)
        out_specs = pl.BlockSpec(queries.shape, lambda n: (0, 0, 0, 0))
        scratch = [pltpu.VMEM((1, 2, pair * rows, width), jnp.float32)] * 2 + scratch
    else:
        out_shape, out_specs = [held, held], [held_spec(queries)] * 2
    return pl.pallas_call(
        functools.partial(attend_kernel, step=step, steerable=bias is not None, last=last),
        grid=(blocks // 2,),
        in_specs=in_specs,
        out_specs=out_specs,
        out_shape=out_shape,
        scratch_shapes=scratch,
        compiler_params=params(),
        cost_estimate=cost(
            pair * (blocks * rows) ** 2 / (1 if step == 1 else 2),
            8 * queries.size + 8 * pair * blocks * rows * width,
        ),
    )(*operands)


def unpack_kernel(scalars, out_a, out_b, attention, heads_ref):
    for n in range(GROUP):
        for group_head in range(2):
            heads_ref[2 * scalars[n] + group_head] = out_a[n, group_head]
            heads_ref[2 * scalars[GROUP + n] + group_head] = out_b[n, group_head]
    attention[...] = jnp.transpose(heads_ref[...], (1, 0, 2))


def unpack(scalars, out_a, out_b):
    blocks, pair, rows, width = out_a.shape
    heads = 2 * blocks * pair
    return pl.pallas_call(
        unpack_kernel,
        in_specs=[smem()] + [vmem()] * 2,
        out_specs=vmem(),
        out_shape=jax.ShapeDtypeStruct((rows, heads, width), out_a.dtype),
        scratch_shapes=[pltpu.VMEM((heads, rows, width), out_a.dtype)],
        compiler_params=params(),
    )(scalars, out_a, out_b)


def per_device(queries, key_value, damping, span_start, steered_heads):
    rows = queries.shape[0]
    device_count = lax.axis_size("seq")
    assert WINDOW == 2 * GROUP * rows and device_count == 4 * GROUP
    assert key_value.shape[2] == 2 * GROUP and queries.shape[1] == 4 * GROUP
    assert steered_heads.shape[0] <= GROUP
    groups = [
        list(range(first, first + GROUP)) for first in range(0, device_count, GROUP)
    ]

    def exchange(blocks):
        return lax.all_to_all(
            blocks, "seq", split_axis=0, concat_axis=0, axis_index_groups=groups, tiled=True
        )

    def onward(blocks, planes=1):
        shift = planes * GROUP
        pairs = [(n, n + shift) for n in range(device_count - shift)]
        return lax.ppermute(blocks, "seq", pairs)

    def after(value, earlier):
        return lax.optimization_barrier((value, earlier))[0]

    index = lax.axis_index("seq").astype(jnp.int32).reshape(1)
    states_a, states_b, scalars = pack_states(index, span_start, steered_heads, key_value)
    queries_a, queries_b = pack_queries(scalars, queries)
    states_a = exchange(states_a)
    back_a = onward(states_a)
    length = GROUP * rows
    span_states = lax.dynamic_slice_in_dim(
        states_a.transpose(1, 0, 2, 3).reshape(2, length, -1),
        jnp.minimum(span_start[0], length - SPAN),
        SPAN,
        1,
    )
    span_states = onward(span_states, 3)
    position = jnp.arange(damping.shape[0], dtype=jnp.int32)
    emphasized = (position >= span_start[0]) & (position < span_start[0] + SPAN)
    bias = jnp.where(emphasized, 0.0, jnp.log2(damping.astype(jnp.float32)))
    bias = bias.reshape(-1, rows)
    queries_a = exchange(after(queries_a, states_a))
    states_b = exchange(after(states_b, queries_a))
    back_b = onward(states_b)
    queries_b = exchange(after(queries_b, states_b))

    held_a = attend(0, scalars, bias, queries_a, states_a)
    far_a = onward(after(back_a, held_a))
    held_a = attend(1, scalars, bias, after(queries_a, states_b), back_a, held_a)
    held_b = attend(0, scalars, None, after(queries_b, held_a), states_b)
    far_b = onward(after(back_b, held_b))
    out_a = attend(2, scalars, bias, queries_a, far_a, held_a, span_states, last=True)
    held_b = after(held_b, out_a)
    out_a = exchange(out_a)
    held_b = attend(1, scalars, None, queries_b, back_b, held_b)
    out_b = attend(2, scalars, None, queries_b, far_b, held_b, last=True)
    out_b = exchange(out_b)
    return unpack(scalars, out_a, out_b)


def solution(mesh):
    in_specs = (
        P(("prompt", "seq"), None, None),
        P(None, ("prompt", "seq"), None, None),
        P("prompt"),
        P("prompt"),
        P(),
    )
    out_specs = P(("prompt", "seq"), None, None)
    return jax.shard_map(
        per_device, mesh=mesh, in_specs=in_specs, out_specs=out_specs, check_vma=False
    )
```

```python
import functools
import math

import jax
import jax.numpy as jnp
from jax import lax
from jax.experimental import pallas as pl
from jax.experimental.pallas import tpu as pltpu
from jax.sharding import PartitionSpec as P

WINDOW = 4096
SPAN = 512

SCORE_SCALE = 144.0 ** (-0.5)
SOFTCAP = 50.0
LOG2_E = math.log2(math.e)

GROUP = 8
CHUNK = 128
TOKEN_STEPS = 4
PAIR_FLOPS = 256
VMEM_BYTES = 60 * 1024 * 1024

FIRST_SCALAR = 32
PLANE, SPAN_FIRST, STEERED_0, STEERED_1 = range(FIRST_SCALAR, FIRST_SCALAR + 4)
SCALARS = FIRST_SCALAR + 4


def smem():
    return pl.BlockSpec(memory_space=pltpu.SMEM)


def vmem():
    return pl.BlockSpec(memory_space=pltpu.VMEM)


def params():
    return pltpu.CompilerParams(vmem_limit_bytes=VMEM_BYTES)


def cost(pairs, moved):
    return pl.CostEstimate(
        flops=int(pairs * PAIR_FLOPS), bytes_accessed=int(moved), transcendentals=int(2 * pairs)
    )


def pack_kernel(
    index_ref, span_ref, steered_ref, queries_ref, states_ref,
    both_a, both_b, states_b, scalars, query_heads, state_heads,
):
    key_heads = states_ref.shape[2]
    steered_count = steered_ref.shape[0]

    @pl.when(pl.program_id(0) == 0)
    def _():
        steered_keys = [lax.div(steered_ref[n], 2) for n in range(steered_count)]
        flags = []
        for head in range(key_heads):
            hit = steered_keys[0] == head
            for n in range(1, steered_count):
                hit = hit | (steered_keys[n] == head)
            flags.append(hit.astype(jnp.int32))
        total = sum(flags[1:], flags[0])
        before = jnp.int32(0)
        for head in range(key_heads):
            rank = jnp.where(flags[head] == 1, before, total + head - before)
            scalars[rank] = jnp.int32(head)
            before = before + flags[head]
        place = lax.rem(index_ref[0], GROUP)
        scalars[PLANE] = lax.div(index_ref[0], GROUP)
        scalars[SPAN_FIRST] = span_ref[0]
        own_head = scalars[place]
        for group_head in range(2):
            hit = steered_ref[0] == 2 * own_head + group_head
            for n in range(1, steered_count):
                hit = hit | (steered_ref[n] == 2 * own_head + group_head)
            scalars[STEERED_0 + group_head] = hit.astype(jnp.int32)

    for part in range(2):
        state_heads[part] = jnp.transpose(states_ref[part], (1, 0, 2))
        for n in range(GROUP):
            both_a[n, part] = state_heads[part, scalars[n]]
            state = state_heads[part, scalars[GROUP + n]]
            both_b[n, part] = state
            states_b[n, part] = state
    query_heads[...] = jnp.transpose(queries_ref[...], (1, 0, 2))
    for n in range(GROUP):
        for group_head in range(2):
            both_a[n, 2 + group_head] = query_heads[2 * scalars[n] + group_head]
            both_b[n, 2 + group_head] = query_heads[2 * scalars[GROUP + n] + group_head]


def pack(index, span_start, steered_heads, queries, states):
    rows, heads, width = queries.shape
    key_heads = states.shape[2]
    some = rows // TOKEN_STEPS

    def sent(parts):
        shape = jax.ShapeDtypeStruct((GROUP, parts, rows, width), queries.dtype)
        return shape, pl.BlockSpec((GROUP, parts, some, width), lambda n: (0, 0, n, 0))

    shapes, specs = zip(sent(4), sent(4), sent(2))
    return pl.pallas_call(
        pack_kernel,
        grid=(TOKEN_STEPS,),
        in_specs=[smem()] * 3
        + [
            pl.BlockSpec((some, heads, width), lambda n: (n, 0, 0)),
            pl.BlockSpec((2, some, key_heads, width), lambda n: (0, n, 0, 0)),
        ],
        out_specs=list(specs) + [smem()],
        out_shape=list(shapes) + [jax.ShapeDtypeStruct((SCALARS,), jnp.int32)],
        scratch_shapes=[
            pltpu.VMEM((heads, some, width), queries.dtype),
            pltpu.VMEM((2, key_heads, some, width), queries.dtype),
        ],
        compiler_params=params(),
        cost_estimate=cost(0, 4 * (queries.size + states.size)),
    )(index, span_start, steered_heads, queries, states)


def raw_scores(query, key):
    return lax.dot_general(
        query, key, (((1,), (1,)), ((), ())), preferred_element_type=jnp.float32
    )


def weights(raw_score, bias=None, visible=None):
    score = jnp.tanh(raw_score * (SCORE_SCALE / SOFTCAP)) * (SOFTCAP * LOG2_E)
    pair = (2, score.shape[0] // 2, score.shape[1])
    if bias is not None:
        score = (score.reshape(pair) + bias).reshape(score.shape)
    weight = jnp.exp2(score)
    if visible is not None:
        weight = jnp.where(visible, weight.reshape(pair), 0.0).reshape(score.shape)
    return weight


def weights_2d(raw_score, bias, visible):
    score = jnp.tanh(raw_score * (SCORE_SCALE / SOFTCAP)) * (SOFTCAP * LOG2_E)
    weight = jnp.exp2(score + bias)
    return weight if visible is None else jnp.where(visible, weight, 0.0)


def product(left, right):
    return jnp.dot(left, right, preferred_element_type=jnp.float32)


def lane_sums(weight, lanes):
    sums = weight[:, :lanes]
    for first in range(lanes, weight.shape[1], lanes):
        sums = sums + weight[:, first : first + lanes]
    return sums


def tile(query, key, value, bias=None, visible=None):
    weight = weights(raw_scores(query, key), bias, visible)
    weighted = jnp.dot(
        weight.astype(jnp.bfloat16), value, preferred_element_type=jnp.float32
    )
    return weighted, lane_sums(weight, query.shape[1])


def attend_kernel(*refs, step, steerable, last):
    refs = list(refs)
    scalars = refs.pop(0)
    bias_ref = refs.pop(0) if steerable else None
    low_ref, high_ref, states_ref = refs.pop(0), refs.pop(0), refs.pop(0)
    span_ref = refs.pop(0) if steerable and last else None
    if step:
        old_weighted, old_sums = refs.pop(0), refs.pop(0)
    if last:
        out_ref = refs.pop(0)
    weighted_ref, sums_ref, query_ref = refs[:3]
    keys_ref = refs[3] if steerable else None
    low = pl.program_id(0)
    blocks, _, rows, width = states_ref.shape
    high = blocks - 1 - low
    plane = scalars[PLANE]
    first_block = (plane - step) * blocks
    query_ref[0] = low_ref[0].reshape(2 * rows, width)
    query_ref[1] = high_ref[0].reshape(2 * rows, width)
    if step:
        weighted_ref[...] = old_weighted[...]
        sums_ref[...] = old_sums[...]
    else:
        weighted_ref[...] = jnp.zeros(weighted_ref.shape, jnp.float32)
        sums_ref[...] = jnp.zeros(sums_ref.shape, jnp.float32)
    flags = [scalars[STEERED_0 + n] for n in range(2)]
    flag_values = [flag.astype(jnp.float32) for flag in flags]

    def states(part, key_block, count):
        if count == 1:
            return states_ref[key_block, part]
        return states_ref[pl.ds(key_block, count), part].reshape(count * rows, width)

    def bias(key_block, count):
        if not steerable:
            return None
        parts = [bias_ref[pl.ds(first_block + key_block + n, 1), :] for n in range(count)]
        row = parts[0] if count == 1 else jnp.concatenate(parts, axis=1)
        return jnp.stack([row * value for value in flag_values])

    def add(tiles):
        ahead = raw_scores(query_ref[tiles[0][0]], states(0, *tiles[0][1:3]))
        for n, (which, key_block, count, visible) in enumerate(tiles):
            raw_score = ahead
            if n + 1 < len(tiles):
                ahead = raw_scores(query_ref[tiles[n + 1][0]], states(0, *tiles[n + 1][1:3]))
            weight = weights(raw_score, bias(key_block, count), visible)
            sums_ref[0, which] += lane_sums(weight, width)
            weighted_ref[0, which] += jnp.dot(
                weight.astype(jnp.bfloat16),
                states(1, key_block, count),
                preferred_element_type=jnp.float32,
            )

    if steerable:

        @pl.when(low == 0)
        def _():
            for n in range(blocks):
                keys_ref[n] = states_ref[n, 0].T

    def narrow_score(which, first, key_block):
        return product(query_ref[which, pl.ds(first, CHUNK), :], keys_ref[key_block])

    def add_narrow(tiles):
        units = [
            (which, first, key_block, visible)
            for which, key_block, _, visible in tiles
            for first in range(0, 2 * rows, CHUNK)
        ]
        ahead = narrow_score(*units[0][:3])
        for n, (which, first, key_block, visible) in enumerate(units):
            raw_score = ahead
            if n + 1 < len(units):
                ahead = narrow_score(*units[n + 1][:3])
            head, start = first // rows, first % rows
            if visible is not None:
                own = visible[head if visible.shape[0] > 1 else 0]
                visible = own if own.shape[0] == 1 else own[start : start + CHUNK]
            row = bias_ref[pl.ds(first_block + key_block, 1), :] * flag_values[head]
            weight = weights_2d(raw_score, row, visible)
            some = pl.ds(first, CHUNK)
            sums_ref[0, which, some, :] += lane_sums(weight, width)
            weighted_ref[0, which, some, :] += product(
                weight.astype(jnp.bfloat16), states_ref[key_block, 1]
            )

    def add_all_narrow():
        rows_of = [(which, first) for which in range(2) for first in range(0, 2 * rows, CHUNK)]
        ahead = narrow_score(0, 0, 0)
        for at, (which, first) in enumerate(rows_of):
            weighted = sums = None
            for n in range(blocks):
                raw_score = ahead
                if n + 1 < blocks:
                    ahead = narrow_score(which, first, n + 1)
                elif at + 1 < len(rows_of):
                    ahead = narrow_score(*rows_of[at + 1], 0)
                row = bias_ref[pl.ds(first_block + n, 1), :] * flag_values[first // rows]
                weight = weights_2d(raw_score, row, None)
                more_sums = lane_sums(weight, width)
                more = product(weight.astype(jnp.bfloat16), states_ref[n, 1])
                sums = more_sums if n == 0 else sums + more_sums
                weighted = more if n == 0 else weighted + more
            some = pl.ds(first, CHUNK)
            sums_ref[0, which, some, :] += sums
            weighted_ref[0, which, some, :] += weighted

    def emphasized(key_block):
        index = (first_block + key_block) * rows + lax.broadcasted_iota(jnp.int32, (1, rows), 1)
        first = scalars[SPAN_FIRST]
        inside = (index >= first) & (index < first + SPAN)
        return jnp.stack([inside & (flag == 1) for flag in flags])

    def compute():
        row = lax.broadcasted_iota(jnp.int32, (rows, rows), 0)
        column = lax.broadcasted_iota(jnp.int32, (rows, rows), 1)
        if step == 1 and steerable:
            add_all_narrow()
            return
        if step == 1:
            add([(which, n, 2, None) for which in range(2) for n in range(0, blocks, 2)])
            return
        tiles = []
        for n in range(blocks - 1):
            if step == 0:
                is_low = n < low
                tiles.append((jnp.where(is_low, 0, 1), jnp.where(is_low, n, n - low), 1, None))
            else:
                is_high = n < low
                tiles.append(
                    (jnp.where(is_high, 1, 0), jnp.where(is_high, high + 1 + n, n + 1), 1, None)
                )
        visible = (row >= column if step == 0 else row < column)[None]
        for which, block in ((0, low), (1, high)):
            seen = visible | emphasized(block) if step and steerable else visible
            tiles.append((which, block, 1, seen))
        if steerable:
            add_narrow(tiles)
        else:
            add(tiles)
        if step == 2 and steerable:
            first = scalars[SPAN_FIRST] - first_block * rows
            span_low = lax.div(jnp.maximum(first, 0), rows)
            span_high = lax.div(jnp.maximum(first + SPAN + rows - 1, 0), rows)
            span_high = jnp.where(flags[0] + flags[1] > 0, span_high, 0)
            for which, block in ((0, low), (1, high)):
                lax.fori_loop(
                    span_low,
                    jnp.minimum(span_high, block),
                    lambda n, c, which=which: (add_narrow([(which, n, 1, emphasized(n))]), c)[1],
                    0,
                )

    def add_far_span():
        start = scalars[SPAN_FIRST]
        length = blocks * rows
        index = (plane - step - 1) * length + jnp.minimum(start, length - SPAN)
        index = index + lax.broadcasted_iota(jnp.int32, (1, SPAN), 1)
        inside = (index >= start) & (index < start + SPAN)
        visible = jnp.stack([inside & (flag == 1) for flag in flags])
        for which in range(2):
            weighted, sums = tile(query_ref[which], span_ref[0], span_ref[1], None, visible)
            weighted_ref[0, which] += weighted
            sums_ref[0, which] += sums

    if step:
        pl.when(plane >= step)(compute)
    else:
        compute()
    if last and steerable:
        far_end = (plane - step) * blocks * rows
        wanted = (plane > step) & (scalars[SPAN_FIRST] < far_end) & (flags[0] + flags[1] > 0)
        pl.when(wanted)(add_far_span)
    if last:
        write_result(out_ref, weighted_ref, sums_ref, low, high)


def write_result(out_ref, weighted_ref, sums_ref, low, high):
    for which, block in ((0, low), (1, high)):
        total = jnp.sum(sums_ref[0, which], axis=-1, keepdims=True)
        result = (weighted_ref[0, which] / total).astype(out_ref.dtype)
        out_ref[block] = result.reshape(out_ref.shape[1:])


def query_specs(both):
    blocks, _, rows, width = both.shape
    one = (1, 2, rows, width)
    return [
        pl.BlockSpec(one, lambda n: (n, 1, 0, 0)),
        pl.BlockSpec(one, lambda n: (blocks - 1 - n, 1, 0, 0)),
    ]


def held_spec(both):
    _, _, rows, width = both.shape
    return pl.BlockSpec((1, 2, 2 * rows, width), lambda n: (n, 0, 0, 0))


def attend(step, scalars, bias, both, states, carried=None, span_states=None, last=False):
    blocks, parts, rows, width = both.shape
    pair = 2
    assert blocks % 2 == 0 and parts == 2 + pair
    held = jax.ShapeDtypeStruct((blocks // 2, 2, pair * rows, width), jnp.float32)
    whole = pl.BlockSpec((blocks, 2, rows, width), lambda n: (0, 0, 0, 0))
    operands, in_specs = [scalars], [smem()]
    if bias is not None:
        operands.append(bias)
        in_specs.append(pl.BlockSpec(bias.shape, lambda n: (0, 0)))
    operands += [both, both, states]
    in_specs += query_specs(both) + [whole]
    if span_states is not None:
        operands.append(span_states)
        in_specs.append(pl.BlockSpec(span_states.shape, lambda n: (0, 0, 0)))
    if carried is not None:
        operands += list(carried)
        in_specs += [held_spec(both)] * 2
    scratch = [pltpu.VMEM((2, pair * rows, width), both.dtype)]
    if bias is not None:
        scratch.append(pltpu.VMEM((blocks, width, rows), both.dtype))
    if last:
        out_shape = jax.ShapeDtypeStruct((blocks, pair, rows, width), both.dtype)
        out_specs = pl.BlockSpec(out_shape.shape, lambda n: (0, 0, 0, 0))
        scratch = [pltpu.VMEM((1, 2, pair * rows, width), jnp.float32)] * 2 + scratch
    else:
        out_shape, out_specs = [held, held], [held_spec(both)] * 2
    return pl.pallas_call(
        functools.partial(attend_kernel, step=step, steerable=bias is not None, last=last),
        grid=(blocks // 2,),
        in_specs=in_specs,
        out_specs=out_specs,
        out_shape=out_shape,
        scratch_shapes=scratch,
        compiler_params=params(),
        cost_estimate=cost(
            pair * (blocks * rows) ** 2 / (1 if step == 1 else 2),
            4 * both.size + 8 * pair * blocks * rows * width,
        ),
    )(*operands)


def unpack_kernel(scalars, out_a, out_b, attention, heads_ref):
    for n in range(GROUP):
        for group_head in range(2):
            heads_ref[2 * scalars[n] + group_head] = out_a[n, group_head]
            heads_ref[2 * scalars[GROUP + n] + group_head] = out_b[n, group_head]
    attention[...] = jnp.transpose(heads_ref[...], (1, 0, 2))


def unpack(scalars, out_a, out_b):
    blocks, pair, rows, width = out_a.shape
    heads = 2 * blocks * pair
    some = rows // TOKEN_STEPS
    received = pl.BlockSpec((blocks, pair, some, width), lambda n: (0, 0, n, 0))
    return pl.pallas_call(
        unpack_kernel,
        grid=(TOKEN_STEPS,),
        in_specs=[smem(), received, received],
        out_specs=pl.BlockSpec((some, heads, width), lambda n: (n, 0, 0)),
        out_shape=jax.ShapeDtypeStruct((rows, heads, width), out_a.dtype),
        scratch_shapes=[pltpu.VMEM((heads, some, width), out_a.dtype)],
        compiler_params=params(),
        cost_estimate=cost(0, 8 * out_a.size),
    )(scalars, out_a, out_b)


def per_device(queries, key_value, damping, span_start, steered_heads):
    rows = queries.shape[0]
    device_count = lax.axis_size("seq")
    assert WINDOW == 2 * GROUP * rows and device_count == 4 * GROUP
    assert key_value.shape[2] == 2 * GROUP and queries.shape[1] == 4 * GROUP
    assert steered_heads.shape[0] <= GROUP
    groups = [
        list(range(first, first + GROUP)) for first in range(0, device_count, GROUP)
    ]

    def exchange(blocks):
        return lax.all_to_all(
            blocks, "seq", split_axis=0, concat_axis=0, axis_index_groups=groups, tiled=True
        )

    def onward(blocks, planes=1):
        shift = planes * GROUP
        pairs = [(n, n + shift) for n in range(device_count - shift)]
        return lax.ppermute(blocks, "seq", pairs)

    def after(value, earlier):
        return lax.optimization_barrier((value, earlier))[0]

    index = lax.axis_index("seq").astype(jnp.int32).reshape(1)
    both_a, both_b, states_b, scalars = pack(
        index, span_start, steered_heads, queries, key_value
    )
    position = jnp.arange(damping.shape[0], dtype=jnp.int32)
    emphasized = (position >= span_start[0]) & (position < span_start[0] + SPAN)
    bias = jnp.where(emphasized, 0.0, jnp.log2(damping.astype(jnp.float32)))
    bias = bias.reshape(-1, rows)

    raw_b = onward(states_b)
    both_a = exchange(both_a)
    states_a = both_a[:, :2]
    back_a = onward(after(states_a, raw_b))
    length = GROUP * rows
    span_states = lax.dynamic_slice_in_dim(
        states_a.transpose(1, 0, 2, 3).reshape(2, length, -1),
        jnp.minimum(span_start[0], length - SPAN),
        SPAN,
        1,
    )
    span_states = onward(span_states, 3)
    both_b = exchange(after(both_b, both_a))
    back_b = exchange(after(raw_b, (both_b, back_a)))
    far_a = onward(back_a)
    far_b = onward(back_b)

    held_a = attend(0, scalars, bias, after(both_a, raw_b), both_a)
    held_a = attend(1, scalars, bias, both_a, back_a, held_a)
    held_b = attend(0, scalars, None, after(both_b, held_a), both_b)
    held_b = attend(1, scalars, None, both_b, back_b, held_b)
    out_a = attend(
        2, scalars, bias, both_a, far_a, after(held_a, held_b), span_states, last=True
    )
    out_a = exchange(out_a)
    out_b = attend(2, scalars, None, both_b, far_b, after(held_b, far_a), last=True)
    out_b = exchange(out_b)
    return unpack(scalars, out_a, out_b)


def solution(mesh):
    in_specs = (
        P(("prompt", "seq"), None, None),
        P(None, ("prompt", "seq"), None, None),
        P("prompt"),
        P("prompt"),
        P(),
    )
    out_specs = P(("prompt", "seq"), None, None)
    return jax.shard_map(
        per_device, mesh=mesh, in_specs=in_specs, out_specs=out_specs, check_vma=False
    )
```

```python
import functools
import math

import jax
import jax.numpy as jnp
from jax import lax
from jax.experimental import pallas as pl
from jax.experimental.pallas import tpu as pltpu
from jax.sharding import PartitionSpec as P

WINDOW = 4096
SPAN = 512

SCORE_SCALE = 144.0 ** (-0.5)
SOFTCAP = 50.0
LOG2_E = math.log2(math.e)

GROUP = 8
TOKEN_STEPS = 4
PAIR_FLOPS = 256
VMEM_BYTES = 48 * 1024 * 1024

FIRST_SCALAR = 32
PLANE, SPAN_FIRST, STEERED_0, STEERED_1 = range(FIRST_SCALAR, FIRST_SCALAR + 4)
SCALARS = FIRST_SCALAR + 4


def smem():
    return pl.BlockSpec(memory_space=pltpu.SMEM)


def vmem():
    return pl.BlockSpec(memory_space=pltpu.VMEM)


def params():
    return pltpu.CompilerParams(vmem_limit_bytes=VMEM_BYTES)


def cost(pairs, moved):
    return pl.CostEstimate(
        flops=int(pairs * PAIR_FLOPS), bytes_accessed=int(moved), transcendentals=int(2 * pairs)
    )


def pack_kernel(
    index_ref, span_ref, steered_ref, queries_ref, states_ref,
    both_a, states_b, queries_b, scalars, query_heads, state_heads,
):
    key_heads = states_ref.shape[2]
    steered_count = steered_ref.shape[0]

    @pl.when(pl.program_id(0) == 0)
    def _():
        steered_keys = [lax.div(steered_ref[n], 2) for n in range(steered_count)]
        flags = []
        for head in range(key_heads):
            hit = steered_keys[0] == head
            for n in range(1, steered_count):
                hit = hit | (steered_keys[n] == head)
            flags.append(hit.astype(jnp.int32))
        total = sum(flags[1:], flags[0])
        before = jnp.int32(0)
        for head in range(key_heads):
            rank = jnp.where(flags[head] == 1, before, total + head - before)
            scalars[rank] = jnp.int32(head)
            before = before + flags[head]
        place = lax.rem(index_ref[0], GROUP)
        scalars[PLANE] = lax.div(index_ref[0], GROUP)
        scalars[SPAN_FIRST] = span_ref[0]
        own_head = scalars[place]
        for group_head in range(2):
            hit = steered_ref[0] == 2 * own_head + group_head
            for n in range(1, steered_count):
                hit = hit | (steered_ref[n] == 2 * own_head + group_head)
            scalars[STEERED_0 + group_head] = hit.astype(jnp.int32)

    for part in range(2):
        state_heads[part] = jnp.transpose(states_ref[part], (1, 0, 2))
        for n in range(GROUP):
            both_a[n, part] = state_heads[part, scalars[n]]
            states_b[n, part] = state_heads[part, scalars[GROUP + n]]
    query_heads[...] = jnp.transpose(queries_ref[...], (1, 0, 2))
    for n in range(GROUP):
        for group_head in range(2):
            both_a[n, 2 + group_head] = query_heads[2 * scalars[n] + group_head]
            queries_b[n, group_head] = query_heads[2 * scalars[GROUP + n] + group_head]


def pack(index, span_start, steered_heads, queries, states):
    rows, heads, width = queries.shape
    key_heads = states.shape[2]
    some = rows // TOKEN_STEPS

    def sent(parts):
        shape = jax.ShapeDtypeStruct((GROUP, parts, rows, width), queries.dtype)
        return shape, pl.BlockSpec((GROUP, parts, some, width), lambda n: (0, 0, n, 0))

    shapes, specs = zip(sent(4), sent(2), sent(2))
    return pl.pallas_call(
        pack_kernel,
        grid=(TOKEN_STEPS,),
        in_specs=[smem()] * 3
        + [
            pl.BlockSpec((some, heads, width), lambda n: (n, 0, 0)),
            pl.BlockSpec((2, some, key_heads, width), lambda n: (0, n, 0, 0)),
        ],
        out_specs=list(specs) + [smem()],
        out_shape=list(shapes) + [jax.ShapeDtypeStruct((SCALARS,), jnp.int32)],
        scratch_shapes=[
            pltpu.VMEM((heads, some, width), queries.dtype),
            pltpu.VMEM((2, key_heads, some, width), queries.dtype),
        ],
        compiler_params=params(),
        cost_estimate=cost(0, 4 * (queries.size + states.size)),
    )(index, span_start, steered_heads, queries, states)


def raw_scores(query, key):
    return lax.dot_general(
        query, key, (((1,), (1,)), ((), ())), preferred_element_type=jnp.float32
    )


def weights(raw_score, bias=None, visible=None):
    score = jnp.tanh(raw_score * (SCORE_SCALE / SOFTCAP)) * (SOFTCAP * LOG2_E)
    pair = (2, score.shape[0] // 2, score.shape[1])
    if bias is not None:
        score = (score.reshape(pair) + bias).reshape(score.shape)
    weight = jnp.exp2(score)
    if visible is not None:
        weight = jnp.where(visible, weight.reshape(pair), 0.0).reshape(score.shape)
    return weight


def lane_sums(weight, lanes):
    sums = weight[:, :lanes]
    for first in range(lanes, weight.shape[1], lanes):
        sums = sums + weight[:, first : first + lanes]
    return sums


def tile(query, key, value, bias=None, visible=None):
    weight = weights(raw_scores(query, key), bias, visible)
    weighted = jnp.dot(
        weight.astype(jnp.bfloat16), value, preferred_element_type=jnp.float32
    )
    return weighted, lane_sums(weight, query.shape[1])


def attend_kernel(*refs, step, steerable, last):
    refs = list(refs)
    scalars = refs.pop(0)
    bias_ref = refs.pop(0) if steerable else None
    low_ref, high_ref, states_ref = refs.pop(0), refs.pop(0), refs.pop(0)
    span_ref = refs.pop(0) if steerable and last else None
    if step:
        old_weighted, old_sums = refs.pop(0), refs.pop(0)
    if last:
        out_ref = refs.pop(0)
    weighted_ref, sums_ref, query_ref = refs
    low = pl.program_id(0)
    blocks, _, rows, width = states_ref.shape
    high = blocks - 1 - low
    plane = scalars[PLANE]
    first_block = (plane - step) * blocks
    query_ref[0] = low_ref[0].reshape(2 * rows, width)
    query_ref[1] = high_ref[0].reshape(2 * rows, width)
    if step:
        weighted_ref[...] = old_weighted[...]
        sums_ref[...] = old_sums[...]
    else:
        weighted_ref[...] = jnp.zeros(weighted_ref.shape, jnp.float32)
        sums_ref[...] = jnp.zeros(sums_ref.shape, jnp.float32)
    flags = [scalars[STEERED_0 + n] for n in range(2)]
    flag_values = [flag.astype(jnp.float32) for flag in flags]

    def states(part, key_block, count):
        if count == 1:
            return states_ref[key_block, part]
        return states_ref[pl.ds(key_block, count), part].reshape(count * rows, width)

    def bias(key_block, count):
        if not steerable:
            return None
        parts = [bias_ref[pl.ds(first_block + key_block + n, 1), :] for n in range(count)]
        row = parts[0] if count == 1 else jnp.concatenate(parts, axis=1)
        return jnp.stack([row * value for value in flag_values])

    def add(tiles):
        ahead = raw_scores(query_ref[tiles[0][0]], states(0, *tiles[0][1:3]))
        for n, (which, key_block, count, visible) in enumerate(tiles):
            raw_score = ahead
            if n + 1 < len(tiles):
                ahead = raw_scores(query_ref[tiles[n + 1][0]], states(0, *tiles[n + 1][1:3]))
            weight = weights(raw_score, bias(key_block, count), visible)
            sums_ref[0, which] += lane_sums(weight, width)
            weighted_ref[0, which] += jnp.dot(
                weight.astype(jnp.bfloat16),
                states(1, key_block, count),
                preferred_element_type=jnp.float32,
            )

    def emphasized(key_block):
        index = (first_block + key_block) * rows + lax.broadcasted_iota(jnp.int32, (1, rows), 1)
        first = scalars[SPAN_FIRST]
        inside = (index >= first) & (index < first + SPAN)
        return jnp.stack([inside & (flag == 1) for flag in flags])

    def compute():
        row = lax.broadcasted_iota(jnp.int32, (rows, rows), 0)
        column = lax.broadcasted_iota(jnp.int32, (rows, rows), 1)
        if step == 1:
            add([(which, n, 2, None) for which in range(2) for n in range(0, blocks, 2)])
            return
        tiles = []
        for n in range(blocks - 1):
            if step == 0:
                is_low = n < low
                tiles.append((jnp.where(is_low, 0, 1), jnp.where(is_low, n, n - low), 1, None))
            else:
                is_high = n < low
                tiles.append(
                    (jnp.where(is_high, 1, 0), jnp.where(is_high, high + 1 + n, n + 1), 1, None)
                )
        visible = (row >= column if step == 0 else row < column)[None]
        for which, block in ((0, low), (1, high)):
            seen = visible | emphasized(block) if step and steerable else visible
            tiles.append((which, block, 1, seen))
        add(tiles)
        if step == 2 and steerable:
            first = scalars[SPAN_FIRST] - first_block * rows
            span_low = lax.div(jnp.maximum(first, 0), rows)
            span_high = lax.div(jnp.maximum(first + SPAN + rows - 1, 0), rows)
            span_high = jnp.where(flags[0] + flags[1] > 0, span_high, 0)
            for which, block in ((0, low), (1, high)):
                lax.fori_loop(
                    span_low,
                    jnp.minimum(span_high, block),
                    lambda n, c, which=which: (add([(which, n, 1, emphasized(n))]), c)[1],
                    0,
                )

    def add_far_span():
        start = scalars[SPAN_FIRST]
        length = blocks * rows
        index = (plane - step - 1) * length + jnp.minimum(start, length - SPAN)
        index = index + lax.broadcasted_iota(jnp.int32, (1, SPAN), 1)
        inside = (index >= start) & (index < start + SPAN)
        visible = jnp.stack([inside & (flag == 1) for flag in flags])
        for which in range(2):
            weighted, sums = tile(query_ref[which], span_ref[0], span_ref[1], None, visible)
            weighted_ref[0, which] += weighted
            sums_ref[0, which] += sums

    if step:
        pl.when(plane >= step)(compute)
    else:
        compute()
    if last and steerable:
        far_end = (plane - step) * blocks * rows
        wanted = (plane > step) & (scalars[SPAN_FIRST] < far_end) & (flags[0] + flags[1] > 0)
        pl.when(wanted)(add_far_span)
    if last:
        write_result(out_ref, weighted_ref, sums_ref, low, high)


def write_result(out_ref, weighted_ref, sums_ref, low, high):
    for which, block in ((0, low), (1, high)):
        total = jnp.sum(sums_ref[0, which], axis=-1, keepdims=True)
        result = (weighted_ref[0, which] / total).astype(out_ref.dtype)
        out_ref[block] = result.reshape(out_ref.shape[1:])


def query_specs(both):
    blocks, _, rows, width = both.shape
    one = (1, 2, rows, width)
    return [
        pl.BlockSpec(one, lambda n: (n, 1, 0, 0)),
        pl.BlockSpec(one, lambda n: (blocks - 1 - n, 1, 0, 0)),
    ]


def held_spec(both):
    _, _, rows, width = both.shape
    return pl.BlockSpec((1, 2, 2 * rows, width), lambda n: (n, 0, 0, 0))


def attend(step, scalars, bias, both, states, carried=None, span_states=None, last=False):
    blocks, parts, rows, width = both.shape
    pair = 2
    assert blocks % 2 == 0 and parts == 2 + pair
    held = pltpu.HBM((blocks // 2, 2, pair * rows, width), jnp.float32)
    whole = pl.BlockSpec((blocks, 2, rows, width), lambda n: (0, 0, 0, 0))
    operands, in_specs = [scalars], [smem()]
    if bias is not None:
        operands.append(bias)
        in_specs.append(pl.BlockSpec(bias.shape, lambda n: (0, 0)))
    operands += [both, both, states]
    in_specs += query_specs(both) + [whole]
    if span_states is not None:
        operands.append(span_states)
        in_specs.append(pl.BlockSpec(span_states.shape, lambda n: (0, 0, 0)))
    if carried is not None:
        operands += list(carried)
        in_specs += [held_spec(both)] * 2
    scratch = [pltpu.VMEM((2, pair * rows, width), both.dtype)]
    if last:
        out_shape = jax.ShapeDtypeStruct((blocks, pair, rows, width), both.dtype)
        out_specs = pl.BlockSpec(out_shape.shape, lambda n: (0, 0, 0, 0))
        scratch = [pltpu.VMEM((1, 2, pair * rows, width), jnp.float32)] * 2 + scratch
    else:
        out_shape, out_specs = [held, held], [held_spec(both)] * 2
    return pl.pallas_call(
        functools.partial(attend_kernel, step=step, steerable=bias is not None, last=last),
        grid=(blocks // 2,),
        in_specs=in_specs,
        out_specs=out_specs,
        out_shape=out_shape,
        scratch_shapes=scratch,
        compiler_params=params(),
        cost_estimate=cost(
            pair * (blocks * rows) ** 2 / (1 if step == 1 else 2),
            4 * both.size + 8 * pair * blocks * rows * width,
        ),
    )(*operands)


def unpack_kernel(scalars, out_a, out_b, attention, heads_ref):
    for n in range(GROUP):
        for group_head in range(2):
            heads_ref[2 * scalars[n] + group_head] = out_a[n, group_head]
            heads_ref[2 * scalars[GROUP + n] + group_head] = out_b[n, group_head]
    attention[...] = jnp.transpose(heads_ref[...], (1, 0, 2))


def unpack(scalars, out_a, out_b):
    blocks, pair, rows, width = out_a.shape
    heads = 2 * blocks * pair
    return pl.pallas_call(
        unpack_kernel,
        in_specs=[smem(), vmem(), vmem()],
        out_specs=vmem(),
        out_shape=jax.ShapeDtypeStruct((rows, heads, width), out_a.dtype),
        scratch_shapes=[pltpu.VMEM((heads, rows, width), out_a.dtype)],
        compiler_params=params(),
        cost_estimate=cost(0, 8 * out_a.size),
    )(scalars, out_a, out_b)


def per_device(queries, key_value, damping, span_start, steered_heads):
    rows = queries.shape[0]
    device_count = lax.axis_size("seq")
    assert WINDOW == 2 * GROUP * rows and device_count == 4 * GROUP
    assert key_value.shape[2] == 2 * GROUP and queries.shape[1] == 4 * GROUP
    assert steered_heads.shape[0] <= GROUP
    groups = [
        list(range(first, first + GROUP)) for first in range(0, device_count, GROUP)
    ]

    def exchange(blocks):
        return lax.all_to_all(
            blocks, "seq", split_axis=0, concat_axis=0, axis_index_groups=groups, tiled=True
        )

    def onward(blocks, planes=1):
        shift = planes * GROUP
        pairs = [(n, n + shift) for n in range(device_count - shift)]
        return lax.ppermute(blocks, "seq", pairs)

    def after(value, earlier):
        return lax.optimization_barrier((value, earlier))[0]

    index = lax.axis_index("seq").astype(jnp.int32).reshape(1)
    both_a, states_b, queries_b, scalars = pack(
        index, span_start, steered_heads, queries, key_value
    )
    both_b = jnp.concatenate([states_b, queries_b], axis=1)
    position = jnp.arange(damping.shape[0], dtype=jnp.int32)
    emphasized = (position >= span_start[0]) & (position < span_start[0] + SPAN)
    bias = jnp.where(emphasized, 0.0, jnp.log2(damping.astype(jnp.float32)))
    bias = bias.reshape(-1, rows)

    raw_b = onward(states_b)
    both_a = exchange(both_a)
    states_a = both_a[:, :2]
    back_a = onward(after(states_a, raw_b))
    length = GROUP * rows
    span_states = lax.dynamic_slice_in_dim(
        states_a.transpose(1, 0, 2, 3).reshape(2, length, -1),
        jnp.minimum(span_start[0], length - SPAN),
        SPAN,
        1,
    )
    span_states = onward(span_states, 3)
    both_b = exchange(after(both_b, both_a))
    held_a = attend(0, scalars, bias, after(both_a, raw_b), both_a)
    far_a = onward(back_a)
    held_a = attend(1, scalars, bias, both_a, back_a, held_a)
    back_b = exchange(after(raw_b, (both_b, held_a)))
    held_b = attend(0, scalars, None, after(both_b, held_a), both_b)
    far_b = onward(back_b)
    out_a = attend(
        2, scalars, bias, both_a, far_a, after(held_a, held_b), span_states, last=True
    )
    held_b = attend(1, scalars, None, both_b, back_b, after(held_b, out_a))
    out_a = exchange(out_a)
    out_b = attend(2, scalars, None, both_b, far_b, held_b, last=True)
    out_b = exchange(out_b)
    return unpack(scalars, out_a, out_b)


def solution(mesh):
    in_specs = (
        P(("prompt", "seq"), None, None),
        P(None, ("prompt", "seq"), None, None),
        P("prompt"),
        P("prompt"),
        P(),
    )
    out_specs = P(("prompt", "seq"), None, None)
    return jax.shard_map(
        per_device, mesh=mesh, in_specs=in_specs, out_specs=out_specs, check_vma=False
    )
```

```python
import functools
import math

import jax
import jax.numpy as jnp
from jax import lax
from jax.experimental import pallas as pl
from jax.experimental.pallas import tpu as pltpu
from jax.sharding import PartitionSpec as P

WINDOW = 4096
SPAN = 512

SCORE_SCALE = 144.0 ** (-0.5)
SOFTCAP = 50.0
LOG2_E = math.log2(math.e)

GROUP = 8
TOKEN_STEPS = 4
PAIR_FLOPS = 256
VMEM_BYTES = 48 * 1024 * 1024

FIRST_SCALAR = 32
PLANE, SPAN_FIRST, STEERED_0, STEERED_1 = range(FIRST_SCALAR, FIRST_SCALAR + 4)
SCALARS = FIRST_SCALAR + 4


def smem():
    return pl.BlockSpec(memory_space=pltpu.SMEM)


def vmem():
    return pl.BlockSpec(memory_space=pltpu.VMEM)


def in_hbm(operand):
    return pltpu.with_memory_space_constraint(operand, pltpu.HBM)


def params():
    return pltpu.CompilerParams(vmem_limit_bytes=VMEM_BYTES)


def cost(pairs, moved):
    return pl.CostEstimate(
        flops=int(pairs * PAIR_FLOPS), bytes_accessed=int(moved), transcendentals=int(2 * pairs)
    )


def pack_kernel(
    index_ref, span_ref, steered_ref, queries_ref, states_ref,
    both_a, states_b, queries_b, scalars, query_heads, state_heads,
):
    key_heads = states_ref.shape[2]
    steered_count = steered_ref.shape[0]

    @pl.when(pl.program_id(0) == 0)
    def _():
        steered_keys = [lax.div(steered_ref[n], 2) for n in range(steered_count)]
        flags = []
        for head in range(key_heads):
            hit = steered_keys[0] == head
            for n in range(1, steered_count):
                hit = hit | (steered_keys[n] == head)
            flags.append(hit.astype(jnp.int32))
        total = sum(flags[1:], flags[0])
        before = jnp.int32(0)
        for head in range(key_heads):
            rank = jnp.where(flags[head] == 1, before, total + head - before)
            scalars[rank] = jnp.int32(head)
            before = before + flags[head]
        place = lax.rem(index_ref[0], GROUP)
        scalars[PLANE] = lax.div(index_ref[0], GROUP)
        scalars[SPAN_FIRST] = span_ref[0]
        own_head = scalars[place]
        for group_head in range(2):
            hit = steered_ref[0] == 2 * own_head + group_head
            for n in range(1, steered_count):
                hit = hit | (steered_ref[n] == 2 * own_head + group_head)
            scalars[STEERED_0 + group_head] = hit.astype(jnp.int32)

    for part in range(2):
        state_heads[part] = jnp.transpose(states_ref[part], (1, 0, 2))
        for n in range(GROUP):
            both_a[n, part] = state_heads[part, scalars[n]]
            states_b[n, part] = state_heads[part, scalars[GROUP + n]]
    query_heads[...] = jnp.transpose(queries_ref[...], (1, 0, 2))
    for n in range(GROUP):
        for group_head in range(2):
            both_a[n, 2 + group_head] = query_heads[2 * scalars[n] + group_head]
            queries_b[n, group_head] = query_heads[2 * scalars[GROUP + n] + group_head]


def pack(index, span_start, steered_heads, queries, states):
    rows, heads, width = queries.shape
    key_heads = states.shape[2]
    some = rows // TOKEN_STEPS

    def sent(parts):
        shape = pltpu.HBM((GROUP, parts, rows, width), queries.dtype)
        return shape, pl.BlockSpec((GROUP, parts, some, width), lambda n: (0, 0, n, 0))

    shapes, specs = zip(sent(4), sent(2), sent(2))
    return pl.pallas_call(
        pack_kernel,
        grid=(TOKEN_STEPS,),
        in_specs=[smem()] * 3
        + [
            pl.BlockSpec((some, heads, width), lambda n: (n, 0, 0)),
            pl.BlockSpec((2, some, key_heads, width), lambda n: (0, n, 0, 0)),
        ],
        out_specs=list(specs) + [smem()],
        out_shape=list(shapes) + [jax.ShapeDtypeStruct((SCALARS,), jnp.int32)],
        scratch_shapes=[
            pltpu.VMEM((heads, some, width), queries.dtype),
            pltpu.VMEM((2, key_heads, some, width), queries.dtype),
        ],
        compiler_params=params(),
        cost_estimate=cost(0, 4 * (queries.size + states.size)),
    )(index, span_start, steered_heads, in_hbm(queries), in_hbm(states))


def raw_scores(query, key):
    return lax.dot_general(
        query, key, (((1,), (1,)), ((), ())), preferred_element_type=jnp.float32
    )


def weights(raw_score, bias=None, visible=None):
    score = jnp.tanh(raw_score * (SCORE_SCALE / SOFTCAP)) * (SOFTCAP * LOG2_E)
    pair = (2, score.shape[0] // 2, score.shape[1])
    if bias is not None:
        score = (score.reshape(pair) + bias).reshape(score.shape)
    weight = jnp.exp2(score)
    if visible is not None:
        weight = jnp.where(visible, weight.reshape(pair), 0.0).reshape(score.shape)
    return weight


def lane_sums(weight, lanes):
    sums = weight[:, :lanes]
    for first in range(lanes, weight.shape[1], lanes):
        sums = sums + weight[:, first : first + lanes]
    return sums


def tile(query, key, value, bias=None, visible=None):
    weight = weights(raw_scores(query, key), bias, visible)
    weighted = jnp.dot(
        weight.astype(jnp.bfloat16), value, preferred_element_type=jnp.float32
    )
    return weighted, lane_sums(weight, query.shape[1])


def attend_kernel(*refs, step, steerable, last):
    refs = list(refs)
    scalars = refs.pop(0)
    bias_ref = refs.pop(0) if steerable else None
    low_ref, high_ref, states_ref = refs.pop(0), refs.pop(0), refs.pop(0)
    span_ref = refs.pop(0) if steerable and last else None
    if step:
        old_weighted, old_sums = refs.pop(0), refs.pop(0)
    if last:
        out_ref = refs.pop(0)
    weighted_ref, sums_ref, query_ref = refs
    low = pl.program_id(0)
    blocks, _, rows, width = states_ref.shape
    high = blocks - 1 - low
    plane = scalars[PLANE]
    first_block = (plane - step) * blocks
    query_ref[0] = low_ref[0].reshape(2 * rows, width)
    query_ref[1] = high_ref[0].reshape(2 * rows, width)
    if step:
        weighted_ref[...] = old_weighted[...]
        sums_ref[...] = old_sums[...]
    else:
        weighted_ref[...] = jnp.zeros(weighted_ref.shape, jnp.float32)
        sums_ref[...] = jnp.zeros(sums_ref.shape, jnp.float32)
    flags = [scalars[STEERED_0 + n] for n in range(2)]
    flag_values = [flag.astype(jnp.float32) for flag in flags]

    def states(part, key_block, count):
        if count == 1:
            return states_ref[key_block, part]
        return states_ref[pl.ds(key_block, count), part].reshape(count * rows, width)

    def bias(key_block, count):
        if not steerable:
            return None
        parts = [bias_ref[pl.ds(first_block + key_block + n, 1), :] for n in range(count)]
        row = parts[0] if count == 1 else jnp.concatenate(parts, axis=1)
        return jnp.stack([row * value for value in flag_values])

    def add(tiles):
        ahead = raw_scores(query_ref[tiles[0][0]], states(0, *tiles[0][1:3]))
        for n, (which, key_block, count, visible) in enumerate(tiles):
            raw_score = ahead
            if n + 1 < len(tiles):
                ahead = raw_scores(query_ref[tiles[n + 1][0]], states(0, *tiles[n + 1][1:3]))
            weight = weights(raw_score, bias(key_block, count), visible)
            sums_ref[0, which] += lane_sums(weight, width)
            weighted_ref[0, which] += jnp.dot(
                weight.astype(jnp.bfloat16),
                states(1, key_block, count),
                preferred_element_type=jnp.float32,
            )

    def emphasized(key_block):
        index = (first_block + key_block) * rows + lax.broadcasted_iota(jnp.int32, (1, rows), 1)
        first = scalars[SPAN_FIRST]
        inside = (index >= first) & (index < first + SPAN)
        return jnp.stack([inside & (flag == 1) for flag in flags])

    def compute():
        row = lax.broadcasted_iota(jnp.int32, (rows, rows), 0)
        column = lax.broadcasted_iota(jnp.int32, (rows, rows), 1)
        if step == 1:
            add([(which, n, 2, None) for which in range(2) for n in range(0, blocks, 2)])
            return
        tiles = []
        for n in range(blocks - 1):
            if step == 0:
                is_low = n < low
                tiles.append((jnp.where(is_low, 0, 1), jnp.where(is_low, n, n - low), 1, None))
            else:
                is_high = n < low
                tiles.append(
                    (jnp.where(is_high, 1, 0), jnp.where(is_high, high + 1 + n, n + 1), 1, None)
                )
        visible = (row >= column if step == 0 else row < column)[None]
        for which, block in ((0, low), (1, high)):
            seen = visible | emphasized(block) if step and steerable else visible
            tiles.append((which, block, 1, seen))
        add(tiles)

    def add_steered(which, head, keys, values, visible):
        some = pl.ds(head * rows, rows)
        query = query_ref[which, some, :]
        ahead = raw_scores(query, keys(0))
        for n in range(len(visible)):
            raw_score = ahead
            if n + 1 < len(visible):
                ahead = raw_scores(query, keys(n + 1))
            weight = jnp.where(visible[n], weights(raw_score), 0.0)
            sums_ref[0, which, some, :] += lane_sums(weight, width)
            weighted_ref[0, which, some, :] += jnp.dot(
                weight.astype(jnp.bfloat16), values(n), preferred_element_type=jnp.float32
            )

    def in_span(index):
        first = scalars[SPAN_FIRST]
        return (index >= first) & (index < first + SPAN)

    def add_span():
        count = SPAN // rows + 1
        first = lax.div(jnp.maximum(scalars[SPAN_FIRST] - first_block * rows, 0), rows)
        first = jnp.minimum(first, blocks - count)
        for which, block in ((0, low), (1, high)):
            visible = []
            for n in range(count):
                index = (first_block + first + n) * rows
                index = index + lax.broadcasted_iota(jnp.int32, (1, rows), 1)
                visible.append(in_span(index) & (first + n < block))
            for head in range(2):
                pl.when((flags[head] == 1) & (first < block))(
                    functools.partial(
                        add_steered,
                        which,
                        head,
                        lambda n: states_ref[first + n, 0],
                        lambda n: states_ref[first + n, 1],
                        visible,
                    )
                )

    def add_far_span():
        length = blocks * rows
        start = (plane - step - 1) * length + jnp.minimum(scalars[SPAN_FIRST], length - SPAN)
        visible = [
            in_span(start + n * rows + lax.broadcasted_iota(jnp.int32, (1, rows), 1))
            for n in range(SPAN // rows)
        ]
        for which in range(2):
            for head in range(2):
                pl.when(flags[head] == 1)(
                    functools.partial(
                        add_steered,
                        which,
                        head,
                        lambda n: span_ref[0, n * rows : (n + 1) * rows, :],
                        lambda n: span_ref[1, n * rows : (n + 1) * rows, :],
                        visible,
                    )
                )

    if step:
        pl.when(plane >= step)(compute)
    else:
        compute()
    if last and steerable:
        span_end = scalars[SPAN_FIRST] + SPAN
        here = first_block * rows
        pl.when(
            (plane >= step) & (span_end > here) & (scalars[SPAN_FIRST] < here + blocks * rows)
        )(add_span)
        pl.when((plane > step) & (scalars[SPAN_FIRST] < here))(add_far_span)
    if last:
        write_result(out_ref, weighted_ref, sums_ref, low, high)


def write_result(out_ref, weighted_ref, sums_ref, low, high):
    for which, block in ((0, low), (1, high)):
        total = jnp.sum(sums_ref[0, which], axis=-1, keepdims=True)
        result = (weighted_ref[0, which] / total).astype(out_ref.dtype)
        out_ref[block] = result.reshape(out_ref.shape[1:])


def query_specs(both):
    blocks, _, rows, width = both.shape
    one = (1, 2, rows, width)
    return [
        pl.BlockSpec(one, lambda n: (n, 1, 0, 0)),
        pl.BlockSpec(one, lambda n: (blocks - 1 - n, 1, 0, 0)),
    ]


def held_spec(both):
    _, _, rows, width = both.shape
    return pl.BlockSpec((1, 2, 2 * rows, width), lambda n: (n, 0, 0, 0))


def attend(step, scalars, bias, both, states, carried=None, span_states=None, last=False):
    blocks, parts, rows, width = both.shape
    pair = 2
    assert blocks % 2 == 0 and parts == 2 + pair
    held = pltpu.HBM((blocks // 2, 2, pair * rows, width), jnp.float32)
    whole = pl.BlockSpec((blocks, 2, rows, width), lambda n: (0, 0, 0, 0))
    operands, in_specs = [scalars], [smem()]
    if bias is not None:
        operands.append(bias)
        in_specs.append(pl.BlockSpec(bias.shape, lambda n: (0, 0)))
    operands += [both, both, states]
    in_specs += query_specs(both) + [whole]
    if span_states is not None:
        operands.append(span_states)
        in_specs.append(pl.BlockSpec(span_states.shape, lambda n: (0, 0, 0)))
    if carried is not None:
        operands += [in_hbm(sums) for sums in carried]
        in_specs += [held_spec(both)] * 2
    scratch = [pltpu.VMEM((2, pair * rows, width), both.dtype)]
    if last:
        out_shape = jax.ShapeDtypeStruct((blocks, pair, rows, width), both.dtype)
        out_specs = pl.BlockSpec(out_shape.shape, lambda n: (0, 0, 0, 0))
        scratch = [pltpu.VMEM((1, 2, pair * rows, width), jnp.float32)] * 2 + scratch
    else:
        out_shape, out_specs = [held, held], [held_spec(both)] * 2
    return pl.pallas_call(
        functools.partial(attend_kernel, step=step, steerable=bias is not None, last=last),
        grid=(blocks // 2,),
        in_specs=in_specs,
        out_specs=out_specs,
        out_shape=out_shape,
        scratch_shapes=scratch,
        compiler_params=params(),
        cost_estimate=cost(
            pair * (blocks * rows) ** 2 / (1 if step == 1 else 2),
            4 * both.size + 8 * pair * blocks * rows * width,
        ),
    )(*operands)


def unpack_kernel(scalars, out_a, out_b, attention, heads_ref):
    for n in range(GROUP):
        for group_head in range(2):
            heads_ref[2 * scalars[n] + group_head] = out_a[n, group_head]
            heads_ref[2 * scalars[GROUP + n] + group_head] = out_b[n, group_head]
    attention[...] = jnp.transpose(heads_ref[...], (1, 0, 2))


def unpack(scalars, out_a, out_b):
    blocks, pair, rows, width = out_a.shape
    heads = 2 * blocks * pair
    return pl.pallas_call(
        unpack_kernel,
        in_specs=[smem(), vmem(), vmem()],
        out_specs=vmem(),
        out_shape=jax.ShapeDtypeStruct((rows, heads, width), out_a.dtype),
        scratch_shapes=[pltpu.VMEM((heads, rows, width), out_a.dtype)],
        compiler_params=params(),
        cost_estimate=cost(0, 8 * out_a.size),
    )(scalars, out_a, out_b)


def per_device(queries, key_value, damping, span_start, steered_heads):
    rows = queries.shape[0]
    device_count = lax.axis_size("seq")
    assert WINDOW == 2 * GROUP * rows and device_count == 4 * GROUP
    assert key_value.shape[2] == 2 * GROUP and queries.shape[1] == 4 * GROUP
    assert steered_heads.shape[0] <= GROUP
    groups = [
        list(range(first, first + GROUP)) for first in range(0, device_count, GROUP)
    ]

    def exchange(blocks):
        return lax.all_to_all(
            blocks, "seq", split_axis=0, concat_axis=0, axis_index_groups=groups, tiled=True
        )

    def onward(blocks, planes=1):
        shift = planes * GROUP
        pairs = [(n, n + shift) for n in range(device_count - shift)]
        return lax.ppermute(blocks, "seq", pairs)

    def after(value, earlier):
        return lax.optimization_barrier((value, earlier))[0]

    index = lax.axis_index("seq").astype(jnp.int32).reshape(1)
    both_a, states_b, queries_b, scalars = pack(
        index, span_start, steered_heads, queries, key_value
    )
    both_b = jnp.concatenate([states_b, queries_b], axis=1)
    position = jnp.arange(damping.shape[0], dtype=jnp.int32)
    emphasized = (position >= span_start[0]) & (position < span_start[0] + SPAN)
    bias = jnp.where(emphasized, 0.0, jnp.log2(damping.astype(jnp.float32)))
    bias = bias.reshape(-1, rows)

    raw_b = onward(states_b)
    both_a = exchange(both_a)
    states_a = both_a[:, :2]
    back_a = onward(after(states_a, raw_b))
    length = GROUP * rows
    span_states = lax.dynamic_slice_in_dim(
        after(both_a, back_a)[:, :2].transpose(1, 0, 2, 3).reshape(2, length, -1),
        jnp.minimum(span_start[0], length - SPAN),
        SPAN,
        1,
    )
    span_states = onward(span_states, 3)
    both_b = exchange(after(both_b, states_a))
    held_a = attend(0, scalars, bias, after(both_a, raw_b), both_a)
    far_a = onward(back_a)
    held_a = attend(1, scalars, bias, both_a, back_a, held_a)
    back_b = exchange(after(raw_b, (both_b, held_a)))
    held_b = attend(0, scalars, None, after(both_b, held_a), both_b)
    far_b = onward(back_b)
    out_a = attend(
        2, scalars, bias, both_a, far_a, after(held_a, held_b), span_states, last=True
    )
    held_b = attend(1, scalars, None, both_b, back_b, after(held_b, out_a))
    out_a = exchange(out_a)
    out_b = attend(2, scalars, None, both_b, far_b, held_b, last=True)
    out_b = exchange(out_b)
    return unpack(scalars, out_a, out_b)


def solution(mesh):
    in_specs = (
        P(("prompt", "seq"), None, None),
        P(None, ("prompt", "seq"), None, None),
        P("prompt"),
        P("prompt"),
        P(),
    )
    out_specs = P(("prompt", "seq"), None, None)
    return jax.shard_map(
        per_device, mesh=mesh, in_specs=in_specs, out_specs=out_specs, check_vma=False
    )
```

```python
import functools
import math

import jax
import jax.numpy as jnp
from jax import lax
from jax.experimental import pallas as pl
from jax.experimental.pallas import tpu as pltpu
from jax.sharding import PartitionSpec as P

WINDOW = 4096
SPAN = 512

SCORE_SCALE = 144.0 ** (-0.5)
SOFTCAP = 50.0
LOG2_E = math.log2(math.e)

GROUP = 8
TOKEN_STEPS = 4
PAIR_FLOPS = 256
VMEM_BYTES = 48 * 1024 * 1024

FIRST_SCALAR = 32
PLANE, SPAN_FIRST, STEERED_0, STEERED_1 = range(FIRST_SCALAR, FIRST_SCALAR + 4)
SCALARS = FIRST_SCALAR + 4


def smem():
    return pl.BlockSpec(memory_space=pltpu.SMEM)


def vmem():
    return pl.BlockSpec(memory_space=pltpu.VMEM)


def in_hbm(operand):
    return pltpu.with_memory_space_constraint(operand, pltpu.HBM)


def params():
    return pltpu.CompilerParams(vmem_limit_bytes=VMEM_BYTES)


def cost(pairs, moved):
    return pl.CostEstimate(
        flops=int(pairs * PAIR_FLOPS), bytes_accessed=int(moved), transcendentals=int(2 * pairs)
    )


def pack_kernel(
    index_ref, span_ref, steered_ref, queries_ref, states_ref,
    both_a, states_b, queries_b, scalars, query_heads, state_heads,
):
    key_heads = states_ref.shape[2]
    steered_count = steered_ref.shape[0]

    @pl.when(pl.program_id(0) == 0)
    def _():
        steered_keys = [lax.div(steered_ref[n], 2) for n in range(steered_count)]
        flags = []
        for head in range(key_heads):
            hit = steered_keys[0] == head
            for n in range(1, steered_count):
                hit = hit | (steered_keys[n] == head)
            flags.append(hit.astype(jnp.int32))
        total = sum(flags[1:], flags[0])
        before = jnp.int32(0)
        for head in range(key_heads):
            rank = jnp.where(flags[head] == 1, before, total + head - before)
            scalars[rank] = jnp.int32(head)
            before = before + flags[head]
        place = lax.rem(index_ref[0], GROUP)
        scalars[PLANE] = lax.div(index_ref[0], GROUP)
        scalars[SPAN_FIRST] = span_ref[0]
        own_head = scalars[place]
        for group_head in range(2):
            hit = steered_ref[0] == 2 * own_head + group_head
            for n in range(1, steered_count):
                hit = hit | (steered_ref[n] == 2 * own_head + group_head)
            scalars[STEERED_0 + group_head] = hit.astype(jnp.int32)

    for part in range(2):
        state_heads[part] = jnp.transpose(states_ref[part], (1, 0, 2))
        for n in range(GROUP):
            both_a[n, part] = state_heads[part, scalars[n]]
            states_b[n, part] = state_heads[part, scalars[GROUP + n]]
    query_heads[...] = jnp.transpose(queries_ref[...], (1, 0, 2))
    for n in range(GROUP):
        for group_head in range(2):
            both_a[n, 2 + group_head] = query_heads[2 * scalars[n] + group_head]
            queries_b[n, group_head] = query_heads[2 * scalars[GROUP + n] + group_head]


def pack(index, span_start, steered_heads, queries, states):
    rows, heads, width = queries.shape
    key_heads = states.shape[2]
    some = rows // TOKEN_STEPS

    def sent(parts):
        shape = pltpu.HBM((GROUP, parts, rows, width), queries.dtype)
        return shape, pl.BlockSpec((GROUP, parts, some, width), lambda n: (0, 0, n, 0))

    shapes, specs = zip(sent(4), sent(2), sent(2))
    return pl.pallas_call(
        pack_kernel,
        grid=(TOKEN_STEPS,),
        in_specs=[smem()] * 3
        + [
            pl.BlockSpec((some, heads, width), lambda n: (n, 0, 0)),
            pl.BlockSpec((2, some, key_heads, width), lambda n: (0, n, 0, 0)),
        ],
        out_specs=list(specs) + [smem()],
        out_shape=list(shapes) + [jax.ShapeDtypeStruct((SCALARS,), jnp.int32)],
        scratch_shapes=[
            pltpu.VMEM((heads, some, width), queries.dtype),
            pltpu.VMEM((2, key_heads, some, width), queries.dtype),
        ],
        compiler_params=params(),
        cost_estimate=cost(0, 4 * (queries.size + states.size)),
    )(index, span_start, steered_heads, in_hbm(queries), in_hbm(states))


def raw_scores(query, key):
    return lax.dot_general(
        query, key, (((1,), (1,)), ((), ())), preferred_element_type=jnp.float32
    )


def weights(raw_score, bias=None, visible=None):
    score = jnp.tanh(raw_score * (SCORE_SCALE / SOFTCAP)) * (SOFTCAP * LOG2_E)
    heads = max([1] + [each.shape[0] for each in (bias, visible) if each is not None])
    if visible is not None:
        heads = score.shape[0] // visible.shape[1]
    split = (heads, score.shape[0] // heads, score.shape[1])
    if bias is not None:
        score = (score.reshape(split) + bias).reshape(score.shape)
    weight = jnp.exp2(score)
    if visible is not None:
        weight = jnp.where(visible, weight.reshape(split), 0.0).reshape(score.shape)
    return weight


def lane_sums(weight, lanes):
    sums = weight[:, :lanes]
    for first in range(lanes, weight.shape[1], lanes):
        sums = sums + weight[:, first : first + lanes]
    return sums


def attend_kernel(*refs, step, steerable, last):
    refs = list(refs)
    scalars = refs.pop(0)
    bias_ref = refs.pop(0) if steerable else None
    low_ref, high_ref, states_ref = refs.pop(0), refs.pop(0), refs.pop(0)
    span_ref = refs.pop(0) if steerable and last else None
    if step:
        old_weighted, old_sums = refs.pop(0), refs.pop(0)
    if last:
        out_ref = refs.pop(0)
    weighted_ref, sums_ref, query_ref = refs[:3]
    turned_ref = refs[3] if steerable else None
    around_ref, gathered_ref = refs[4:] if steerable and last else (None, None)
    heads_at_once = 2 if steerable else 1
    low = pl.program_id(0)
    blocks, _, rows, width = states_ref.shape
    high = blocks - 1 - low
    plane = scalars[PLANE]
    first_block = (plane - step) * blocks
    query_ref[0] = low_ref[0].reshape(2 * rows, width)
    query_ref[1] = high_ref[0].reshape(2 * rows, width)
    if step:
        weighted_ref[...] = old_weighted[...]
        sums_ref[...] = old_sums[...]
    else:
        weighted_ref[...] = jnp.zeros(weighted_ref.shape, jnp.float32)
        sums_ref[...] = jnp.zeros(sums_ref.shape, jnp.float32)
    flags = [scalars[STEERED_0 + n] for n in range(2)]
    flag_values = [flag.astype(jnp.float32) for flag in flags]

    def states(part, key_block, count):
        if count == 1:
            return states_ref[key_block, part]
        return states_ref[pl.ds(key_block, count), part].reshape(count * rows, width)

    def bias(key_block, count):
        if not steerable:
            return None
        parts = [bias_ref[pl.ds(first_block + key_block + n, 1), :] for n in range(count)]
        row = parts[0] if count == 1 else jnp.concatenate(parts, axis=1)
        return jnp.stack([row * value for value in flag_values])

    def add(tiles):
        units = []
        for which, key_block, count, visible in tiles:
            for head in range(0, 2, heads_at_once):
                units.append((which, head, key_block, count, visible))

        def of_span(key_block):
            return isinstance(key_block, int) and key_block < 0

        def score(unit):
            which, head, key_block, count, _ = unit
            query = query_ref[which, head * rows : (head + heads_at_once) * rows, :]
            if of_span(key_block):
                return raw_scores(query, gathered_ref[0, ~key_block])
            return raw_scores(query, states(0, key_block, count))

        ahead = score(units[0])
        for n, unit in enumerate(units):
            raw_score = ahead
            if n + 1 < len(units):
                ahead = score(units[n + 1])
            which, head, key_block, count, visible = unit
            some = slice(head * rows, (head + heads_at_once) * rows)
            span = of_span(key_block)
            weight = weights(raw_score, None if span else bias(key_block, count), visible)
            sums_ref[0, which, some, :] += lane_sums(weight, width)
            weight = weight.astype(jnp.bfloat16)
            if span:
                weighted = jnp.dot(
                    weight, gathered_ref[1, ~key_block], preferred_element_type=jnp.float32
                )
            elif steerable:
                weighted = raw_scores(weight, turned(key_block, count))
            else:
                weighted = jnp.dot(
                    weight, states(1, key_block, count), preferred_element_type=jnp.float32
                )
            weighted_ref[0, which, some, :] += weighted

    def turned(key_block, count):
        if count == 1:
            return turned_ref[key_block]
        parts = [turned_ref[key_block + n] for n in range(count)]
        return jnp.concatenate(parts, axis=1)

    if steerable:

        @pl.when(low == 0)
        def _():
            for n in range(blocks):
                turned_ref[n] = states_ref[n, 1].T

    def gather_span():
        start = scalars[SPAN_FIRST] - first_block * rows
        pad = SPAN // rows
        for part in range(2):
            before = span_ref[part].astype(jnp.float32)

            @pl.when(start < 0)
            def _():
                around_ref[:SPAN, :] = before
                for n in range(2):
                    around_ref[SPAN + n * rows : SPAN + (n + 1) * rows, :] = states_ref[
                        n, part
                    ].astype(jnp.float32)

            block = jnp.clip(lax.div(jnp.maximum(start, 0), rows), 0, blocks - pad - 1)

            @pl.when(start >= 0)
            def _():
                for n in range(pad + 1):
                    around_ref[n * rows : (n + 1) * rows, :] = states_ref[
                        block + n, part
                    ].astype(jnp.float32)
                around_ref[(pad + 1) * rows :, :] = jnp.zeros((SPAN, width), jnp.float32)

            offset = jnp.where(start < 0, jnp.maximum(start + SPAN, 0), start - block * rows)
            for n in range(pad):
                gathered_ref[part, n] = around_ref[pl.ds(offset + n * rows, rows), :].astype(
                    jnp.bfloat16
                )

    def span_tiles():
        row = lax.broadcasted_iota(jnp.int32, (rows, rows), 0)
        column = lax.broadcasted_iota(jnp.int32, (rows, rows), 1)
        tiles = []
        for which, block in ((0, low), (1, high)):
            for n in range(SPAN // rows):
                nearest = scalars[SPAN_FIRST] + n * rows + WINDOW - (plane * blocks + block) * rows
                seen = [
                    row - column >= jnp.where(flag == 1, nearest, 2 * rows) for flag in flags
                ]
                tiles.append((which, ~n, 1, jnp.stack(seen)))
        return tiles

    def compute():
        row = lax.broadcasted_iota(jnp.int32, (rows, rows), 0)
        column = lax.broadcasted_iota(jnp.int32, (rows, rows), 1)
        if step == 1:
            add([(which, n, 2, None) for which in range(2) for n in range(0, blocks, 2)])
            return
        tiles = []
        for n in range(blocks - 1):
            if step == 0:
                is_low = n < low
                tiles.append((jnp.where(is_low, 0, 1), jnp.where(is_low, n, n - low), 1, None))
            else:
                is_high = n < low
                tiles.append(
                    (jnp.where(is_high, 1, 0), jnp.where(is_high, high + 1 + n, n + 1), 1, None)
                )
        visible = (row >= column if step == 0 else row < column)[None]
        for which, block in ((0, low), (1, high)):
            tiles.append((which, block, 1, visible))
        if not (steerable and last):
            add(tiles)
            return
        wanted = flags[0] + flags[1] > 0
        wanted = wanted & (scalars[SPAN_FIRST] < (first_block + blocks) * rows)
        pl.when(wanted & (low == 0))(gather_span)
        pl.when(wanted)(lambda: add(tiles + span_tiles()))
        pl.when(jnp.logical_not(wanted))(lambda: add(tiles))

    if step:
        pl.when(plane >= step)(compute)
    else:
        compute()
    if last:
        write_result(out_ref, weighted_ref, sums_ref, low, high)


def write_result(out_ref, weighted_ref, sums_ref, low, high):
    for which, block in ((0, low), (1, high)):
        total = jnp.sum(sums_ref[0, which], axis=-1, keepdims=True)
        result = (weighted_ref[0, which] / total).astype(out_ref.dtype)
        out_ref[block] = result.reshape(out_ref.shape[1:])


def query_specs(both):
    blocks, _, rows, width = both.shape
    one = (1, 2, rows, width)
    return [
        pl.BlockSpec(one, lambda n: (n, 1, 0, 0)),
        pl.BlockSpec(one, lambda n: (blocks - 1 - n, 1, 0, 0)),
    ]


def held_spec(both):
    _, _, rows, width = both.shape
    return pl.BlockSpec((1, 2, 2 * rows, width), lambda n: (n, 0, 0, 0))


def attend(step, scalars, bias, both, states, carried=None, span_states=None, last=False):
    blocks, parts, rows, width = both.shape
    pair = 2
    assert blocks % 2 == 0 and parts == 2 + pair
    held = pltpu.HBM((blocks // 2, 2, pair * rows, width), jnp.float32)
    whole = pl.BlockSpec((blocks, 2, rows, width), lambda n: (0, 0, 0, 0))
    operands, in_specs = [scalars], [smem()]
    if bias is not None:
        operands.append(bias)
        in_specs.append(pl.BlockSpec(bias.shape, lambda n: (0, 0)))
    operands += [both, both, states]
    in_specs += query_specs(both) + [whole]
    if span_states is not None:
        operands.append(span_states)
        in_specs.append(pl.BlockSpec(span_states.shape, lambda n: (0, 0, 0)))
    if carried is not None:
        operands += [in_hbm(sums) for sums in carried]
        in_specs += [held_spec(both)] * 2
    scratch = [pltpu.VMEM((2, pair * rows, width), both.dtype)]
    if bias is not None:
        scratch.append(pltpu.VMEM((blocks, width, rows), both.dtype))
    if span_states is not None:
        scratch.append(pltpu.VMEM((2 * SPAN + rows, width), jnp.float32))
        scratch.append(pltpu.VMEM((2, SPAN // rows, rows, width), both.dtype))
    if last:
        out_shape = jax.ShapeDtypeStruct((blocks, pair, rows, width), both.dtype)
        out_specs = pl.BlockSpec(out_shape.shape, lambda n: (0, 0, 0, 0))
        scratch = [pltpu.VMEM((1, 2, pair * rows, width), jnp.float32)] * 2 + scratch
    else:
        out_shape, out_specs = [held, held], [held_spec(both)] * 2
    return pl.pallas_call(
        functools.partial(attend_kernel, step=step, steerable=bias is not None, last=last),
        grid=(blocks // 2,),
        in_specs=in_specs,
        out_specs=out_specs,
        out_shape=out_shape,
        scratch_shapes=scratch,
        compiler_params=params(),
        cost_estimate=cost(
            pair * (blocks * rows) ** 2 / (1 if step == 1 else 2),
            4 * both.size + 8 * pair * blocks * rows * width,
        ),
    )(*operands)


def unpack_kernel(scalars, out_a, out_b, attention, heads_ref):
    for n in range(GROUP):
        for group_head in range(2):
            heads_ref[2 * scalars[n] + group_head] = out_a[n, group_head]
            heads_ref[2 * scalars[GROUP + n] + group_head] = out_b[n, group_head]
    attention[...] = jnp.transpose(heads_ref[...], (1, 0, 2))


def unpack(scalars, out_a, out_b):
    blocks, pair, rows, width = out_a.shape
    heads = 2 * blocks * pair
    return pl.pallas_call(
        unpack_kernel,
        in_specs=[smem(), vmem(), vmem()],
        out_specs=vmem(),
        out_shape=jax.ShapeDtypeStruct((rows, heads, width), out_a.dtype),
        scratch_shapes=[pltpu.VMEM((heads, rows, width), out_a.dtype)],
        compiler_params=params(),
        cost_estimate=cost(0, 8 * out_a.size),
    )(scalars, out_a, out_b)


def per_device(queries, key_value, damping, span_start, steered_heads):
    rows = queries.shape[0]
    device_count = lax.axis_size("seq")
    assert WINDOW == 2 * GROUP * rows and device_count == 4 * GROUP
    assert key_value.shape[2] == 2 * GROUP and queries.shape[1] == 4 * GROUP
    assert steered_heads.shape[0] <= GROUP
    groups = [
        list(range(first, first + GROUP)) for first in range(0, device_count, GROUP)
    ]

    def exchange(blocks):
        return lax.all_to_all(
            blocks, "seq", split_axis=0, concat_axis=0, axis_index_groups=groups, tiled=True
        )

    def onward(blocks, planes=1):
        shift = planes * GROUP
        pairs = [(n, n + shift) for n in range(device_count - shift)]
        return lax.ppermute(blocks, "seq", pairs)

    def after(value, earlier):
        return lax.optimization_barrier((value, earlier))[0]

    index = lax.axis_index("seq").astype(jnp.int32).reshape(1)
    both_a, states_b, queries_b, scalars = pack(
        index, span_start, steered_heads, queries, key_value
    )
    both_b = jnp.concatenate([states_b, queries_b], axis=1)
    position = jnp.arange(damping.shape[0], dtype=jnp.int32)
    emphasized = (position >= span_start[0]) & (position < span_start[0] + SPAN)
    bias = jnp.where(emphasized, 0.0, jnp.log2(damping.astype(jnp.float32)))
    bias = bias.reshape(-1, rows)

    raw_b = onward(states_b)
    both_a = exchange(both_a)
    states_a = both_a[:, :2]
    back_a = onward(after(states_a, raw_b))
    length = GROUP * rows
    span_states = lax.dynamic_slice_in_dim(
        after(both_a, back_a)[:, :2].transpose(1, 0, 2, 3).reshape(2, length, -1),
        jnp.minimum(span_start[0], length - SPAN),
        SPAN,
        1,
    )
    span_states = onward(span_states, 3)
    both_b = exchange(after(both_b, states_a))
    held_a = attend(0, scalars, bias, after(both_a, raw_b), both_a)
    back_b = exchange(after(raw_b, (both_b, held_a)))
    far_a = onward(back_a)
    held_b = attend(0, scalars, None, after(both_b, (held_a, back_a)), both_b)
    far_b = onward(back_b)
    held_a = attend(1, scalars, bias, after(both_a, (held_b, back_b)), back_a, held_a)
    out_a = attend(2, scalars, bias, both_a, far_a, held_a, span_states, last=True)
    held_b = attend(1, scalars, None, both_b, back_b, after(held_b, out_a))
    out_a = exchange(out_a)
    out_b = attend(2, scalars, None, both_b, far_b, held_b, last=True)
    out_b = exchange(out_b)
    return unpack(scalars, out_a, out_b)


def solution(mesh):
    in_specs = (
        P(("prompt", "seq"), None, None),
        P(None, ("prompt", "seq"), None, None),
        P("prompt"),
        P("prompt"),
        P(),
    )
    out_specs = P(("prompt", "seq"), None, None)
    return jax.shard_map(
        per_device, mesh=mesh, in_specs=in_specs, out_specs=out_specs, check_vma=False
    )
```

```python
import functools
import math

import jax
import jax.numpy as jnp
from jax import lax
from jax.experimental import pallas as pl
from jax.experimental.pallas import tpu as pltpu
from jax.sharding import PartitionSpec as P

WINDOW = 4096
SPAN = 512

SCORE_SCALE = 144.0 ** (-0.5)
SOFTCAP = 50.0
LOG2_E = math.log2(math.e)

TANH_LIMIT = 0.6
TANH_TERMS = (
    0.9999999268688397,
    -0.3333230997334083,
    0.13310173643325,
    -0.05210147946765075,
    0.015475426590504583,
)
TANH_SERIES = [
    term * SOFTCAP * LOG2_E * (SCORE_SCALE / SOFTCAP) ** (2 * n + 1)
    for n, term in enumerate(TANH_TERMS)
]

GROUP = 8
TOKEN_STEPS = 4
PAIR_FLOPS = 256
VMEM_BYTES = 48 * 1024 * 1024

FIRST_SCALAR = 32
PLANE, SPAN_FIRST, STEERED_0, STEERED_1 = range(FIRST_SCALAR, FIRST_SCALAR + 4)
SCALARS = FIRST_SCALAR + 4


def smem():
    return pl.BlockSpec(memory_space=pltpu.SMEM)


def vmem():
    return pl.BlockSpec(memory_space=pltpu.VMEM)


def in_hbm(operand):
    return pltpu.with_memory_space_constraint(operand, pltpu.HBM)


def params():
    return pltpu.CompilerParams(vmem_limit_bytes=VMEM_BYTES)


def cost(pairs, moved):
    return pl.CostEstimate(
        flops=int(pairs * PAIR_FLOPS), bytes_accessed=int(moved), transcendentals=int(2 * pairs)
    )


def pack_kernel(
    index_ref, span_ref, steered_ref, queries_ref, states_ref,
    both_a, states_b, queries_b, scalars, query_heads, state_heads,
):
    key_heads = states_ref.shape[2]
    steered_count = steered_ref.shape[0]

    @pl.when(pl.program_id(0) == 0)
    def _():
        steered_keys = [lax.div(steered_ref[n], 2) for n in range(steered_count)]
        flags = []
        for head in range(key_heads):
            hit = steered_keys[0] == head
            for n in range(1, steered_count):
                hit = hit | (steered_keys[n] == head)
            flags.append(hit.astype(jnp.int32))
        total = sum(flags[1:], flags[0])
        before = jnp.int32(0)
        for head in range(key_heads):
            rank = jnp.where(flags[head] == 1, before, total + head - before)
            scalars[rank] = jnp.int32(head)
            before = before + flags[head]
        place = lax.rem(index_ref[0], GROUP)
        scalars[PLANE] = lax.div(index_ref[0], GROUP)
        scalars[SPAN_FIRST] = span_ref[0]
        own_head = scalars[place]
        for group_head in range(2):
            hit = steered_ref[0] == 2 * own_head + group_head
            for n in range(1, steered_count):
                hit = hit | (steered_ref[n] == 2 * own_head + group_head)
            scalars[STEERED_0 + group_head] = hit.astype(jnp.int32)

    for part in range(2):
        state_heads[part] = jnp.transpose(states_ref[part], (1, 0, 2))
        for n in range(GROUP):
            both_a[n, part] = state_heads[part, scalars[n]]
            states_b[n, part] = state_heads[part, scalars[GROUP + n]]
    query_heads[...] = jnp.transpose(queries_ref[...], (1, 0, 2))
    for n in range(GROUP):
        for group_head in range(2):
            both_a[n, 2 + group_head] = query_heads[2 * scalars[n] + group_head]
            queries_b[n, group_head] = query_heads[2 * scalars[GROUP + n] + group_head]


def pack(index, span_start, steered_heads, queries, states):
    rows, heads, width = queries.shape
    key_heads = states.shape[2]
    some = rows // TOKEN_STEPS

    def sent(parts):
        shape = pltpu.HBM((GROUP, parts, rows, width), queries.dtype)
        return shape, pl.BlockSpec((GROUP, parts, some, width), lambda n: (0, 0, n, 0))

    shapes, specs = zip(sent(4), sent(2), sent(2))
    return pl.pallas_call(
        pack_kernel,
        grid=(TOKEN_STEPS,),
        in_specs=[smem()] * 3
        + [
            pl.BlockSpec((some, heads, width), lambda n: (n, 0, 0)),
            pl.BlockSpec((2, some, key_heads, width), lambda n: (0, n, 0, 0)),
        ],
        out_specs=list(specs) + [smem()],
        out_shape=list(shapes) + [jax.ShapeDtypeStruct((SCALARS,), jnp.int32)],
        scratch_shapes=[
            pltpu.VMEM((heads, some, width), queries.dtype),
            pltpu.VMEM((2, key_heads, some, width), queries.dtype),
        ],
        compiler_params=params(),
        cost_estimate=cost(0, 4 * (queries.size + states.size)),
    )(index, span_start, steered_heads, in_hbm(queries), in_hbm(states))


def raw_scores(query, key):
    return lax.dot_general(
        query, key, (((1,), (1,)), ((), ())), preferred_element_type=jnp.float32
    )


def weights(raw_score, bias=None, visible=None, square=None):
    if square is None:
        score = jnp.tanh(raw_score * (SCORE_SCALE / SOFTCAP)) * (SOFTCAP * LOG2_E)
    else:
        ratio = TANH_SERIES[-1]
        for term in TANH_SERIES[-2::-1]:
            ratio = ratio * square + term
        score = raw_score * ratio
    heads = max([1] + [each.shape[0] for each in (bias, visible) if each is not None])
    if visible is not None:
        heads = score.shape[0] // visible.shape[1]
    split = (heads, score.shape[0] // heads, score.shape[1])
    if bias is not None:
        score = (score.reshape(split) + bias).reshape(score.shape)
    weight = jnp.exp2(score)
    if visible is not None:
        weight = jnp.where(visible, weight.reshape(split), 0.0).reshape(score.shape)
    return weight


def lane_largest(square, lanes):
    rows, columns = square.shape
    largest = jnp.max(square.reshape(rows // 8, 8, columns), axis=0)
    result = largest[:, :lanes]
    for first in range(lanes, columns, lanes):
        result = jnp.maximum(result, largest[:, first : first + lanes])
    return result


def lane_sums(weight, lanes):
    sums = weight[:, :lanes]
    for first in range(lanes, weight.shape[1], lanes):
        sums = sums + weight[:, first : first + lanes]
    return sums


def attend_kernel(*refs, step, steerable, last, series):
    refs = list(refs)
    scalars = refs.pop(0)
    bias_ref = refs.pop(0) if steerable else None
    low_ref, high_ref, states_ref = refs.pop(0), refs.pop(0), refs.pop(0)
    span_ref = refs.pop(0) if steerable and last else None
    if step:
        old_weighted, old_sums = refs.pop(0), refs.pop(0)
    if last:
        out_ref = refs.pop(0)
    weighted_ref, sums_ref, query_ref = refs[:3]
    around_ref, gathered_ref = refs[3:] if steerable and last else (None, None)
    limit_ref = refs[3] if series else None
    heads_at_once = 2 if steerable or step == 1 else 1
    low = pl.program_id(0)
    blocks, _, rows, width = states_ref.shape
    high = blocks - 1 - low
    plane = scalars[PLANE]
    first_block = (plane - step) * blocks
    query_ref[0] = low_ref[0].reshape(2 * rows, width)
    query_ref[1] = high_ref[0].reshape(2 * rows, width)
    def start():
        if step:
            weighted_ref[...] = old_weighted[...]
            sums_ref[...] = old_sums[...]
        else:
            weighted_ref[...] = jnp.zeros(weighted_ref.shape, jnp.float32)
            sums_ref[...] = jnp.zeros(sums_ref.shape, jnp.float32)

    start()
    flags = [scalars[STEERED_0 + n] for n in range(2)]
    flag_values = [flag.astype(jnp.float32) for flag in flags]

    def states(part, key_block, count):
        if count == 1:
            return states_ref[key_block, part]
        return states_ref[pl.ds(key_block, count), part].reshape(count * rows, width)

    def bias(key_block, count):
        if not steerable:
            return None
        parts = [bias_ref[pl.ds(first_block + key_block + n, 1), :] for n in range(count)]
        row = parts[0] if count == 1 else jnp.concatenate(parts, axis=1)
        return jnp.stack([row * value for value in flag_values])

    def add(tiles, series=False):
        units = []
        for which, key_block, count, visible in tiles:
            for head in range(0, 2, heads_at_once):
                units.append((which, head, key_block, count, visible))

        def of_span(key_block):
            return isinstance(key_block, int) and key_block < 0

        def score(unit):
            which, head, key_block, count, _ = unit
            query = query_ref[which, head * rows : (head + heads_at_once) * rows, :]
            if of_span(key_block):
                return raw_scores(query, gathered_ref[0, ~key_block])
            return raw_scores(query, states(0, key_block, count))

        ahead = score(units[0])
        for n, unit in enumerate(units):
            raw_score = ahead
            if n + 1 < len(units):
                ahead = score(units[n + 1])
            which, head, key_block, count, visible = unit
            some = slice(head * rows, (head + heads_at_once) * rows)
            span = of_span(key_block)
            square = raw_score * raw_score if series else None
            if series:
                limit_ref[...] = jnp.maximum(limit_ref[...], lane_largest(square, width))
            weight = weights(raw_score, None if span else bias(key_block, count), visible, square)
            sums_ref[0, which, some, :] += lane_sums(weight, width)
            weight = weight.astype(jnp.bfloat16)
            if span:
                weighted = jnp.dot(
                    weight, gathered_ref[1, ~key_block], preferred_element_type=jnp.float32
                )
            else:
                weighted = jnp.dot(
                    weight, states(1, key_block, count), preferred_element_type=jnp.float32
                )
            weighted_ref[0, which, some, :] += weighted

    def gather_span():
        start = scalars[SPAN_FIRST] - first_block * rows
        pad = SPAN // rows
        for part in range(2):
            before = span_ref[part].astype(jnp.float32)

            @pl.when(start < 0)
            def _():
                around_ref[:SPAN, :] = before
                for n in range(2):
                    around_ref[SPAN + n * rows : SPAN + (n + 1) * rows, :] = states_ref[
                        n, part
                    ].astype(jnp.float32)

            block = jnp.clip(lax.div(jnp.maximum(start, 0), rows), 0, blocks - pad - 1)

            @pl.when(start >= 0)
            def _():
                for n in range(pad + 1):
                    around_ref[n * rows : (n + 1) * rows, :] = states_ref[
                        block + n, part
                    ].astype(jnp.float32)
                around_ref[(pad + 1) * rows :, :] = jnp.zeros((SPAN, width), jnp.float32)

            offset = jnp.where(start < 0, jnp.maximum(start + SPAN, 0), start - block * rows)
            for n in range(pad):
                gathered_ref[part, n] = around_ref[pl.ds(offset + n * rows, rows), :].astype(
                    jnp.bfloat16
                )

    def span_tiles():
        row = lax.broadcasted_iota(jnp.int32, (rows, rows), 0)
        column = lax.broadcasted_iota(jnp.int32, (rows, rows), 1)
        tiles = []
        for which, block in ((0, low), (1, high)):
            for n in range(SPAN // rows):
                nearest = scalars[SPAN_FIRST] + n * rows + WINDOW - (plane * blocks + block) * rows
                seen = [
                    row - column >= jnp.where(flag == 1, nearest, 2 * rows) for flag in flags
                ]
                tiles.append((which, ~n, 1, jnp.stack(seen)))
        return tiles

    def compute():
        row = lax.broadcasted_iota(jnp.int32, (rows, rows), 0)
        column = lax.broadcasted_iota(jnp.int32, (rows, rows), 1)
        if step == 1:
            tiles = [(which, n, 2, None) for which in range(2) for n in range(0, blocks, 2)]
            if not series:
                add(tiles)
                return
            limit_ref[...] = jnp.zeros(limit_ref.shape, jnp.float32)
            add(tiles, series=True)
            largest = (TANH_LIMIT * SOFTCAP / SCORE_SCALE) ** 2

            @pl.when(jnp.max(limit_ref[...]) > largest)
            def _():
                start()
                add(tiles)

            return
        tiles = []
        for n in range(blocks - 1):
            if step == 0:
                is_low = n < low
                tiles.append((jnp.where(is_low, 0, 1), jnp.where(is_low, n, n - low), 1, None))
            else:
                is_high = n < low
                tiles.append(
                    (jnp.where(is_high, 1, 0), jnp.where(is_high, high + 1 + n, n + 1), 1, None)
                )
        visible = (row >= column if step == 0 else row < column)[None]
        for which, block in ((0, low), (1, high)):
            tiles.append((which, block, 1, visible))
        if not (steerable and last):
            add(tiles)
            return
        wanted = flags[0] + flags[1] > 0
        wanted = wanted & (scalars[SPAN_FIRST] < (first_block + blocks) * rows)
        pl.when(wanted & (low == 0))(gather_span)
        pl.when(wanted)(lambda: add(tiles + span_tiles()))
        pl.when(jnp.logical_not(wanted))(lambda: add(tiles))

    if step:
        pl.when(plane >= step)(compute)
    else:
        compute()
    if last:
        write_result(out_ref, weighted_ref, sums_ref, low, high)


def write_result(out_ref, weighted_ref, sums_ref, low, high):
    for which, block in ((0, low), (1, high)):
        total = jnp.sum(sums_ref[0, which], axis=-1, keepdims=True)
        result = (weighted_ref[0, which] / total).astype(out_ref.dtype)
        out_ref[block] = result.reshape(out_ref.shape[1:])


def query_specs(both):
    blocks, _, rows, width = both.shape
    one = (1, 2, rows, width)
    return [
        pl.BlockSpec(one, lambda n: (n, 1, 0, 0)),
        pl.BlockSpec(one, lambda n: (blocks - 1 - n, 1, 0, 0)),
    ]


def held_spec(both):
    _, _, rows, width = both.shape
    return pl.BlockSpec((1, 2, 2 * rows, width), lambda n: (n, 0, 0, 0))


def attend(step, scalars, bias, both, states, carried=None, span_states=None, last=False):
    blocks, parts, rows, width = both.shape
    pair = 2
    assert blocks % 2 == 0 and parts == 2 + pair
    held = pltpu.HBM((blocks // 2, 2, pair * rows, width), jnp.float32)
    whole = pl.BlockSpec((blocks, 2, rows, width), lambda n: (0, 0, 0, 0))
    operands, in_specs = [scalars], [smem()]
    if bias is not None:
        operands.append(bias)
        in_specs.append(pl.BlockSpec(bias.shape, lambda n: (0, 0)))
    operands += [both, both, states]
    in_specs += query_specs(both) + [whole]
    if span_states is not None:
        operands.append(span_states)
        in_specs.append(pl.BlockSpec(span_states.shape, lambda n: (0, 0, 0)))
    if carried is not None:
        operands += [in_hbm(sums) for sums in carried]
        in_specs += [held_spec(both)] * 2
    scratch = [pltpu.VMEM((2, pair * rows, width), both.dtype)]
    series = bias is None and step == 1
    if series:
        scratch.append(pltpu.VMEM((8, width), jnp.float32))
    if span_states is not None:
        scratch.append(pltpu.VMEM((2 * SPAN + rows, width), jnp.float32))
        scratch.append(pltpu.VMEM((2, SPAN // rows, rows, width), both.dtype))
    if last:
        out_shape = jax.ShapeDtypeStruct((blocks, pair, rows, width), both.dtype)
        out_specs = pl.BlockSpec(out_shape.shape, lambda n: (0, 0, 0, 0))
        scratch = [pltpu.VMEM((1, 2, pair * rows, width), jnp.float32)] * 2 + scratch
    else:
        out_shape, out_specs = [held, held], [held_spec(both)] * 2
    return pl.pallas_call(
        functools.partial(
            attend_kernel, step=step, steerable=bias is not None, last=last, series=series
        ),
        grid=(blocks // 2,),
        in_specs=in_specs,
        out_specs=out_specs,
        out_shape=out_shape,
        scratch_shapes=scratch,
        compiler_params=params(),
        cost_estimate=cost(
            pair * (blocks * rows) ** 2 / (1 if step == 1 else 2),
            4 * both.size + 8 * pair * blocks * rows * width,
        ),
    )(*operands)


def unpack_kernel(scalars, out_a, out_b, attention, heads_ref):
    for n in range(GROUP):
        for group_head in range(2):
            heads_ref[2 * scalars[n] + group_head] = out_a[n, group_head]
            heads_ref[2 * scalars[GROUP + n] + group_head] = out_b[n, group_head]
    attention[...] = jnp.transpose(heads_ref[...], (1, 0, 2))


def unpack(scalars, out_a, out_b):
    blocks, pair, rows, width = out_a.shape
    heads = 2 * blocks * pair
    return pl.pallas_call(
        unpack_kernel,
        in_specs=[smem(), vmem(), vmem()],
        out_specs=vmem(),
        out_shape=jax.ShapeDtypeStruct((rows, heads, width), out_a.dtype),
        scratch_shapes=[pltpu.VMEM((heads, rows, width), out_a.dtype)],
        compiler_params=params(),
        cost_estimate=cost(0, 8 * out_a.size),
    )(scalars, out_a, out_b)


def per_device(queries, key_value, damping, span_start, steered_heads):
    rows = queries.shape[0]
    device_count = lax.axis_size("seq")
    assert WINDOW == 2 * GROUP * rows and device_count == 4 * GROUP
    assert key_value.shape[2] == 2 * GROUP and queries.shape[1] == 4 * GROUP
    assert steered_heads.shape[0] <= GROUP
    groups = [
        list(range(first, first + GROUP)) for first in range(0, device_count, GROUP)
    ]

    def exchange(blocks):
        return lax.all_to_all(
            blocks, "seq", split_axis=0, concat_axis=0, axis_index_groups=groups, tiled=True
        )

    def onward(blocks, planes=1):
        shift = planes * GROUP
        pairs = [(n, n + shift) for n in range(device_count - shift)]
        return lax.ppermute(blocks, "seq", pairs)

    def after(value, earlier):
        return lax.optimization_barrier((value, earlier))[0]

    index = lax.axis_index("seq").astype(jnp.int32).reshape(1)
    both_a, states_b, queries_b, scalars = pack(
        index, span_start, steered_heads, queries, key_value
    )
    both_b = jnp.concatenate([states_b, queries_b], axis=1)
    position = jnp.arange(damping.shape[0], dtype=jnp.int32)
    emphasized = (position >= span_start[0]) & (position < span_start[0] + SPAN)
    bias = jnp.where(emphasized, 0.0, jnp.log2(damping.astype(jnp.float32)))
    bias = bias.reshape(-1, rows)

    raw_b = onward(states_b)
    both_a = exchange(both_a)
    states_a = both_a[:, :2]
    back_a = onward(after(states_a, raw_b))
    length = GROUP * rows
    span_states = lax.dynamic_slice_in_dim(
        after(both_a, back_a)[:, :2].transpose(1, 0, 2, 3).reshape(2, length, -1),
        jnp.minimum(span_start[0], length - SPAN),
        SPAN,
        1,
    )
    span_states = onward(span_states, 3)
    back_b = exchange(after(raw_b, states_a))
    held_a = attend(0, scalars, bias, after(both_a, raw_b), both_a)
    both_b = exchange(after(both_b, (back_b, held_a)))
    far_a = onward(back_a)
    held_a = attend(1, scalars, bias, both_a, back_a, held_a)
    held_b = attend(0, scalars, None, after(both_b, held_a), both_b)
    far_b = onward(after(back_b, held_b))
    held_b = attend(1, scalars, None, both_b, back_b, held_b)
    out_a = attend(
        2, scalars, bias, both_a, far_a, after(held_a, held_b), span_states, last=True
    )
    held_b = after(held_b, out_a)
    out_a = exchange(out_a)
    out_b = attend(2, scalars, None, both_b, far_b, held_b, last=True)
    out_b = exchange(out_b)
    return unpack(scalars, out_a, out_b)


def solution(mesh):
    in_specs = (
        P(("prompt", "seq"), None, None),
        P(None, ("prompt", "seq"), None, None),
        P("prompt"),
        P("prompt"),
        P(),
    )
    out_specs = P(("prompt", "seq"), None, None)
    return jax.shard_map(
        per_device, mesh=mesh, in_specs=in_specs, out_specs=out_specs, check_vma=False
    )
```

```python
import functools
import math

import jax
import jax.numpy as jnp
from jax import lax
from jax.experimental import pallas as pl
from jax.experimental.pallas import tpu as pltpu
from jax.sharding import PartitionSpec as P

WINDOW = 4096
SPAN = 512

SCORE_SCALE = 144.0 ** (-0.5)
SOFTCAP = 50.0
LOG2_E = math.log2(math.e)

GROUP = 8
CHUNK = 64
TOKEN_STEPS = 4
PAIR_FLOPS = 256
VMEM_BYTES = 48 * 1024 * 1024

FIRST_SCALAR = 32
PLANE, SPAN_FIRST, STEERED_0, STEERED_1 = range(FIRST_SCALAR, FIRST_SCALAR + 4)
SCALARS = FIRST_SCALAR + 4


def smem():
    return pl.BlockSpec(memory_space=pltpu.SMEM)


def vmem():
    return pl.BlockSpec(memory_space=pltpu.VMEM)


def in_hbm(operand):
    return pltpu.with_memory_space_constraint(operand, pltpu.HBM)


def params():
    return pltpu.CompilerParams(vmem_limit_bytes=VMEM_BYTES)


def cost(pairs, moved):
    return pl.CostEstimate(
        flops=int(pairs * PAIR_FLOPS), bytes_accessed=int(moved), transcendentals=int(2 * pairs)
    )


def pack_kernel(
    index_ref, span_ref, steered_ref, queries_ref, states_ref,
    both_a, states_b, queries_b, scalars, query_heads, state_heads,
):
    key_heads = states_ref.shape[2]
    steered_count = steered_ref.shape[0]

    @pl.when(pl.program_id(0) == 0)
    def _():
        steered_keys = [lax.div(steered_ref[n], 2) for n in range(steered_count)]
        flags = []
        for head in range(key_heads):
            hit = steered_keys[0] == head
            for n in range(1, steered_count):
                hit = hit | (steered_keys[n] == head)
            flags.append(hit.astype(jnp.int32))
        total = sum(flags[1:], flags[0])
        before = jnp.int32(0)
        for head in range(key_heads):
            rank = jnp.where(flags[head] == 1, before, total + head - before)
            scalars[rank] = jnp.int32(head)
            before = before + flags[head]
        place = lax.rem(index_ref[0], GROUP)
        scalars[PLANE] = lax.div(index_ref[0], GROUP)
        scalars[SPAN_FIRST] = span_ref[0]
        own_head = scalars[place]
        for group_head in range(2):
            hit = steered_ref[0] == 2 * own_head + group_head
            for n in range(1, steered_count):
                hit = hit | (steered_ref[n] == 2 * own_head + group_head)
            scalars[STEERED_0 + group_head] = hit.astype(jnp.int32)

    for part in range(2):
        state_heads[part] = jnp.transpose(states_ref[part], (1, 0, 2))
        for n in range(GROUP):
            both_a[n, part] = state_heads[part, scalars[n]]
            states_b[n, part] = state_heads[part, scalars[GROUP + n]]
    query_heads[...] = jnp.transpose(queries_ref[...], (1, 0, 2))
    for n in range(GROUP):
        for group_head in range(2):
            both_a[n, 2 + group_head] = query_heads[2 * scalars[n] + group_head]
            queries_b[n, group_head] = query_heads[2 * scalars[GROUP + n] + group_head]


def pack(index, span_start, steered_heads, queries, states):
    rows, heads, width = queries.shape
    key_heads = states.shape[2]
    some = rows // TOKEN_STEPS

    def sent(parts):
        shape = pltpu.HBM((GROUP, parts, rows, width), queries.dtype)
        return shape, pl.BlockSpec((GROUP, parts, some, width), lambda n: (0, 0, n, 0))

    shapes, specs = zip(sent(4), sent(2), sent(2))
    return pl.pallas_call(
        pack_kernel,
        grid=(TOKEN_STEPS,),
        in_specs=[smem()] * 3
        + [
            pl.BlockSpec((some, heads, width), lambda n: (n, 0, 0)),
            pl.BlockSpec((2, some, key_heads, width), lambda n: (0, n, 0, 0)),
        ],
        out_specs=list(specs) + [smem()],
        out_shape=list(shapes) + [jax.ShapeDtypeStruct((SCALARS,), jnp.int32)],
        scratch_shapes=[
            pltpu.VMEM((heads, some, width), queries.dtype),
            pltpu.VMEM((2, key_heads, some, width), queries.dtype),
        ],
        compiler_params=params(),
        cost_estimate=cost(0, 4 * (queries.size + states.size)),
    )(index, span_start, steered_heads, in_hbm(queries), in_hbm(states))


def raw_scores(query, key):
    return lax.dot_general(
        query, key, (((1,), (1,)), ((), ())), preferred_element_type=jnp.float32
    )


def weights(raw_score, bias, visible):
    score = jnp.tanh(raw_score * (SCORE_SCALE / SOFTCAP)) * (SOFTCAP * LOG2_E)
    weight = jnp.exp2(score if bias is None else score + bias)
    return weight if visible is None else jnp.where(visible, weight, 0.0)


def lane_sums(weight, lanes):
    sums = weight[:, :lanes]
    for first in range(lanes, weight.shape[1], lanes):
        sums = sums + weight[:, first : first + lanes]
    return sums


def attend_kernel(*refs, step, steerable, last):
    refs = list(refs)
    scalars = refs.pop(0)
    bias_ref = refs.pop(0) if steerable else None
    low_ref, high_ref, states_ref = refs.pop(0), refs.pop(0), refs.pop(0)
    span_ref = refs.pop(0) if steerable and last else None
    if step:
        old_weighted, old_sums = refs.pop(0), refs.pop(0)
    if last:
        out_ref = refs.pop(0)
    weighted_ref, sums_ref, query_ref = refs[:3]
    around_ref, gathered_ref = refs[3:] if steerable and last else (None, None)
    low = pl.program_id(0)
    blocks, _, rows, width = states_ref.shape
    high = blocks - 1 - low
    plane = scalars[PLANE]
    first_block = (plane - step) * blocks
    query_ref[0] = low_ref[0].reshape(2 * rows, width)
    query_ref[1] = high_ref[0].reshape(2 * rows, width)
    if step:
        weighted_ref[...] = old_weighted[...]
        sums_ref[...] = old_sums[...]
    else:
        weighted_ref[...] = jnp.zeros(weighted_ref.shape, jnp.float32)
        sums_ref[...] = jnp.zeros(sums_ref.shape, jnp.float32)
    flags = [scalars[STEERED_0 + n] for n in range(2)]
    flag_values = [flag.astype(jnp.float32) for flag in flags]

    def states(part, key_block, count):
        if count == 1:
            return states_ref[key_block, part]
        return states_ref[pl.ds(key_block, count), part].reshape(count * rows, width)

    def bias(key_block, count):
        if not steerable:
            return None
        parts = [bias_ref[pl.ds(first_block + key_block + n, 1), :] for n in range(count)]
        row = parts[0] if count == 1 else jnp.concatenate(parts, axis=1)
        return [row * value for value in flag_values]

    def add(tiles):
        def of_span(key_block):
            return isinstance(key_block, int) and key_block < 0

        def part_of(part, key_block, count):
            if of_span(key_block):
                return gathered_ref[part, ~key_block]
            return states(part, key_block, count)

        def score(tile):
            which, key_block, count, _ = tile
            return raw_scores(query_ref[which], part_of(0, key_block, count))

        ahead = score(tiles[0])
        for n, (which, key_block, count, visible) in enumerate(tiles):
            raw_score = ahead
            if n + 1 < len(tiles):
                ahead = score(tiles[n + 1])
            added = None if of_span(key_block) else bias(key_block, count)
            chunk = CHUNK // count
            rounded = []
            for first in range(0, 2 * rows, chunk):
                head, row = first // rows, first % rows
                weight = weights(
                    raw_score[first : first + chunk],
                    None if added is None else added[head],
                    None if visible is None else visible(head, row, chunk),
                )
                some = pl.ds(first, chunk)
                sums_ref[0, which, some, :] += lane_sums(weight, width)
                rounded.append(weight.astype(jnp.bfloat16))
            weighted_ref[0, which] += jnp.dot(
                jnp.concatenate(rounded, axis=0),
                part_of(1, key_block, count),
                preferred_element_type=jnp.float32,
            )

    def gather_span():
        start = scalars[SPAN_FIRST] - first_block * rows
        pad = SPAN // rows
        for part in range(2):
            before = span_ref[part].astype(jnp.float32)

            @pl.when(start < 0)
            def _():
                around_ref[:SPAN, :] = before
                for n in range(2):
                    around_ref[SPAN + n * rows : SPAN + (n + 1) * rows, :] = states_ref[
                        n, part
                    ].astype(jnp.float32)

            block = jnp.clip(lax.div(jnp.maximum(start, 0), rows), 0, blocks - pad - 1)

            @pl.when(start >= 0)
            def _():
                for n in range(pad + 1):
                    around_ref[n * rows : (n + 1) * rows, :] = states_ref[
                        block + n, part
                    ].astype(jnp.float32)
                around_ref[(pad + 1) * rows :, :] = jnp.zeros((SPAN, width), jnp.float32)

            offset = jnp.where(start < 0, jnp.maximum(start + SPAN, 0), start - block * rows)
            for n in range(pad):
                gathered_ref[part, n] = around_ref[pl.ds(offset + n * rows, rows), :].astype(
                    jnp.bfloat16
                )

    def ranks(row, count):
        shape = (count, rows)
        return (
            row
            + lax.broadcasted_iota(jnp.int32, shape, 0)
            - lax.broadcasted_iota(jnp.int32, shape, 1)
        )

    def span_tiles():
        tiles = []
        for which, block in ((0, low), (1, high)):
            for n in range(SPAN // rows):
                nearest = scalars[SPAN_FIRST] + n * rows + WINDOW - (plane * blocks + block) * rows
                least = [jnp.where(flag == 1, nearest, 2 * rows) for flag in flags]

                def visible(head, row, count, least=least):
                    return ranks(row, count) >= least[head]

                tiles.append((which, ~n, 1, visible))
        return tiles

    def compute():
        if step == 1:
            add([(which, n, 2, None) for which in range(2) for n in range(0, blocks, 2)])
            return
        tiles = []
        for n in range(blocks - 1):
            if step == 0:
                is_low = n < low
                tiles.append((jnp.where(is_low, 0, 1), jnp.where(is_low, n, n - low), 1, None))
            else:
                is_high = n < low
                tiles.append(
                    (jnp.where(is_high, 1, 0), jnp.where(is_high, high + 1 + n, n + 1), 1, None)
                )

        def visible(head, row, count):
            return ranks(row, count) >= 0 if step == 0 else ranks(row, count) < 0

        for which, block in ((0, low), (1, high)):
            tiles.append((which, block, 1, visible))
        if not (steerable and last):
            add(tiles)
            return
        wanted = flags[0] + flags[1] > 0
        wanted = wanted & (scalars[SPAN_FIRST] < (first_block + blocks) * rows)
        pl.when(wanted & (low == 0))(gather_span)
        pl.when(wanted)(lambda: add(tiles + span_tiles()))
        pl.when(jnp.logical_not(wanted))(lambda: add(tiles))

    if step:
        pl.when(plane >= step)(compute)
    else:
        compute()
    if last:
        write_result(out_ref, weighted_ref, sums_ref, low, high)


def write_result(out_ref, weighted_ref, sums_ref, low, high):
    for which, block in ((0, low), (1, high)):
        total = jnp.sum(sums_ref[0, which], axis=-1, keepdims=True)
        result = (weighted_ref[0, which] / total).astype(out_ref.dtype)
        out_ref[block] = result.reshape(out_ref.shape[1:])


def query_specs(both):
    blocks, _, rows, width = both.shape
    one = (1, 2, rows, width)
    return [
        pl.BlockSpec(one, lambda n: (n, 1, 0, 0)),
        pl.BlockSpec(one, lambda n: (blocks - 1 - n, 1, 0, 0)),
    ]


def held_spec(both):
    _, _, rows, width = both.shape
    return pl.BlockSpec((1, 2, 2 * rows, width), lambda n: (n, 0, 0, 0))


def attend(step, scalars, bias, both, states, carried=None, span_states=None, last=False):
    blocks, parts, rows, width = both.shape
    pair = 2
    assert blocks % 2 == 0 and parts == 2 + pair
    held = pltpu.HBM((blocks // 2, 2, pair * rows, width), jnp.float32)
    whole = pl.BlockSpec((blocks, 2, rows, width), lambda n: (0, 0, 0, 0))
    operands, in_specs = [scalars], [smem()]
    if bias is not None:
        operands.append(bias)
        in_specs.append(pl.BlockSpec(bias.shape, lambda n: (0, 0)))
    operands += [both, both, states]
    in_specs += query_specs(both) + [whole]
    if span_states is not None:
        operands.append(span_states)
        in_specs.append(pl.BlockSpec(span_states.shape, lambda n: (0, 0, 0)))
    if carried is not None:
        operands += [in_hbm(sums) for sums in carried]
        in_specs += [held_spec(both)] * 2
    scratch = [pltpu.VMEM((2, pair * rows, width), both.dtype)]
    if span_states is not None:
        scratch.append(pltpu.VMEM((2 * SPAN + rows, width), jnp.float32))
        scratch.append(pltpu.VMEM((2, SPAN // rows, rows, width), both.dtype))
    if last:
        out_shape = jax.ShapeDtypeStruct((blocks, pair, rows, width), both.dtype)
        out_specs = pl.BlockSpec(out_shape.shape, lambda n: (0, 0, 0, 0))
        scratch = [pltpu.VMEM((1, 2, pair * rows, width), jnp.float32)] * 2 + scratch
    else:
        out_shape, out_specs = [held, held], [held_spec(both)] * 2
    return pl.pallas_call(
        functools.partial(attend_kernel, step=step, steerable=bias is not None, last=last),
        grid=(blocks // 2,),
        in_specs=in_specs,
        out_specs=out_specs,
        out_shape=out_shape,
        scratch_shapes=scratch,
        compiler_params=params(),
        cost_estimate=cost(
            pair * (blocks * rows) ** 2 / (1 if step == 1 else 2),
            4 * both.size + 8 * pair * blocks * rows * width,
        ),
    )(*operands)


def unpack_kernel(scalars, out_a, out_b, attention, heads_ref):
    for n in range(GROUP):
        for group_head in range(2):
            heads_ref[2 * scalars[n] + group_head] = out_a[n, group_head]
            heads_ref[2 * scalars[GROUP + n] + group_head] = out_b[n, group_head]
    attention[...] = jnp.transpose(heads_ref[...], (1, 0, 2))


def unpack(scalars, out_a, out_b):
    blocks, pair, rows, width = out_a.shape
    heads = 2 * blocks * pair
    return pl.pallas_call(
        unpack_kernel,
        in_specs=[smem(), vmem(), vmem()],
        out_specs=vmem(),
        out_shape=jax.ShapeDtypeStruct((rows, heads, width), out_a.dtype),
        scratch_shapes=[pltpu.VMEM((heads, rows, width), out_a.dtype)],
        compiler_params=params(),
        cost_estimate=cost(0, 8 * out_a.size),
    )(scalars, out_a, out_b)


def per_device(queries, key_value, damping, span_start, steered_heads):
    rows = queries.shape[0]
    device_count = lax.axis_size("seq")
    assert WINDOW == 2 * GROUP * rows and device_count == 4 * GROUP
    assert key_value.shape[2] == 2 * GROUP and queries.shape[1] == 4 * GROUP
    assert steered_heads.shape[0] <= GROUP
    groups = [
        list(range(first, first + GROUP)) for first in range(0, device_count, GROUP)
    ]

    def exchange(blocks):
        return lax.all_to_all(
            blocks, "seq", split_axis=0, concat_axis=0, axis_index_groups=groups, tiled=True
        )

    def onward(blocks, planes=1):
        shift = planes * GROUP
        pairs = [(n, n + shift) for n in range(device_count - shift)]
        return lax.ppermute(blocks, "seq", pairs)

    def after(value, earlier):
        return lax.optimization_barrier((value, earlier))[0]

    index = lax.axis_index("seq").astype(jnp.int32).reshape(1)
    both_a, states_b, queries_b, scalars = pack(
        index, span_start, steered_heads, queries, key_value
    )
    both_b = jnp.concatenate([states_b, queries_b], axis=1)
    position = jnp.arange(damping.shape[0], dtype=jnp.int32)
    emphasized = (position >= span_start[0]) & (position < span_start[0] + SPAN)
    bias = jnp.where(emphasized, 0.0, jnp.log2(damping.astype(jnp.float32)))
    bias = bias.reshape(-1, rows)

    raw_b = onward(states_b)
    both_a = exchange(both_a)
    states_a = both_a[:, :2]
    back_a = onward(after(states_a, raw_b))
    length = GROUP * rows
    span_states = lax.dynamic_slice_in_dim(
        after(both_a, back_a)[:, :2].transpose(1, 0, 2, 3).reshape(2, length, -1),
        jnp.minimum(span_start[0], length - SPAN),
        SPAN,
        1,
    )
    span_states = onward(span_states, 3)
    both_b = exchange(after(both_b, states_a))
    held_a = attend(0, scalars, bias, after(both_a, raw_b), both_a)
    back_b = exchange(after(raw_b, (both_b, held_a)))
    far_a = onward(back_a)
    held_b = attend(0, scalars, None, after(both_b, (held_a, back_a)), both_b)
    far_b = onward(back_b)
    held_a = attend(1, scalars, bias, after(both_a, (held_b, back_b)), back_a, held_a)
    out_a = attend(2, scalars, bias, both_a, far_a, held_a, span_states, last=True)
    held_b = attend(1, scalars, None, both_b, back_b, after(held_b, out_a))
    out_a = exchange(out_a)
    out_b = attend(2, scalars, None, both_b, far_b, held_b, last=True)
    out_b = exchange(out_b)
    return unpack(scalars, out_a, out_b)


def solution(mesh):
    in_specs = (
        P(("prompt", "seq"), None, None),
        P(None, ("prompt", "seq"), None, None),
        P("prompt"),
        P("prompt"),
        P(),
    )
    out_specs = P(("prompt", "seq"), None, None)
    return jax.shard_map(
        per_device, mesh=mesh, in_specs=in_specs, out_specs=out_specs, check_vma=False
    )
```

```python
import functools
import math

import jax
import jax.numpy as jnp
from jax import lax
from jax.experimental import pallas as pl
from jax.experimental.pallas import tpu as pltpu
from jax.sharding import PartitionSpec as P

WINDOW = 4096
SPAN = 512

SCORE_SCALE = 144.0 ** (-0.5)
SOFTCAP = 50.0
LOG2_E = math.log2(math.e)

GROUP = 8
CHUNK = 64
TOKEN_STEPS = 4
PAIR_FLOPS = 256
VMEM_BYTES = 48 * 1024 * 1024

FIRST_SCALAR = 32
PLANE, SPAN_FIRST, STEERED_0, STEERED_1 = range(FIRST_SCALAR, FIRST_SCALAR + 4)
SCALARS = FIRST_SCALAR + 4


def smem():
    return pl.BlockSpec(memory_space=pltpu.SMEM)


def vmem():
    return pl.BlockSpec(memory_space=pltpu.VMEM)


def in_hbm(operand):
    return pltpu.with_memory_space_constraint(operand, pltpu.HBM)


def params():
    return pltpu.CompilerParams(vmem_limit_bytes=VMEM_BYTES)


def cost(pairs, moved):
    return pl.CostEstimate(
        flops=int(pairs * PAIR_FLOPS), bytes_accessed=int(moved), transcendentals=int(2 * pairs)
    )


def pack_kernel(
    index_ref, span_ref, steered_ref, queries_ref, states_ref,
    states_a, queries_a, states_b, queries_b, scalars, query_heads, state_heads,
):
    key_heads = states_ref.shape[2]
    steered_count = steered_ref.shape[0]

    @pl.when(pl.program_id(0) == 0)
    def _():
        steered_keys = [lax.div(steered_ref[n], 2) for n in range(steered_count)]
        flags = []
        for head in range(key_heads):
            hit = steered_keys[0] == head
            for n in range(1, steered_count):
                hit = hit | (steered_keys[n] == head)
            flags.append(hit.astype(jnp.int32))
        total = sum(flags[1:], flags[0])
        before = jnp.int32(0)
        for head in range(key_heads):
            rank = jnp.where(flags[head] == 1, before, total + head - before)
            scalars[rank] = jnp.int32(head)
            before = before + flags[head]
        place = lax.rem(index_ref[0], GROUP)
        scalars[PLANE] = lax.div(index_ref[0], GROUP)
        scalars[SPAN_FIRST] = span_ref[0]
        own_head = scalars[place]
        for group_head in range(2):
            hit = steered_ref[0] == 2 * own_head + group_head
            for n in range(1, steered_count):
                hit = hit | (steered_ref[n] == 2 * own_head + group_head)
            scalars[STEERED_0 + group_head] = hit.astype(jnp.int32)

    for part in range(2):
        state_heads[part] = jnp.transpose(states_ref[part], (1, 0, 2))
        for n in range(GROUP):
            states_a[n, part] = state_heads[part, scalars[n]]
            states_b[n, part] = state_heads[part, scalars[GROUP + n]]
    query_heads[...] = jnp.transpose(queries_ref[...], (1, 0, 2))
    for n in range(GROUP):
        for group_head in range(2):
            queries_a[n, group_head] = query_heads[2 * scalars[n] + group_head]
            queries_b[n, group_head] = query_heads[2 * scalars[GROUP + n] + group_head]


def pack(index, span_start, steered_heads, queries, states):
    rows, heads, width = queries.shape
    key_heads = states.shape[2]
    some = rows // TOKEN_STEPS

    sent = pltpu.HBM((GROUP, 2, rows, width), queries.dtype)
    sent_spec = pl.BlockSpec((GROUP, 2, some, width), lambda n: (0, 0, n, 0))
    return pl.pallas_call(
        pack_kernel,
        grid=(TOKEN_STEPS,),
        in_specs=[smem()] * 3
        + [
            pl.BlockSpec((some, heads, width), lambda n: (n, 0, 0)),
            pl.BlockSpec((2, some, key_heads, width), lambda n: (0, n, 0, 0)),
        ],
        out_specs=[sent_spec] * 4 + [smem()],
        out_shape=[sent] * 4 + [jax.ShapeDtypeStruct((SCALARS,), jnp.int32)],
        scratch_shapes=[
            pltpu.VMEM((heads, some, width), queries.dtype),
            pltpu.VMEM((2, key_heads, some, width), queries.dtype),
        ],
        compiler_params=params(),
        cost_estimate=cost(0, 4 * (queries.size + states.size)),
    )(index, span_start, steered_heads, in_hbm(queries), in_hbm(states))


def raw_scores(query, key):
    return lax.dot_general(
        query, key, (((1,), (1,)), ((), ())), preferred_element_type=jnp.float32
    )


def weights(raw_score, bias, visible):
    capped = jnp.tanh(raw_score * (SCORE_SCALE / SOFTCAP))
    if bias is None:
        weight = jnp.exp2(capped * (SOFTCAP * LOG2_E))
    else:
        weight = jnp.exp(capped * SOFTCAP + bias)
    return weight if visible is None else jnp.where(visible, weight, 0.0)


def lane_sums(weight, lanes):
    sums = weight[:, :lanes]
    for first in range(lanes, weight.shape[1], lanes):
        sums = sums + weight[:, first : first + lanes]
    return sums


def attend_kernel(*refs, step, steerable, last):
    refs = list(refs)
    scalars = refs.pop(0)
    bias_ref = refs.pop(0) if steerable else None
    low_ref, high_ref, states_ref = refs.pop(0), refs.pop(0), refs.pop(0)
    span_ref = refs.pop(0) if steerable and last else None
    if step:
        old_weighted, old_sums = refs.pop(0), refs.pop(0)
    if last:
        out_ref = refs.pop(0)
    weighted_ref, sums_ref, query_ref = refs[:3]
    around_ref, gathered_ref = refs[3:] if steerable and last else (None, None)
    low = pl.program_id(0)
    blocks, _, rows, width = states_ref.shape
    high = blocks - 1 - low
    plane = scalars[PLANE]
    first_block = (plane - step) * blocks
    query_ref[0] = low_ref[0].reshape(2 * rows, width)
    query_ref[1] = high_ref[0].reshape(2 * rows, width)
    if step:
        weighted_ref[...] = old_weighted[...]
        sums_ref[...] = old_sums[...]
    else:
        weighted_ref[...] = jnp.zeros(weighted_ref.shape, jnp.float32)
        sums_ref[...] = jnp.zeros(sums_ref.shape, jnp.float32)
    flags = [scalars[STEERED_0 + n] for n in range(2)]
    flag_values = [flag.astype(jnp.float32) for flag in flags]

    def states(part, key_block, count):
        if count == 1:
            return states_ref[key_block, part]
        return states_ref[pl.ds(key_block, count), part].reshape(count * rows, width)

    def bias(key_block, count):
        if not steerable:
            return None
        if isinstance(key_block, int) and key_block < 0:
            return [jnp.zeros((1, count * rows), jnp.float32)] * 2
        parts = [bias_ref[pl.ds(first_block + key_block + n, 1), :] for n in range(count)]
        row = parts[0] if count == 1 else jnp.concatenate(parts, axis=1)
        return [row * value for value in flag_values]

    def add(tiles):
        def of_span(key_block):
            return isinstance(key_block, int) and key_block < 0

        def part_of(part, key_block, count):
            if of_span(key_block):
                return gathered_ref[part, ~key_block]
            return states(part, key_block, count)

        def score(tile):
            which, key_block, count, _ = tile
            return raw_scores(query_ref[which], part_of(0, key_block, count))

        ahead = score(tiles[0])
        for n, (which, key_block, count, visible) in enumerate(tiles):
            raw_score = ahead
            if n + 1 < len(tiles):
                ahead = score(tiles[n + 1])
            added = bias(key_block, count)
            chunk = CHUNK // count
            rounded = []
            for first in range(0, 2 * rows, chunk):
                head, row = first // rows, first % rows
                columns = slice(0, count * rows)
                if visible is in_order:
                    columns = slice(0, -(-(row + chunk) // width) * width)
                    if step:
                        columns = slice(row // width * width, rows)
                weight = weights(
                    raw_score[first : first + chunk, columns],
                    None if added is None else added[head][:, columns],
                    None if visible is None else visible(head, row, chunk)[:, columns],
                )
                some = pl.ds(first, chunk)
                sums_ref[0, which, some, :] += lane_sums(weight, width)
                weight = weight.astype(jnp.bfloat16)
                sides = [
                    jnp.zeros((chunk, size), jnp.bfloat16)
                    for size in (columns.start, count * rows - columns.stop)
                ]
                parts = [part for part in (sides[0], weight, sides[1]) if part.shape[1]]
                rounded.append(parts[0] if len(parts) == 1 else jnp.concatenate(parts, axis=1))
            weighted_ref[0, which] += jnp.dot(
                jnp.concatenate(rounded, axis=0),
                part_of(1, key_block, count),
                preferred_element_type=jnp.float32,
            )

    def gather_span():
        start = scalars[SPAN_FIRST] - first_block * rows
        pad = SPAN // rows
        for part in range(2):
            before = span_ref[part].astype(jnp.float32)

            @pl.when(start < 0)
            def _():
                around_ref[:SPAN, :] = before
                for n in range(2):
                    around_ref[SPAN + n * rows : SPAN + (n + 1) * rows, :] = states_ref[
                        n, part
                    ].astype(jnp.float32)

            block = jnp.clip(lax.div(jnp.maximum(start, 0), rows), 0, blocks - pad - 1)

            @pl.when(start >= 0)
            def _():
                for n in range(pad + 1):
                    around_ref[n * rows : (n + 1) * rows, :] = states_ref[
                        block + n, part
                    ].astype(jnp.float32)
                around_ref[(pad + 1) * rows :, :] = jnp.zeros((SPAN, width), jnp.float32)

            offset = jnp.where(start < 0, jnp.maximum(start + SPAN, 0), start - block * rows)
            for n in range(pad):
                gathered_ref[part, n] = around_ref[pl.ds(offset + n * rows, rows), :].astype(
                    jnp.bfloat16
                )

    def ranks(row, count):
        shape = (count, rows)
        return (
            row
            + lax.broadcasted_iota(jnp.int32, shape, 0)
            - lax.broadcasted_iota(jnp.int32, shape, 1)
        )

    def in_order(head, row, count):
        return ranks(row, count) >= 0 if step == 0 else ranks(row, count) < 0

    def span_tiles():
        tiles = []
        for which, block in ((0, low), (1, high)):
            for n in range(SPAN // rows):
                nearest = scalars[SPAN_FIRST] + n * rows + WINDOW - (plane * blocks + block) * rows
                least = [jnp.where(flag == 1, nearest, 2 * rows) for flag in flags]

                def visible(head, row, count, least=least):
                    return ranks(row, count) >= least[head]

                tiles.append((which, ~n, 1, visible))
        return tiles

    def compute():
        if step == 1:
            add([(which, n, 2, None) for which in range(2) for n in range(0, blocks, 2)])
            return
        tiles = []
        for n in range(blocks - 1):
            if step == 0:
                is_low = n < low
                tiles.append((jnp.where(is_low, 0, 1), jnp.where(is_low, n, n - low), 1, None))
            else:
                is_high = n < low
                tiles.append(
                    (jnp.where(is_high, 1, 0), jnp.where(is_high, high + 1 + n, n + 1), 1, None)
                )

        for which, block in ((0, low), (1, high)):
            tiles.append((which, block, 1, in_order))
        if not (steerable and last):
            add(tiles)
            return
        wanted = flags[0] + flags[1] > 0
        wanted = wanted & (scalars[SPAN_FIRST] < (first_block + blocks) * rows)
        pl.when(wanted & (low == 0))(gather_span)
        pl.when(wanted)(lambda: add(tiles + span_tiles()))
        pl.when(jnp.logical_not(wanted))(lambda: add(tiles))

    if step:
        pl.when(plane >= step)(compute)
    else:
        compute()
    if last:
        write_result(out_ref, weighted_ref, sums_ref, low, high)


def write_result(out_ref, weighted_ref, sums_ref, low, high):
    for which, block in ((0, low), (1, high)):
        total = jnp.sum(sums_ref[0, which], axis=-1, keepdims=True)
        result = (weighted_ref[0, which] / total).astype(out_ref.dtype)
        out_ref[block] = result.reshape(out_ref.shape[1:])


def query_specs(queries):
    blocks, parts, rows, width = queries.shape
    one, at = (1, 2, rows, width), parts // 2 - 1
    return [
        pl.BlockSpec(one, lambda n: (n, at, 0, 0)),
        pl.BlockSpec(one, lambda n: (blocks - 1 - n, at, 0, 0)),
    ]


def held_spec(queries):
    _, _, rows, width = queries.shape
    return pl.BlockSpec((1, 2, 2 * rows, width), lambda n: (n, 0, 0, 0))


def attend(step, scalars, bias, queries, states, carried=None, span_states=None, last=False):
    blocks, _, rows, width = queries.shape
    pair = 2
    assert blocks % 2 == 0
    held = pltpu.HBM((blocks // 2, 2, pair * rows, width), jnp.float32)
    whole = pl.BlockSpec((blocks, 2, rows, width), lambda n: (0, 0, 0, 0))
    operands, in_specs = [scalars], [smem()]
    if bias is not None:
        operands.append(bias)
        in_specs.append(pl.BlockSpec(bias.shape, lambda n: (0, 0)))
    operands += [queries, queries, states]
    in_specs += query_specs(queries) + [whole]
    if span_states is not None:
        operands.append(span_states)
        in_specs.append(pl.BlockSpec(span_states.shape, lambda n: (0, 0, 0)))
    if carried is not None:
        operands += [in_hbm(sums) for sums in carried]
        in_specs += [held_spec(queries)] * 2
    scratch = [pltpu.VMEM((2, pair * rows, width), queries.dtype)]
    if span_states is not None:
        scratch.append(pltpu.VMEM((2 * SPAN + rows, width), jnp.float32))
        scratch.append(pltpu.VMEM((2, SPAN // rows, rows, width), queries.dtype))
    if last:
        out_shape = jax.ShapeDtypeStruct((blocks, pair, rows, width), queries.dtype)
        out_specs = pl.BlockSpec(out_shape.shape, lambda n: (0, 0, 0, 0))
        scratch = [pltpu.VMEM((1, 2, pair * rows, width), jnp.float32)] * 2 + scratch
    else:
        out_shape, out_specs = [held, held], [held_spec(queries)] * 2
    return pl.pallas_call(
        functools.partial(attend_kernel, step=step, steerable=bias is not None, last=last),
        grid=(blocks // 2,),
        in_specs=in_specs,
        out_specs=out_specs,
        out_shape=out_shape,
        scratch_shapes=scratch,
        compiler_params=params(),
        cost_estimate=cost(
            pair * (blocks * rows) ** 2 / (1 if step == 1 else 2),
            8 * queries.size + 8 * pair * blocks * rows * width,
        ),
    )(*operands)


def unpack_kernel(scalars, out_a, out_b, attention, heads_ref):
    for n in range(GROUP):
        for group_head in range(2):
            heads_ref[2 * scalars[n] + group_head] = out_a[n, group_head]
            heads_ref[2 * scalars[GROUP + n] + group_head] = out_b[n, group_head]
    attention[...] = jnp.transpose(heads_ref[...], (1, 0, 2))


def unpack(scalars, out_a, out_b):
    blocks, pair, rows, width = out_a.shape
    heads = 2 * blocks * pair
    return pl.pallas_call(
        unpack_kernel,
        in_specs=[smem(), vmem(), vmem()],
        out_specs=vmem(),
        out_shape=jax.ShapeDtypeStruct((rows, heads, width), out_a.dtype),
        scratch_shapes=[pltpu.VMEM((heads, rows, width), out_a.dtype)],
        compiler_params=params(),
        cost_estimate=cost(0, 8 * out_a.size),
    )(scalars, out_a, out_b)


def per_device(queries, key_value, damping, span_start, steered_heads):
    rows = queries.shape[0]
    device_count = lax.axis_size("seq")
    assert WINDOW == 2 * GROUP * rows and device_count == 4 * GROUP
    assert key_value.shape[2] == 2 * GROUP and queries.shape[1] == 4 * GROUP
    assert steered_heads.shape[0] <= GROUP
    groups = [
        list(range(first, first + GROUP)) for first in range(0, device_count, GROUP)
    ]

    def exchange(blocks):
        return lax.all_to_all(
            blocks, "seq", split_axis=0, concat_axis=0, axis_index_groups=groups, tiled=True
        )

    def onward(blocks, planes=1):
        shift = planes * GROUP
        pairs = [(n, n + shift) for n in range(device_count - shift)]
        return lax.ppermute(blocks, "seq", pairs)

    def after(value, earlier):
        return lax.optimization_barrier((value, earlier))[0]

    index = lax.axis_index("seq").astype(jnp.int32).reshape(1)
    states_a, queries_a, states_b, queries_b, scalars = pack(
        index, span_start, steered_heads, queries, key_value
    )
    both_b = jnp.concatenate([states_b, queries_b], axis=1)
    position = jnp.arange(damping.shape[0], dtype=jnp.int32)
    emphasized = (position >= span_start[0]) & (position < span_start[0] + SPAN)
    bias = jnp.where(emphasized, 0.0, jnp.log(damping.astype(jnp.float32)))
    bias = bias.reshape(-1, rows)

    raw_b = onward(states_b)
    states_a = exchange(states_a)
    back_a = onward(after(states_a, raw_b))
    queries_a = exchange(after(queries_a, states_a))
    both_b = exchange(after(both_b, queries_a))
    held_a = attend(0, scalars, bias, after(queries_a, raw_b), states_a)
    far_a = onward(back_a)
    length = GROUP * rows
    span_states = lax.dynamic_slice_in_dim(
        after(states_a, (back_a, held_a)).transpose(1, 0, 2, 3).reshape(2, length, -1),
        jnp.minimum(span_start[0], length - SPAN),
        SPAN,
        1,
    )
    span_states = onward(span_states, 3)
    held_a = attend(1, scalars, bias, queries_a, back_a, held_a)
    back_b = exchange(after(raw_b, (both_b, held_a)))
    held_b = attend(0, scalars, None, after(both_b, held_a), both_b)
    far_b = onward(back_b)
    out_a = attend(
        2, scalars, bias, queries_a, far_a, after(held_a, held_b), span_states, last=True
    )
    held_b = attend(1, scalars, None, both_b, back_b, after(held_b, out_a))
    out_a = exchange(out_a)
    out_b = attend(2, scalars, None, both_b, far_b, held_b, last=True)
    out_b = exchange(out_b)
    return unpack(scalars, out_a, out_b)


def solution(mesh):
    in_specs = (
        P(("prompt", "seq"), None, None),
        P(None, ("prompt", "seq"), None, None),
        P("prompt"),
        P("prompt"),
        P(),
    )
    out_specs = P(("prompt", "seq"), None, None)
    return jax.shard_map(
        per_device, mesh=mesh, in_specs=in_specs, out_specs=out_specs, check_vma=False
    )
```

```python
import functools
import math

import jax
import jax.numpy as jnp
from jax import lax
from jax.experimental import pallas as pl
from jax.experimental.pallas import tpu as pltpu
from jax.sharding import PartitionSpec as P

WINDOW = 4096
SPAN = 512

SCORE_SCALE = 144.0 ** (-0.5)
SOFTCAP = 50.0
LOG2_E = math.log2(math.e)

GROUP = 8
CHUNK = 64
TOKEN_STEPS = 4
PAIR_FLOPS = 256
VMEM_BYTES = 48 * 1024 * 1024

FIRST_SCALAR = 32
PLANE, SPAN_FIRST, STEERED_0, STEERED_1 = range(FIRST_SCALAR, FIRST_SCALAR + 4)
SCALARS = FIRST_SCALAR + 4


def smem():
    return pl.BlockSpec(memory_space=pltpu.SMEM)


def vmem():
    return pl.BlockSpec(memory_space=pltpu.VMEM)


def in_hbm(operand):
    return pltpu.with_memory_space_constraint(operand, pltpu.HBM)


def params():
    return pltpu.CompilerParams(vmem_limit_bytes=VMEM_BYTES)


def cost(pairs, moved):
    return pl.CostEstimate(
        flops=int(pairs * PAIR_FLOPS), bytes_accessed=int(moved), transcendentals=int(2 * pairs)
    )


def pack_kernel(
    index_ref, span_ref, steered_ref, queries_ref, states_ref,
    both_a, states_b, all_b, scalars, query_heads, state_heads,
):
    key_heads = states_ref.shape[2]
    steered_count = steered_ref.shape[0]

    @pl.when(pl.program_id(0) == 0)
    def _():
        steered_keys = [lax.div(steered_ref[n], 2) for n in range(steered_count)]
        flags = []
        for head in range(key_heads):
            hit = steered_keys[0] == head
            for n in range(1, steered_count):
                hit = hit | (steered_keys[n] == head)
            flags.append(hit.astype(jnp.int32))
        total = sum(flags[1:], flags[0])
        before = jnp.int32(0)
        for head in range(key_heads):
            rank = jnp.where(flags[head] == 1, before, total + head - before)
            scalars[rank] = jnp.int32(head)
            before = before + flags[head]
        place = lax.rem(index_ref[0], GROUP)
        scalars[PLANE] = lax.div(index_ref[0], GROUP)
        scalars[SPAN_FIRST] = span_ref[0]
        own_head = scalars[place]
        for group_head in range(2):
            hit = steered_ref[0] == 2 * own_head + group_head
            for n in range(1, steered_count):
                hit = hit | (steered_ref[n] == 2 * own_head + group_head)
            scalars[STEERED_0 + group_head] = hit.astype(jnp.int32)

    for part in range(2):
        state_heads[part] = jnp.transpose(states_ref[part], (1, 0, 2))
        for n in range(GROUP):
            both_a[n, part] = state_heads[part, scalars[n]]
            state = state_heads[part, scalars[GROUP + n]]
            states_b[n, part] = state
            all_b[n, 2 + part] = state
    query_heads[...] = jnp.transpose(queries_ref[...], (1, 0, 2))
    for n in range(GROUP):
        for group_head in range(2):
            both_a[n, 2 + group_head] = query_heads[2 * scalars[n] + group_head]
            all_b[n, 4 + group_head] = query_heads[2 * scalars[GROUP + n] + group_head]


def pack(index, span_start, steered_heads, queries, states):
    rows, heads, width = queries.shape
    key_heads = states.shape[2]
    some = rows // TOKEN_STEPS


    def sent(parts):
        shape = pltpu.HBM((GROUP, parts, rows, width), queries.dtype)
        return shape, pl.BlockSpec((GROUP, parts, some, width), lambda n: (0, 0, n, 0))

    shapes, specs = zip(sent(4), sent(2), sent(6))
    return pl.pallas_call(
        pack_kernel,
        grid=(TOKEN_STEPS,),
        in_specs=[smem()] * 3
        + [
            pl.BlockSpec((some, heads, width), lambda n: (n, 0, 0)),
            pl.BlockSpec((2, some, key_heads, width), lambda n: (0, n, 0, 0)),
        ],
        out_specs=list(specs) + [smem()],
        out_shape=list(shapes) + [jax.ShapeDtypeStruct((SCALARS,), jnp.int32)],
        scratch_shapes=[
            pltpu.VMEM((heads, some, width), queries.dtype),
            pltpu.VMEM((2, key_heads, some, width), queries.dtype),
        ],
        compiler_params=params(),
        cost_estimate=cost(0, 4 * (queries.size + states.size)),
    )(index, span_start, steered_heads, in_hbm(queries), in_hbm(states))


def raw_scores(query, key):
    return lax.dot_general(
        query, key, (((1,), (1,)), ((), ())), preferred_element_type=jnp.float32
    )


def weights(raw_score, bias, visible):
    score = jnp.tanh(raw_score * (SCORE_SCALE / SOFTCAP)) * (SOFTCAP * LOG2_E)
    weight = jnp.exp2(score if bias is None else score + bias)
    return weight if visible is None else jnp.where(visible, weight, 0.0)


def lane_sums(weight, lanes):
    sums = weight[:, :lanes]
    for first in range(lanes, weight.shape[1], lanes):
        sums = sums + weight[:, first : first + lanes]
    return sums


def attend_kernel(*refs, step, steerable, last):
    refs = list(refs)
    scalars = refs.pop(0)
    bias_ref = refs.pop(0) if steerable else None
    low_ref, high_ref, states_ref = refs.pop(0), refs.pop(0), refs.pop(0)
    span_ref = refs.pop(0) if steerable and last else None
    if step:
        old_weighted, old_sums = refs.pop(0), refs.pop(0)
    if last:
        out_ref = refs.pop(0)
    weighted_ref, sums_ref, query_ref = refs[:3]
    around_ref, gathered_ref = refs[3:] if steerable and last else (None, None)
    low = pl.program_id(0)
    blocks, _, rows, width = states_ref.shape
    high = blocks - 1 - low
    plane = scalars[PLANE]
    first_block = (plane - step) * blocks
    query_ref[0] = low_ref[0].reshape(2 * rows, width)
    query_ref[1] = high_ref[0].reshape(2 * rows, width)
    if step:
        weighted_ref[...] = old_weighted[...]
        sums_ref[...] = old_sums[...]
    else:
        weighted_ref[...] = jnp.zeros(weighted_ref.shape, jnp.float32)
        sums_ref[...] = jnp.zeros(sums_ref.shape, jnp.float32)
    flags = [scalars[STEERED_0 + n] for n in range(2)]
    flag_values = [flag.astype(jnp.float32) for flag in flags]

    def states(part, key_block, count):
        if count == 1:
            return states_ref[key_block, part]
        return states_ref[pl.ds(key_block, count), part].reshape(count * rows, width)

    def bias(key_block, count):
        if not steerable:
            return None
        parts = [bias_ref[pl.ds(first_block + key_block + n, 1), :] for n in range(count)]
        row = parts[0] if count == 1 else jnp.concatenate(parts, axis=1)
        return [row * value for value in flag_values]

    def add(tiles):
        def of_span(key_block):
            return isinstance(key_block, int) and key_block < 0

        def part_of(part, key_block, count):
            if of_span(key_block):
                return gathered_ref[part, ~key_block]
            return states(part, key_block, count)

        def score(tile):
            which, key_block, count, _ = tile
            return raw_scores(query_ref[which], part_of(0, key_block, count))

        ahead = score(tiles[0])
        for n, (which, key_block, count, visible) in enumerate(tiles):
            raw_score = ahead
            if n + 1 < len(tiles):
                ahead = score(tiles[n + 1])
            added = None if of_span(key_block) else bias(key_block, count)
            chunk = CHUNK // count
            rounded = []
            for first in range(0, 2 * rows, chunk):
                head, row = first // rows, first % rows
                columns = slice(0, count * rows)
                if visible is in_order:
                    columns = slice(0, -(-(row + chunk) // width) * width)
                    if step:
                        columns = slice(row // width * width, rows)
                weight = weights(
                    raw_score[first : first + chunk, columns],
                    None if added is None else added[head][:, columns],
                    None if visible is None else visible(head, row, chunk)[:, columns],
                )
                some = pl.ds(first, chunk)
                sums_ref[0, which, some, :] += lane_sums(weight, width)
                weight = weight.astype(jnp.bfloat16)
                sides = [
                    jnp.zeros((chunk, size), jnp.bfloat16)
                    for size in (columns.start, count * rows - columns.stop)
                ]
                parts = [part for part in (sides[0], weight, sides[1]) if part.shape[1]]
                rounded.append(parts[0] if len(parts) == 1 else jnp.concatenate(parts, axis=1))
            weighted_ref[0, which] += jnp.dot(
                jnp.concatenate(rounded, axis=0),
                part_of(1, key_block, count),
                preferred_element_type=jnp.float32,
            )

    def gather_span():
        start = scalars[SPAN_FIRST] - first_block * rows
        pad = SPAN // rows
        for part in range(2):
            before = span_ref[part].astype(jnp.float32)

            @pl.when(start < 0)
            def _():
                around_ref[:SPAN, :] = before
                for n in range(2):
                    around_ref[SPAN + n * rows : SPAN + (n + 1) * rows, :] = states_ref[
                        n, part
                    ].astype(jnp.float32)

            block = jnp.clip(lax.div(jnp.maximum(start, 0), rows), 0, blocks - pad - 1)

            @pl.when(start >= 0)
            def _():
                for n in range(pad + 1):
                    around_ref[n * rows : (n + 1) * rows, :] = states_ref[
                        block + n, part
                    ].astype(jnp.float32)
                around_ref[(pad + 1) * rows :, :] = jnp.zeros((SPAN, width), jnp.float32)

            offset = jnp.where(start < 0, jnp.maximum(start + SPAN, 0), start - block * rows)
            for n in range(pad):
                gathered_ref[part, n] = around_ref[pl.ds(offset + n * rows, rows), :].astype(
                    jnp.bfloat16
                )

    def ranks(row, count):
        shape = (count, rows)
        return (
            row
            + lax.broadcasted_iota(jnp.int32, shape, 0)
            - lax.broadcasted_iota(jnp.int32, shape, 1)
        )

    def in_order(head, row, count):
        return ranks(row, count) >= 0 if step == 0 else ranks(row, count) < 0

    def span_tiles():
        tiles = []
        for which, block in ((0, low), (1, high)):
            for n in range(SPAN // rows):
                nearest = scalars[SPAN_FIRST] + n * rows + WINDOW - (plane * blocks + block) * rows
                least = [jnp.where(flag == 1, nearest, 2 * rows) for flag in flags]

                def visible(head, row, count, least=least):
                    return ranks(row, count) >= least[head]

                tiles.append((which, ~n, 1, visible))
        return tiles

    def compute():
        if step == 1:
            add([(which, n, 2, None) for which in range(2) for n in range(0, blocks, 2)])
            return
        tiles = []
        for n in range(blocks - 1):
            if step == 0:
                is_low = n < low
                tiles.append((jnp.where(is_low, 0, 1), jnp.where(is_low, n, n - low), 1, None))
            else:
                is_high = n < low
                tiles.append(
                    (jnp.where(is_high, 1, 0), jnp.where(is_high, high + 1 + n, n + 1), 1, None)
                )

        for which, block in ((0, low), (1, high)):
            tiles.append((which, block, 1, in_order))
        if not (steerable and last):
            add(tiles)
            return
        wanted = flags[0] + flags[1] > 0
        wanted = wanted & (scalars[SPAN_FIRST] < (first_block + blocks) * rows)
        pl.when(wanted & (low == 0))(gather_span)
        pl.when(wanted)(lambda: add(tiles + span_tiles()))
        pl.when(jnp.logical_not(wanted))(lambda: add(tiles))

    if step:
        pl.when(plane >= step)(compute)
    else:
        compute()
    if last:
        write_result(out_ref, weighted_ref, sums_ref, low, high)


def write_result(out_ref, weighted_ref, sums_ref, low, high):
    for which, block in ((0, low), (1, high)):
        total = jnp.sum(sums_ref[0, which], axis=-1, keepdims=True)
        result = (weighted_ref[0, which] / total).astype(out_ref.dtype)
        out_ref[block] = result.reshape(out_ref.shape[1:])


def query_specs(queries):
    blocks, parts, rows, width = queries.shape
    one, at = (1, 2, rows, width), parts // 2 - 1
    return [
        pl.BlockSpec(one, lambda n: (n, at, 0, 0)),
        pl.BlockSpec(one, lambda n: (blocks - 1 - n, at, 0, 0)),
    ]


def held_spec(queries):
    _, _, rows, width = queries.shape
    return pl.BlockSpec((1, 2, 2 * rows, width), lambda n: (n, 0, 0, 0))


def attend(
    step, scalars, bias, queries, states, carried=None, span_states=None, last=False, states_at=0
):
    blocks, _, rows, width = queries.shape
    pair = 2
    assert blocks % 2 == 0
    held = pltpu.HBM((blocks // 2, 2, pair * rows, width), jnp.float32)
    whole = pl.BlockSpec((blocks, 2, rows, width), lambda n: (0, states_at, 0, 0))
    operands, in_specs = [scalars], [smem()]
    if bias is not None:
        operands.append(bias)
        in_specs.append(pl.BlockSpec(bias.shape, lambda n: (0, 0)))
    operands += [queries, queries, states]
    in_specs += query_specs(queries) + [whole]
    if span_states is not None:
        operands.append(span_states)
        in_specs.append(pl.BlockSpec(span_states.shape, lambda n: (0, 0, 0)))
    if carried is not None:
        operands += [in_hbm(sums) for sums in carried]
        in_specs += [held_spec(queries)] * 2
    scratch = [pltpu.VMEM((2, pair * rows, width), queries.dtype)]
    if span_states is not None:
        scratch.append(pltpu.VMEM((2 * SPAN + rows, width), jnp.float32))
        scratch.append(pltpu.VMEM((2, SPAN // rows, rows, width), queries.dtype))
    if last:
        out_shape = jax.ShapeDtypeStruct((blocks, pair, rows, width), queries.dtype)
        out_specs = pl.BlockSpec(out_shape.shape, lambda n: (0, 0, 0, 0))
        scratch = [pltpu.VMEM((1, 2, pair * rows, width), jnp.float32)] * 2 + scratch
    else:
        out_shape, out_specs = [held, held], [held_spec(queries)] * 2
    return pl.pallas_call(
        functools.partial(attend_kernel, step=step, steerable=bias is not None, last=last),
        grid=(blocks // 2,),
        in_specs=in_specs,
        out_specs=out_specs,
        out_shape=out_shape,
        scratch_shapes=scratch,
        compiler_params=params(),
        cost_estimate=cost(
            pair * (blocks * rows) ** 2 / (1 if step == 1 else 2),
            8 * queries.size + 8 * pair * blocks * rows * width,
        ),
    )(*operands)


def unpack_kernel(scalars, out_a, out_b, attention, heads_ref):
    for n in range(GROUP):
        for group_head in range(2):
            heads_ref[2 * scalars[n] + group_head] = out_a[n, group_head]
            heads_ref[2 * scalars[GROUP + n] + group_head] = out_b[n, group_head]
    attention[...] = jnp.transpose(heads_ref[...], (1, 0, 2))


def unpack(scalars, out_a, out_b):
    blocks, pair, rows, width = out_a.shape
    heads = 2 * blocks * pair
    return pl.pallas_call(
        unpack_kernel,
        in_specs=[smem(), vmem(), vmem()],
        out_specs=vmem(),
        out_shape=jax.ShapeDtypeStruct((rows, heads, width), out_a.dtype),
        scratch_shapes=[pltpu.VMEM((heads, rows, width), out_a.dtype)],
        compiler_params=params(),
        cost_estimate=cost(0, 8 * out_a.size),
    )(scalars, out_a, out_b)


def per_device(queries, key_value, damping, span_start, steered_heads):
    rows = queries.shape[0]
    device_count = lax.axis_size("seq")
    assert WINDOW == 2 * GROUP * rows and device_count == 4 * GROUP
    assert key_value.shape[2] == 2 * GROUP and queries.shape[1] == 4 * GROUP
    assert steered_heads.shape[0] <= GROUP
    groups = [
        list(range(first, first + GROUP)) for first in range(0, device_count, GROUP)
    ]

    def exchange(blocks):
        return lax.all_to_all(
            blocks, "seq", split_axis=0, concat_axis=0, axis_index_groups=groups, tiled=True
        )

    def onward(blocks, planes=1):
        shift = planes * GROUP
        pairs = [(n, n + shift) for n in range(device_count - shift)]
        return lax.ppermute(blocks, "seq", pairs)

    def after(value, earlier):
        return lax.optimization_barrier((value, earlier))[0]

    index = lax.axis_index("seq").astype(jnp.int32).reshape(1)
    both_a, states_b, all_b, scalars = pack(
        index, span_start, steered_heads, queries, key_value
    )
    position = jnp.arange(damping.shape[0], dtype=jnp.int32)
    emphasized = (position >= span_start[0]) & (position < span_start[0] + SPAN)
    bias = jnp.where(emphasized, 0.0, jnp.log2(damping.astype(jnp.float32)))
    bias = bias.reshape(-1, rows)

    raw_b = onward(states_b)
    both_a = exchange(both_a)
    states_a = both_a[:, :2]
    back_a = onward(after(states_a, raw_b))
    all_b = lax.dynamic_update_slice(all_b, after(raw_b, states_a), (0, 0, 0, 0))
    all_b = exchange(all_b)
    held_a = attend(0, scalars, bias, after(both_a, raw_b), both_a)
    far_a = onward(after(back_a, held_a))
    length = GROUP * rows
    span_states = lax.dynamic_slice_in_dim(
        after(both_a, (back_a, held_a))[:, :2].transpose(1, 0, 2, 3).reshape(2, length, -1),
        jnp.minimum(span_start[0], length - SPAN),
        SPAN,
        1,
    )
    span_states = onward(span_states, 3)
    held_a = attend(1, scalars, bias, both_a, back_a, held_a)
    all_b = after(all_b, held_a)
    far_b = onward(all_b[:, :2])
    held_b = attend(0, scalars, None, all_b, all_b, states_at=1)
    out_a = attend(
        2, scalars, bias, both_a, far_a, after(held_a, held_b), span_states, last=True
    )
    held_b = attend(1, scalars, None, all_b, all_b, after(held_b, out_a))
    out_a = exchange(out_a)
    out_b = attend(2, scalars, None, all_b, far_b, held_b, last=True)
    out_b = exchange(out_b)
    return unpack(scalars, out_a, out_b)


def solution(mesh):
    in_specs = (
        P(("prompt", "seq"), None, None),
        P(None, ("prompt", "seq"), None, None),
        P("prompt"),
        P("prompt"),
        P(),
    )
    out_specs = P(("prompt", "seq"), None, None)
    return jax.shard_map(
        per_device, mesh=mesh, in_specs=in_specs, out_specs=out_specs, check_vma=False
    )
```

```python
import functools
import math

import jax
import jax.numpy as jnp
from jax import lax
from jax.experimental import pallas as pl
from jax.experimental.pallas import tpu as pltpu
from jax.sharding import PartitionSpec as P

WINDOW = 4096
SPAN = 512

SCORE_SCALE = 144.0 ** (-0.5)
SOFTCAP = 50.0
LOG2_E = math.log2(math.e)

GROUP = 8
CHUNK = 64
TOKEN_STEPS = 4
PAIR_FLOPS = 256
VMEM_BYTES = 48 * 1024 * 1024

FIRST_SCALAR = 32
PLANE, SPAN_FIRST, STEERED_0, STEERED_1 = range(FIRST_SCALAR, FIRST_SCALAR + 4)
SCALARS = FIRST_SCALAR + 4


def smem():
    return pl.BlockSpec(memory_space=pltpu.SMEM)


def vmem():
    return pl.BlockSpec(memory_space=pltpu.VMEM)


def in_hbm(operand):
    return pltpu.with_memory_space_constraint(operand, pltpu.HBM)


def params():
    return pltpu.CompilerParams(vmem_limit_bytes=VMEM_BYTES)


def cost(pairs, moved):
    return pl.CostEstimate(
        flops=int(pairs * PAIR_FLOPS), bytes_accessed=int(moved), transcendentals=int(2 * pairs)
    )


def pack_kernel(
    index_ref, span_ref, steered_ref, queries_ref, states_ref,
    both_a, states_b, all_b, scalars, query_heads, state_heads,
):
    key_heads = states_ref.shape[2]
    steered_count = steered_ref.shape[0]

    @pl.when(pl.program_id(0) == 0)
    def _():
        steered_keys = [lax.div(steered_ref[n], 2) for n in range(steered_count)]
        flags = []
        for head in range(key_heads):
            hit = steered_keys[0] == head
            for n in range(1, steered_count):
                hit = hit | (steered_keys[n] == head)
            flags.append(hit.astype(jnp.int32))
        total = sum(flags[1:], flags[0])
        before = jnp.int32(0)
        for head in range(key_heads):
            rank = jnp.where(flags[head] == 1, before, total + head - before)
            scalars[rank] = jnp.int32(head)
            before = before + flags[head]
        place = lax.rem(index_ref[0], GROUP)
        scalars[PLANE] = lax.div(index_ref[0], GROUP)
        scalars[SPAN_FIRST] = span_ref[0]
        own_head = scalars[place]
        for group_head in range(2):
            hit = steered_ref[0] == 2 * own_head + group_head
            for n in range(1, steered_count):
                hit = hit | (steered_ref[n] == 2 * own_head + group_head)
            scalars[STEERED_0 + group_head] = hit.astype(jnp.int32)

    for part in range(2):
        state_heads[part] = jnp.transpose(states_ref[part], (1, 0, 2))
        for n in range(GROUP):
            both_a[n, part] = state_heads[part, scalars[n]]
            state = state_heads[part, scalars[GROUP + n]]
            states_b[n, part] = state
            all_b[n, 2 + part] = state
    query_heads[...] = jnp.transpose(queries_ref[...], (1, 0, 2))
    for n in range(GROUP):
        for group_head in range(2):
            both_a[n, 2 + group_head] = query_heads[2 * scalars[n] + group_head]
            all_b[n, 4 + group_head] = query_heads[2 * scalars[GROUP + n] + group_head]


def pack(index, span_start, steered_heads, queries, states):
    rows, heads, width = queries.shape
    key_heads = states.shape[2]
    some = rows // TOKEN_STEPS


    def sent(parts):
        shape = pltpu.HBM((GROUP, parts, rows, width), queries.dtype)
        return shape, pl.BlockSpec((GROUP, parts, some, width), lambda n: (0, 0, n, 0))

    shapes, specs = zip(sent(4), sent(2), sent(6))
    return pl.pallas_call(
        pack_kernel,
        grid=(TOKEN_STEPS,),
        in_specs=[smem()] * 3
        + [
            pl.BlockSpec((some, heads, width), lambda n: (n, 0, 0)),
            pl.BlockSpec((2, some, key_heads, width), lambda n: (0, n, 0, 0)),
        ],
        out_specs=list(specs) + [smem()],
        out_shape=list(shapes) + [jax.ShapeDtypeStruct((SCALARS,), jnp.int32)],
        scratch_shapes=[
            pltpu.VMEM((heads, some, width), queries.dtype),
            pltpu.VMEM((2, key_heads, some, width), queries.dtype),
        ],
        compiler_params=params(),
        cost_estimate=cost(0, 4 * (queries.size + states.size)),
    )(index, span_start, steered_heads, in_hbm(queries), in_hbm(states))


def raw_scores(query, key):
    return lax.dot_general(
        query, key, (((1,), (1,)), ((), ())), preferred_element_type=jnp.float32
    )


def weights(raw_score, bias, visible):
    score = jnp.tanh(raw_score * (SCORE_SCALE / SOFTCAP)) * (SOFTCAP * LOG2_E)
    weight = jnp.exp2(score if bias is None else score + bias)
    return weight if visible is None else jnp.where(visible, weight, 0.0)


def lane_sums(weight, lanes):
    sums = weight[:, :lanes]
    for first in range(lanes, weight.shape[1], lanes):
        sums = sums + weight[:, first : first + lanes]
    return sums


def attend_kernel(*refs, step, steerable, last):
    refs = list(refs)
    scalars = refs.pop(0)
    bias_ref = refs.pop(0) if steerable else None
    low_ref, high_ref, states_ref = refs.pop(0), refs.pop(0), refs.pop(0)
    span_ref = refs.pop(0) if steerable and last else None
    if step:
        old_weighted, old_sums = refs.pop(0), refs.pop(0)
    if last:
        out_ref = refs.pop(0)
    weighted_ref, sums_ref, query_ref = refs[:3]
    around_ref, gathered_ref = refs[3:] if steerable and last else (None, None)
    low = pl.program_id(0)
    blocks, _, rows, width = states_ref.shape
    high = blocks - 1 - low
    plane = scalars[PLANE]
    first_block = (plane - step) * blocks
    query_ref[0] = low_ref[0].reshape(2 * rows, width)
    query_ref[1] = high_ref[0].reshape(2 * rows, width)
    if step:
        weighted_ref[...] = old_weighted[...]
        sums_ref[...] = old_sums[...]
    else:
        weighted_ref[...] = jnp.zeros(weighted_ref.shape, jnp.float32)
        sums_ref[...] = jnp.zeros(sums_ref.shape, jnp.float32)
    flags = [scalars[STEERED_0 + n] for n in range(2)]
    flag_values = [flag.astype(jnp.float32) for flag in flags]

    def states(part, key_block, count):
        if count == 1:
            return states_ref[key_block, part]
        return states_ref[pl.ds(key_block, count), part].reshape(count * rows, width)

    def bias(key_block, count):
        if not steerable:
            return None
        parts = [bias_ref[pl.ds(first_block + key_block + n, 1), :] for n in range(count)]
        row = parts[0] if count == 1 else jnp.concatenate(parts, axis=1)
        return [row * value for value in flag_values]

    def add(tiles):
        def of_span(key_block):
            return isinstance(key_block, int) and key_block < 0

        def part_of(part, key_block, count):
            if of_span(key_block):
                return gathered_ref[part, ~key_block]
            return states(part, key_block, count)

        def score(tile):
            which, key_block, count, _ = tile
            return raw_scores(query_ref[which], part_of(0, key_block, count))

        ahead = score(tiles[0])
        for n, (which, key_block, count, visible) in enumerate(tiles):
            raw_score = ahead
            if n + 1 < len(tiles):
                ahead = score(tiles[n + 1])
            added = None if of_span(key_block) else bias(key_block, count)
            chunk = CHUNK // count
            rounded = []
            for first in range(0, 2 * rows, chunk):
                head, row = first // rows, first % rows
                columns = slice(0, count * rows)
                if visible is in_order:
                    columns = slice(0, -(-(row + chunk) // width) * width)
                    if step:
                        columns = slice(row // width * width, rows)
                weight = weights(
                    raw_score[first : first + chunk, columns],
                    None if added is None else added[head][:, columns],
                    None if visible is None else visible(head, row, chunk)[:, columns],
                )
                some = pl.ds(first, chunk)
                sums_ref[0, which, some, :] += lane_sums(weight, width)
                weight = weight.astype(jnp.bfloat16)
                sides = [
                    jnp.zeros((chunk, size), jnp.bfloat16)
                    for size in (columns.start, count * rows - columns.stop)
                ]
                parts = [part for part in (sides[0], weight, sides[1]) if part.shape[1]]
                rounded.append(parts[0] if len(parts) == 1 else jnp.concatenate(parts, axis=1))
            weighted_ref[0, which] += jnp.dot(
                jnp.concatenate(rounded, axis=0),
                part_of(1, key_block, count),
                preferred_element_type=jnp.float32,
            )

    def gather_span():
        start = scalars[SPAN_FIRST] - first_block * rows
        pad = SPAN // rows
        for part in range(2):
            before = span_ref[part].astype(jnp.float32)

            @pl.when(start < 0)
            def _():
                around_ref[:SPAN, :] = before
                for n in range(2):
                    around_ref[SPAN + n * rows : SPAN + (n + 1) * rows, :] = states_ref[
                        n, part
                    ].astype(jnp.float32)

            block = jnp.clip(lax.div(jnp.maximum(start, 0), rows), 0, blocks - pad - 1)

            @pl.when(start >= 0)
            def _():
                for n in range(pad + 1):
                    around_ref[n * rows : (n + 1) * rows, :] = states_ref[
                        block + n, part
                    ].astype(jnp.float32)
                around_ref[(pad + 1) * rows :, :] = jnp.zeros((SPAN, width), jnp.float32)

            offset = jnp.where(start < 0, jnp.maximum(start + SPAN, 0), start - block * rows)
            for n in range(pad):
                gathered_ref[part, n] = around_ref[pl.ds(offset + n * rows, rows), :].astype(
                    jnp.bfloat16
                )

    def ranks(row, count):
        shape = (count, rows)
        return (
            row
            + lax.broadcasted_iota(jnp.int32, shape, 0)
            - lax.broadcasted_iota(jnp.int32, shape, 1)
        )

    def in_order(head, row, count):
        return ranks(row, count) >= 0 if step == 0 else ranks(row, count) < 0

    def span_tiles():
        tiles = []
        for which, block in ((0, low), (1, high)):
            for n in range(SPAN // rows):
                nearest = scalars[SPAN_FIRST] + n * rows + WINDOW - (plane * blocks + block) * rows
                least = [jnp.where(flag == 1, nearest, 2 * rows) for flag in flags]

                def visible(head, row, count, least=least):
                    return ranks(row, count) >= least[head]

                tiles.append((which, ~n, 1, visible))
        return tiles

    def compute():
        if step == 1:
            add([(which, n, 2, None) for which in range(2) for n in range(0, blocks, 2)])
            return
        tiles = []
        for n in range(blocks - 1):
            if step == 0:
                is_low = n < low
                tiles.append((jnp.where(is_low, 0, 1), jnp.where(is_low, n, n - low), 1, None))
            else:
                is_high = n < low
                tiles.append(
                    (jnp.where(is_high, 1, 0), jnp.where(is_high, high + 1 + n, n + 1), 1, None)
                )

        for which, block in ((0, low), (1, high)):
            tiles.append((which, block, 1, in_order))
        if not (steerable and last):
            add(tiles)
            return
        wanted = flags[0] + flags[1] > 0
        wanted = wanted & (scalars[SPAN_FIRST] < (first_block + blocks) * rows)
        pl.when(wanted & (low == 0))(gather_span)
        pl.when(wanted)(lambda: add(tiles + span_tiles()))
        pl.when(jnp.logical_not(wanted))(lambda: add(tiles))

    if step:
        pl.when(plane >= step)(compute)
    else:
        compute()
    if last:
        write_result(out_ref, weighted_ref, sums_ref, low, high)


def write_result(out_ref, weighted_ref, sums_ref, low, high):
    for which, block in ((0, low), (1, high)):
        total = jnp.sum(sums_ref[0, which], axis=-1, keepdims=True)
        result = (weighted_ref[0, which] / total).astype(out_ref.dtype)
        out_ref[block] = result.reshape(out_ref.shape[1:])


def query_specs(queries):
    blocks, parts, rows, width = queries.shape
    one, at = (1, 2, rows, width), parts // 2 - 1
    return [
        pl.BlockSpec(one, lambda n: (n, at, 0, 0)),
        pl.BlockSpec(one, lambda n: (blocks - 1 - n, at, 0, 0)),
    ]


def held_spec(queries):
    _, _, rows, width = queries.shape
    return pl.BlockSpec((1, 2, 2 * rows, width), lambda n: (n, 0, 0, 0))


def attend(
    step, scalars, bias, queries, states, carried=None, span_states=None, last=False, states_at=0
):
    blocks, _, rows, width = queries.shape
    pair = 2
    assert blocks % 2 == 0
    held = pltpu.HBM((blocks // 2, 2, pair * rows, width), jnp.float32)
    whole = pl.BlockSpec((blocks, 2, rows, width), lambda n: (0, states_at, 0, 0))
    operands, in_specs = [scalars], [smem()]
    if bias is not None:
        operands.append(bias)
        in_specs.append(pl.BlockSpec(bias.shape, lambda n: (0, 0)))
    operands += [queries, queries, states]
    in_specs += query_specs(queries) + [whole]
    if span_states is not None:
        operands.append(span_states)
        in_specs.append(pl.BlockSpec(span_states.shape, lambda n: (0, 0, 0)))
    if carried is not None:
        operands += [in_hbm(sums) for sums in carried]
        in_specs += [held_spec(queries)] * 2
    scratch = [pltpu.VMEM((2, pair * rows, width), queries.dtype)]
    if span_states is not None:
        scratch.append(pltpu.VMEM((2 * SPAN + rows, width), jnp.float32))
        scratch.append(pltpu.VMEM((2, SPAN // rows, rows, width), queries.dtype))
    if last:
        out_shape = jax.ShapeDtypeStruct((blocks, pair, rows, width), queries.dtype)
        out_specs = pl.BlockSpec(out_shape.shape, lambda n: (0, 0, 0, 0))
        scratch = [pltpu.VMEM((1, 2, pair * rows, width), jnp.float32)] * 2 + scratch
    else:
        out_shape, out_specs = [held, held], [held_spec(queries)] * 2
    return pl.pallas_call(
        functools.partial(attend_kernel, step=step, steerable=bias is not None, last=last),
        grid=(blocks // 2,),
        in_specs=in_specs,
        out_specs=out_specs,
        out_shape=out_shape,
        scratch_shapes=scratch,
        compiler_params=params(),
        cost_estimate=cost(
            pair * (blocks * rows) ** 2 * (16 if step == 1 and bias is not None else 1) / 2,
            8 * queries.size + 8 * pair * blocks * rows * width,
        ),
    )(*operands)


def unpack_kernel(scalars, out_a, out_b, attention, heads_ref):
    for n in range(GROUP):
        for group_head in range(2):
            heads_ref[2 * scalars[n] + group_head] = out_a[n, group_head]
            heads_ref[2 * scalars[GROUP + n] + group_head] = out_b[n, group_head]
    attention[...] = jnp.transpose(heads_ref[...], (1, 0, 2))


def unpack(scalars, out_a, out_b):
    blocks, pair, rows, width = out_a.shape
    heads = 2 * blocks * pair
    return pl.pallas_call(
        unpack_kernel,
        in_specs=[smem(), vmem(), vmem()],
        out_specs=vmem(),
        out_shape=jax.ShapeDtypeStruct((rows, heads, width), out_a.dtype),
        scratch_shapes=[pltpu.VMEM((heads, rows, width), out_a.dtype)],
        compiler_params=params(),
        cost_estimate=cost(0, 8 * out_a.size),
    )(scalars, out_a, out_b)


def per_device(queries, key_value, damping, span_start, steered_heads):
    rows = queries.shape[0]
    device_count = lax.axis_size("seq")
    assert WINDOW == 2 * GROUP * rows and device_count == 4 * GROUP
    assert key_value.shape[2] == 2 * GROUP and queries.shape[1] == 4 * GROUP
    assert steered_heads.shape[0] <= GROUP
    groups = [
        list(range(first, first + GROUP)) for first in range(0, device_count, GROUP)
    ]

    def exchange(blocks):
        return lax.all_to_all(
            blocks, "seq", split_axis=0, concat_axis=0, axis_index_groups=groups, tiled=True
        )

    def onward(blocks, planes=1):
        shift = planes * GROUP
        pairs = [(n, n + shift) for n in range(device_count - shift)]
        return lax.ppermute(blocks, "seq", pairs)

    def after(value, earlier):
        return lax.optimization_barrier((value, earlier))[0]

    index = lax.axis_index("seq").astype(jnp.int32).reshape(1)
    both_a, states_b, all_b, scalars = pack(
        index, span_start, steered_heads, queries, key_value
    )
    position = jnp.arange(damping.shape[0], dtype=jnp.int32)
    emphasized = (position >= span_start[0]) & (position < span_start[0] + SPAN)
    bias = jnp.where(emphasized, 0.0, jnp.log2(damping.astype(jnp.float32)))
    bias = bias.reshape(-1, rows)

    raw_b = onward(states_b)
    both_a = exchange(both_a)
    states_a = both_a[:, :2]
    back_a = onward(after(states_a, raw_b))
    held_a = attend(0, scalars, bias, after(both_a, raw_b), both_a)
    all_b = lax.dynamic_update_slice(all_b, after(raw_b, held_a), (0, 0, 0, 0))
    all_b = exchange(all_b)
    far_a = onward(after(back_a, held_a))
    length = GROUP * rows
    span_states = lax.dynamic_slice_in_dim(
        after(both_a, (back_a, held_a))[:, :2].transpose(1, 0, 2, 3).reshape(2, length, -1),
        jnp.minimum(span_start[0], length - SPAN),
        SPAN,
        1,
    )
    span_states = onward(span_states, 3)
    held_a = attend(1, scalars, bias, both_a, back_a, held_a)
    all_b = after(all_b, held_a)
    far_b = onward(all_b[:, :2])
    held_b = attend(0, scalars, None, all_b, all_b, states_at=1)
    out_a = attend(
        2, scalars, bias, both_a, far_a, after(held_a, held_b), span_states, last=True
    )
    held_b = attend(1, scalars, None, all_b, all_b, after(held_b, out_a))
    out_a = exchange(out_a)
    out_b = attend(2, scalars, None, all_b, far_b, held_b, last=True)
    out_b = exchange(out_b)
    return unpack(scalars, out_a, out_b)


def solution(mesh):
    in_specs = (
        P(("prompt", "seq"), None, None),
        P(None, ("prompt", "seq"), None, None),
        P("prompt"),
        P("prompt"),
        P(),
    )
    out_specs = P(("prompt", "seq"), None, None)
    return jax.shard_map(
        per_device, mesh=mesh, in_specs=in_specs, out_specs=out_specs, check_vma=False
    )
```

```python
import functools
import math

import jax
import jax.numpy as jnp
from jax import lax
from jax.experimental import pallas as pl
from jax.experimental.pallas import tpu as pltpu
from jax.sharding import PartitionSpec as P

WINDOW = 4096
SPAN = 512

SCORE_SCALE = 144.0 ** (-0.5)
SOFTCAP = 50.0
LOG2_E = math.log2(math.e)

GROUP = 8
CHUNK = 64
TOKEN_STEPS = 4
PAIR_FLOPS = 256
VMEM_BYTES = 48 * 1024 * 1024

FIRST_SCALAR = 32
PLANE, SPAN_FIRST, STEERED_0, STEERED_1 = range(FIRST_SCALAR, FIRST_SCALAR + 4)
SCALARS = FIRST_SCALAR + 4


def smem():
    return pl.BlockSpec(memory_space=pltpu.SMEM)


def vmem():
    return pl.BlockSpec(memory_space=pltpu.VMEM)


def in_hbm(operand):
    return pltpu.with_memory_space_constraint(operand, pltpu.HBM)


def params():
    return pltpu.CompilerParams(vmem_limit_bytes=VMEM_BYTES)


def cost(pairs, moved):
    return pl.CostEstimate(
        flops=int(pairs * PAIR_FLOPS), bytes_accessed=int(moved), transcendentals=int(2 * pairs)
    )


def pack_kernel(
    index_ref, span_ref, steered_ref, queries_ref, states_ref,
    both_a, states_b, all_b, scalars, query_heads, state_heads,
):
    key_heads = states_ref.shape[2]
    steered_count = steered_ref.shape[0]

    @pl.when(pl.program_id(0) == 0)
    def _():
        steered_keys = [lax.div(steered_ref[n], 2) for n in range(steered_count)]
        flags = []
        for head in range(key_heads):
            hit = steered_keys[0] == head
            for n in range(1, steered_count):
                hit = hit | (steered_keys[n] == head)
            flags.append(hit.astype(jnp.int32))
        total = sum(flags[1:], flags[0])
        before = jnp.int32(0)
        for head in range(key_heads):
            rank = jnp.where(flags[head] == 1, before, total + head - before)
            scalars[rank] = jnp.int32(head)
            before = before + flags[head]
        place = lax.rem(index_ref[0], GROUP)
        scalars[PLANE] = lax.div(index_ref[0], GROUP)
        scalars[SPAN_FIRST] = span_ref[0]
        own_head = scalars[place]
        for group_head in range(2):
            hit = steered_ref[0] == 2 * own_head + group_head
            for n in range(1, steered_count):
                hit = hit | (steered_ref[n] == 2 * own_head + group_head)
            scalars[STEERED_0 + group_head] = hit.astype(jnp.int32)

    for part in range(2):
        state_heads[part] = jnp.transpose(states_ref[part], (1, 0, 2))
        for n in range(GROUP):
            both_a[n, part] = state_heads[part, scalars[n]]
            state = state_heads[part, scalars[GROUP + n]]
            states_b[n, part] = state
            all_b[n, 2 + part] = state
    query_heads[...] = jnp.transpose(queries_ref[...], (1, 0, 2))
    for n in range(GROUP):
        for group_head in range(2):
            both_a[n, 2 + group_head] = query_heads[2 * scalars[n] + group_head]
            all_b[n, 4 + group_head] = query_heads[2 * scalars[GROUP + n] + group_head]


def pack(index, span_start, steered_heads, queries, states):
    rows, heads, width = queries.shape
    key_heads = states.shape[2]
    some = rows // TOKEN_STEPS


    def sent(parts):
        shape = pltpu.HBM((GROUP, parts, rows, width), queries.dtype)
        return shape, pl.BlockSpec((GROUP, parts, some, width), lambda n: (0, 0, n, 0))

    shapes, specs = zip(sent(4), sent(2), sent(6))
    return pl.pallas_call(
        pack_kernel,
        grid=(TOKEN_STEPS,),
        in_specs=[smem()] * 3
        + [
            pl.BlockSpec((some, heads, width), lambda n: (n, 0, 0)),
            pl.BlockSpec((2, some, key_heads, width), lambda n: (0, n, 0, 0)),
        ],
        out_specs=list(specs) + [smem()],
        out_shape=list(shapes) + [jax.ShapeDtypeStruct((SCALARS,), jnp.int32)],
        scratch_shapes=[
            pltpu.VMEM((heads, some, width), queries.dtype),
            pltpu.VMEM((2, key_heads, some, width), queries.dtype),
        ],
        compiler_params=params(),
        cost_estimate=cost(0, 4 * (queries.size + states.size)),
    )(index, span_start, steered_heads, in_hbm(queries), in_hbm(states))


def raw_scores(query, key):
    return lax.dot_general(
        query, key, (((1,), (1,)), ((), ())), preferred_element_type=jnp.float32
    )


def weights(raw_score, bias, visible):
    score = jnp.tanh(raw_score * (SCORE_SCALE / SOFTCAP)) * (SOFTCAP * LOG2_E)
    weight = jnp.exp2(score if bias is None else score + bias)
    return weight if visible is None else jnp.where(visible, weight, 0.0)


def lane_sums(weight, lanes):
    sums = weight[:, :lanes]
    for first in range(lanes, weight.shape[1], lanes):
        sums = sums + weight[:, first : first + lanes]
    return sums


def attend_kernel(*refs, step, steerable, last):
    refs = list(refs)
    scalars = refs.pop(0)
    bias_ref = refs.pop(0) if steerable else None
    low_ref, high_ref, states_ref = refs.pop(0), refs.pop(0), refs.pop(0)
    span_ref = refs.pop(0) if steerable and last else None
    if step:
        old_weighted, old_sums = refs.pop(0), refs.pop(0)
    if last:
        out_ref = refs.pop(0)
    weighted_ref, sums_ref, query_ref = refs[:3]
    around_ref, gathered_ref = refs[3:] if steerable and last else (None, None)
    low = pl.program_id(0)
    blocks, _, rows, width = states_ref.shape
    high = blocks - 1 - low
    plane = scalars[PLANE]
    first_block = (plane - step) * blocks
    query_ref[0] = low_ref[0].reshape(2 * rows, width)
    query_ref[1] = high_ref[0].reshape(2 * rows, width)
    if step:
        weighted_ref[...] = old_weighted[...]
        sums_ref[...] = old_sums[...]
    else:
        weighted_ref[...] = jnp.zeros(weighted_ref.shape, jnp.float32)
        sums_ref[...] = jnp.zeros(sums_ref.shape, jnp.float32)
    flags = [scalars[STEERED_0 + n] for n in range(2)]
    flag_values = [flag.astype(jnp.float32) for flag in flags]

    def states(part, key_block, count):
        if count == 1:
            return states_ref[key_block, part]
        return states_ref[pl.ds(key_block, count), part].reshape(count * rows, width)

    def bias(key_block, count):
        if not steerable:
            return None
        parts = [bias_ref[pl.ds(first_block + key_block + n, 1), :] for n in range(count)]
        row = parts[0] if count == 1 else jnp.concatenate(parts, axis=1)
        return [row * value for value in flag_values]

    def add(tiles):
        def of_span(key_block):
            return isinstance(key_block, int) and key_block < 0

        def part_of(part, key_block, count):
            if of_span(key_block):
                return gathered_ref[part, ~key_block]
            return states(part, key_block, count)

        def score(tile):
            which, key_block, count, _ = tile
            return raw_scores(query_ref[which], part_of(0, key_block, count))

        ahead = score(tiles[0])
        for n, (which, key_block, count, visible) in enumerate(tiles):
            raw_score = ahead
            if n + 1 < len(tiles):
                ahead = score(tiles[n + 1])
            added = None if of_span(key_block) else bias(key_block, count)
            chunk = CHUNK // count
            rounded = []
            for first in range(0, 2 * rows, chunk):
                head, row = first // rows, first % rows
                columns = slice(0, count * rows)
                if visible is in_order:
                    columns = slice(0, -(-(row + chunk) // width) * width)
                    if step:
                        columns = slice(row // width * width, rows)
                weight = weights(
                    raw_score[first : first + chunk, columns],
                    None if added is None else added[head][:, columns],
                    None if visible is None else visible(head, row, chunk)[:, columns],
                )
                some = pl.ds(first, chunk)
                sums_ref[0, which, some, :] += lane_sums(weight, width)
                weight = weight.astype(jnp.bfloat16)
                sides = [
                    jnp.zeros((chunk, size), jnp.bfloat16)
                    for size in (columns.start, count * rows - columns.stop)
                ]
                parts = [part for part in (sides[0], weight, sides[1]) if part.shape[1]]
                rounded.append(parts[0] if len(parts) == 1 else jnp.concatenate(parts, axis=1))
            weighted_ref[0, which] += jnp.dot(
                jnp.concatenate(rounded, axis=0),
                part_of(1, key_block, count),
                preferred_element_type=jnp.float32,
            )

    def gather_span():
        start = scalars[SPAN_FIRST] - first_block * rows
        pad = SPAN // rows
        for part in range(2):
            before = span_ref[part].astype(jnp.float32)

            @pl.when(start < 0)
            def _():
                around_ref[:SPAN, :] = before
                for n in range(2):
                    around_ref[SPAN + n * rows : SPAN + (n + 1) * rows, :] = states_ref[
                        n, part
                    ].astype(jnp.float32)

            block = jnp.clip(lax.div(jnp.maximum(start, 0), rows), 0, blocks - pad - 1)

            @pl.when(start >= 0)
            def _():
                for n in range(pad + 1):
                    around_ref[n * rows : (n + 1) * rows, :] = states_ref[
                        block + n, part
                    ].astype(jnp.float32)
                around_ref[(pad + 1) * rows :, :] = jnp.zeros((SPAN, width), jnp.float32)

            offset = jnp.where(start < 0, jnp.maximum(start + SPAN, 0), start - block * rows)
            for n in range(pad):
                gathered_ref[part, n] = around_ref[pl.ds(offset + n * rows, rows), :].astype(
                    jnp.bfloat16
                )

    def ranks(row, count):
        shape = (count, rows)
        return (
            row
            + lax.broadcasted_iota(jnp.int32, shape, 0)
            - lax.broadcasted_iota(jnp.int32, shape, 1)
        )

    def in_order(head, row, count):
        return ranks(row, count) >= 0 if step == 0 else ranks(row, count) < 0

    def span_tiles():
        tiles = []
        for which, block in ((0, low), (1, high)):
            for n in range(SPAN // rows):
                nearest = scalars[SPAN_FIRST] + n * rows + WINDOW - (plane * blocks + block) * rows
                least = [jnp.where(flag == 1, nearest, 2 * rows) for flag in flags]

                def visible(head, row, count, least=least):
                    return ranks(row, count) >= least[head]

                tiles.append((which, ~n, 1, visible))
        return tiles

    def compute():
        if step == 1:
            add([(which, n, 2, None) for which in range(2) for n in range(0, blocks, 2)])
            return
        tiles = []
        for n in range(blocks - 1):
            if step == 0:
                is_low = n < low
                tiles.append((jnp.where(is_low, 0, 1), jnp.where(is_low, n, n - low), 1, None))
            else:
                is_high = n < low
                tiles.append(
                    (jnp.where(is_high, 1, 0), jnp.where(is_high, high + 1 + n, n + 1), 1, None)
                )

        for which, block in ((0, low), (1, high)):
            tiles.append((which, block, 1, in_order))
        if not (steerable and last):
            add(tiles)
            return
        wanted = flags[0] + flags[1] > 0
        wanted = wanted & (scalars[SPAN_FIRST] < (first_block + blocks) * rows)
        pl.when(wanted & (low == 0))(gather_span)
        pl.when(wanted)(lambda: add(tiles + span_tiles()))
        pl.when(jnp.logical_not(wanted))(lambda: add(tiles))

    if step:
        pl.when(plane >= step)(compute)
    else:
        compute()
    if last:
        write_result(out_ref, weighted_ref, sums_ref, low, high)


def write_result(out_ref, weighted_ref, sums_ref, low, high):
    for which, block in ((0, low), (1, high)):
        total = jnp.sum(sums_ref[0, which], axis=-1, keepdims=True)
        result = (weighted_ref[0, which] / total).astype(out_ref.dtype)
        out_ref[block] = result.reshape(out_ref.shape[1:])


def query_specs(queries):
    blocks, parts, rows, width = queries.shape
    one, at = (1, 2, rows, width), parts // 2 - 1
    return [
        pl.BlockSpec(one, lambda n: (n, at, 0, 0)),
        pl.BlockSpec(one, lambda n: (blocks - 1 - n, at, 0, 0)),
    ]


def held_spec(queries):
    _, _, rows, width = queries.shape
    return pl.BlockSpec((1, 2, 2 * rows, width), lambda n: (n, 0, 0, 0))


def attend(
    step, scalars, bias, queries, states, carried=None, span_states=None, last=False, states_at=0
):
    blocks, _, rows, width = queries.shape
    pair = 2
    assert blocks % 2 == 0
    held = pltpu.HBM((blocks // 2, 2, pair * rows, width), jnp.float32)
    whole = pl.BlockSpec((blocks, 2, rows, width), lambda n: (0, states_at, 0, 0))
    operands, in_specs = [scalars], [smem()]
    if bias is not None:
        operands.append(bias)
        in_specs.append(pl.BlockSpec(bias.shape, lambda n: (0, 0)))
    operands += [queries, queries, states]
    in_specs += query_specs(queries) + [whole]
    if span_states is not None:
        operands.append(span_states)
        in_specs.append(pl.BlockSpec(span_states.shape, lambda n: (0, 0, 0)))
    if carried is not None:
        operands += [in_hbm(sums) for sums in carried]
        in_specs += [held_spec(queries)] * 2
    scratch = [pltpu.VMEM((2, pair * rows, width), queries.dtype)]
    if span_states is not None:
        scratch.append(pltpu.VMEM((2 * SPAN + rows, width), jnp.float32))
        scratch.append(pltpu.VMEM((2, SPAN // rows, rows, width), queries.dtype))
    if last:
        out_shape = jax.ShapeDtypeStruct((blocks, pair, rows, width), queries.dtype)
        out_specs = pl.BlockSpec(out_shape.shape, lambda n: (0, 0, 0, 0))
        scratch = [pltpu.VMEM((1, 2, pair * rows, width), jnp.float32)] * 2 + scratch
    else:
        out_shape, out_specs = [held, held], [held_spec(queries)] * 2
    return pl.pallas_call(
        functools.partial(attend_kernel, step=step, steerable=bias is not None, last=last),
        grid=(blocks // 2,),
        in_specs=in_specs,
        out_specs=out_specs,
        out_shape=out_shape,
        scratch_shapes=scratch,
        compiler_params=params(),
        cost_estimate=cost(
            pair * (blocks * rows) ** 2 * (16 if step == 1 and bias is not None else 1) / 2,
            8 * queries.size + 8 * pair * blocks * rows * width,
        ),
    )(*operands)


def unpack_kernel(scalars, out_a, out_b, attention, heads_ref):
    for n in range(GROUP):
        for group_head in range(2):
            heads_ref[2 * scalars[n] + group_head] = out_a[n, group_head]
            heads_ref[2 * scalars[GROUP + n] + group_head] = out_b[n, group_head]
    attention[...] = jnp.transpose(heads_ref[...], (1, 0, 2))


def unpack(scalars, out_a, out_b):
    blocks, pair, rows, width = out_a.shape
    heads = 2 * blocks * pair
    return pl.pallas_call(
        unpack_kernel,
        in_specs=[smem(), vmem(), vmem()],
        out_specs=vmem(),
        out_shape=jax.ShapeDtypeStruct((rows, heads, width), out_a.dtype),
        scratch_shapes=[pltpu.VMEM((heads, rows, width), out_a.dtype)],
        compiler_params=params(),
        cost_estimate=cost(0, 8 * out_a.size),
    )(scalars, out_a, out_b)


def per_device(queries, key_value, damping, span_start, steered_heads):
    rows = queries.shape[0]
    device_count = lax.axis_size("seq")
    assert WINDOW == 2 * GROUP * rows and device_count == 4 * GROUP
    assert key_value.shape[2] == 2 * GROUP and queries.shape[1] == 4 * GROUP
    assert steered_heads.shape[0] <= GROUP
    groups = [
        list(range(first, first + GROUP)) for first in range(0, device_count, GROUP)
    ]

    def exchange(blocks):
        return lax.all_to_all(
            blocks, "seq", split_axis=0, concat_axis=0, axis_index_groups=groups, tiled=True
        )

    def onward(blocks, planes=1):
        shift = planes * GROUP
        pairs = [(n, n + shift) for n in range(device_count - shift)]
        return lax.ppermute(blocks, "seq", pairs)

    def after(value, earlier):
        return lax.optimization_barrier((value, earlier))[0]

    index = lax.axis_index("seq").astype(jnp.int32).reshape(1)
    both_a, states_b, all_b, scalars = pack(
        index, span_start, steered_heads, queries, key_value
    )
    position = jnp.arange(damping.shape[0], dtype=jnp.int32)
    emphasized = (position >= span_start[0]) & (position < span_start[0] + SPAN)
    bias = jnp.where(emphasized, 0.0, jnp.log2(damping.astype(jnp.float32)))
    bias = bias.reshape(-1, rows)

    raw_b = onward(states_b)
    both_a = exchange(both_a)
    states_a = both_a[:, :2]
    back_a = onward(after(states_a, raw_b))
    held_a = attend(0, scalars, bias, after(both_a, raw_b), both_a)
    all_b = lax.dynamic_update_slice(all_b, after(raw_b, states_a), (0, 0, 0, 0))
    all_b = exchange(all_b)
    far_a = onward(after(back_a, held_a))
    length = GROUP * rows
    span_states = lax.dynamic_slice_in_dim(
        after(both_a, (back_a, held_a))[:, :2].transpose(1, 0, 2, 3).reshape(2, length, -1),
        jnp.minimum(span_start[0], length - SPAN),
        SPAN,
        1,
    )
    span_states = onward(span_states, 3)
    held_a = attend(1, scalars, bias, both_a, back_a, held_a)
    all_b = after(all_b, held_a)
    far_b = onward(all_b[:, :2])
    held_b = attend(0, scalars, None, all_b, all_b, states_at=1)
    out_a = attend(
        2, scalars, bias, both_a, far_a, after(held_a, held_b), span_states, last=True
    )
    held_b = attend(1, scalars, None, all_b, all_b, after(held_b, out_a))
    out_a = exchange(out_a)
    out_b = attend(2, scalars, None, all_b, far_b, held_b, last=True)
    out_b = exchange(out_b)
    return unpack(scalars, out_a, out_b)


def solution(mesh):
    in_specs = (
        P(("prompt", "seq"), None, None),
        P(None, ("prompt", "seq"), None, None),
        P("prompt"),
        P("prompt"),
        P(),
    )
    out_specs = P(("prompt", "seq"), None, None)
    return jax.shard_map(
        per_device, mesh=mesh, in_specs=in_specs, out_specs=out_specs, check_vma=False
    )
```

```python
import functools
import math

import jax
import jax.numpy as jnp
from jax import lax
from jax.experimental import pallas as pl
from jax.experimental.pallas import tpu as pltpu
from jax.sharding import PartitionSpec as P

WINDOW = 4096
SPAN = 512

SCORE_SCALE = 144.0 ** (-0.5)
SOFTCAP = 50.0
LOG2_E = math.log2(math.e)

GROUP = 8
CHUNK = 64
TOKEN_STEPS = 4
PAIR_FLOPS = 256
VMEM_BYTES = 48 * 1024 * 1024

FIRST_SCALAR = 32
PLANE, SPAN_FIRST, STEERED_0, STEERED_1 = range(FIRST_SCALAR, FIRST_SCALAR + 4)
SCALARS = FIRST_SCALAR + 4


def smem():
    return pl.BlockSpec(memory_space=pltpu.SMEM)


def vmem():
    return pl.BlockSpec(memory_space=pltpu.VMEM)


def in_hbm(operand):
    return pltpu.with_memory_space_constraint(operand, pltpu.HBM)


def params():
    return pltpu.CompilerParams(vmem_limit_bytes=VMEM_BYTES)


def cost(pairs, moved):
    return pl.CostEstimate(
        flops=int(pairs * PAIR_FLOPS), bytes_accessed=int(moved), transcendentals=int(2 * pairs)
    )


def pack_kernel(
    index_ref, span_ref, steered_ref, queries_ref, states_ref,
    both_a, states_b, all_b, scalars, query_heads, state_heads,
):
    key_heads = states_ref.shape[2]
    steered_count = steered_ref.shape[0]

    @pl.when(pl.program_id(0) == 0)
    def _():
        steered_keys = [lax.div(steered_ref[n], 2) for n in range(steered_count)]
        flags = []
        for head in range(key_heads):
            hit = steered_keys[0] == head
            for n in range(1, steered_count):
                hit = hit | (steered_keys[n] == head)
            flags.append(hit.astype(jnp.int32))
        total = sum(flags[1:], flags[0])
        before = jnp.int32(0)
        for head in range(key_heads):
            rank = jnp.where(flags[head] == 1, before, total + head - before)
            scalars[rank] = jnp.int32(head)
            before = before + flags[head]
        place = lax.rem(index_ref[0], GROUP)
        scalars[PLANE] = lax.div(index_ref[0], GROUP)
        scalars[SPAN_FIRST] = span_ref[0]
        own_head = scalars[place]
        for group_head in range(2):
            hit = steered_ref[0] == 2 * own_head + group_head
            for n in range(1, steered_count):
                hit = hit | (steered_ref[n] == 2 * own_head + group_head)
            scalars[STEERED_0 + group_head] = hit.astype(jnp.int32)

    for part in range(2):
        state_heads[part] = jnp.transpose(states_ref[part], (1, 0, 2))
        for n in range(GROUP):
            both_a[n, part] = state_heads[part, scalars[n]]
            state = state_heads[part, scalars[GROUP + n]]
            states_b[n, part] = state
            all_b[n, 2 + part] = state
    query_heads[...] = jnp.transpose(queries_ref[...], (1, 0, 2))
    for n in range(GROUP):
        for group_head in range(2):
            both_a[n, 2 + group_head] = query_heads[2 * scalars[n] + group_head]
            all_b[n, 4 + group_head] = query_heads[2 * scalars[GROUP + n] + group_head]


def pack(index, span_start, steered_heads, queries, states):
    rows, heads, width = queries.shape
    key_heads = states.shape[2]
    some = rows // TOKEN_STEPS


    def sent(parts):
        shape = pltpu.HBM((GROUP, parts, rows, width), queries.dtype)
        return shape, pl.BlockSpec((GROUP, parts, some, width), lambda n: (0, 0, n, 0))

    shapes, specs = zip(sent(4), sent(2), sent(6))
    return pl.pallas_call(
        pack_kernel,
        grid=(TOKEN_STEPS,),
        in_specs=[smem()] * 3
        + [
            pl.BlockSpec((some, heads, width), lambda n: (n, 0, 0)),
            pl.BlockSpec((2, some, key_heads, width), lambda n: (0, n, 0, 0)),
        ],
        out_specs=list(specs) + [smem()],
        out_shape=list(shapes) + [jax.ShapeDtypeStruct((SCALARS,), jnp.int32)],
        scratch_shapes=[
            pltpu.VMEM((heads, some, width), queries.dtype),
            pltpu.VMEM((2, key_heads, some, width), queries.dtype),
        ],
        compiler_params=params(),
        cost_estimate=cost(0, 4 * (queries.size + states.size)),
    )(index, span_start, steered_heads, in_hbm(queries), in_hbm(states))


def raw_scores(query, key):
    return lax.dot_general(
        query, key, (((1,), (1,)), ((), ())), preferred_element_type=jnp.float32
    )


def weights(raw_score, bias, visible):
    score = jnp.tanh(raw_score * (SCORE_SCALE / SOFTCAP)) * (SOFTCAP * LOG2_E)
    weight = jnp.exp2(score if bias is None else score + bias)
    return weight if visible is None else jnp.where(visible, weight, 0.0)


def lane_sums(weight, lanes):
    sums = weight[:, :lanes]
    for first in range(lanes, weight.shape[1], lanes):
        sums = sums + weight[:, first : first + lanes]
    return sums


def attend_kernel(*refs, step, steerable, last, joined):
    refs = list(refs)
    scalars = refs.pop(0)
    bias_ref = refs.pop(0) if steerable else None
    low_ref, high_ref, states_ref = refs.pop(0), refs.pop(0), refs.pop(0)
    far_ref = refs.pop(0) if joined else None
    span_ref = refs.pop(0) if steerable and last else None
    if step:
        old_weighted, old_sums = refs.pop(0), refs.pop(0)
    if last:
        out_ref = refs.pop(0)
    weighted_ref, sums_ref, query_ref = refs[:3]
    around_ref, gathered_ref = refs[3:] if steerable and last else (None, None)
    low = pl.program_id(0)
    blocks, _, rows, width = states_ref.shape
    high = blocks - 1 - low
    plane = scalars[PLANE]
    first_block = (plane - step) * blocks
    query_ref[0] = low_ref[0].reshape(2 * rows, width)
    query_ref[1] = high_ref[0].reshape(2 * rows, width)
    if step:
        weighted_ref[...] = old_weighted[...]
        sums_ref[...] = old_sums[...]
    else:
        weighted_ref[...] = jnp.zeros(weighted_ref.shape, jnp.float32)
        sums_ref[...] = jnp.zeros(sums_ref.shape, jnp.float32)
    flags = [scalars[STEERED_0 + n] for n in range(2)]
    flag_values = [flag.astype(jnp.float32) for flag in flags]

    def states(part, key_block, count):
        if isinstance(key_block, tuple):
            return far_ref[key_block[0], part]
        if count == 1:
            return states_ref[key_block, part]
        return states_ref[pl.ds(key_block, count), part].reshape(count * rows, width)

    def bias(key_block, count):
        if not steerable:
            return None
        parts = [bias_ref[pl.ds(first_block + key_block + n, 1), :] for n in range(count)]
        row = parts[0] if count == 1 else jnp.concatenate(parts, axis=1)
        return [row * value for value in flag_values]

    def add(tiles):
        def of_span(key_block):
            return isinstance(key_block, int) and key_block < 0

        def part_of(part, key_block, count):
            if of_span(key_block):
                return gathered_ref[part, ~key_block]
            return states(part, key_block, count)

        def score(tile):
            which, key_block, count, _ = tile
            return raw_scores(query_ref[which], part_of(0, key_block, count))

        ahead = score(tiles[0])
        for n, (which, key_block, count, visible) in enumerate(tiles):
            raw_score = ahead
            if n + 1 < len(tiles):
                ahead = score(tiles[n + 1])
            added = None if of_span(key_block) else bias(key_block, count)
            chunk = CHUNK // count
            rounded = []
            for first in range(0, 2 * rows, chunk):
                head, row = first // rows, first % rows
                columns = slice(0, count * rows)
                if visible is in_order:
                    columns = slice(0, -(-(row + chunk) // width) * width)
                    if step:
                        columns = slice(row // width * width, rows)
                weight = weights(
                    raw_score[first : first + chunk, columns],
                    None if added is None else added[head][:, columns],
                    None if visible is None else visible(head, row, chunk)[:, columns],
                )
                some = pl.ds(first, chunk)
                sums_ref[0, which, some, :] += lane_sums(weight, width)
                weight = weight.astype(jnp.bfloat16)
                sides = [
                    jnp.zeros((chunk, size), jnp.bfloat16)
                    for size in (columns.start, count * rows - columns.stop)
                ]
                parts = [part for part in (sides[0], weight, sides[1]) if part.shape[1]]
                rounded.append(parts[0] if len(parts) == 1 else jnp.concatenate(parts, axis=1))
            weighted_ref[0, which] += jnp.dot(
                jnp.concatenate(rounded, axis=0),
                part_of(1, key_block, count),
                preferred_element_type=jnp.float32,
            )

    def gather_span():
        start = scalars[SPAN_FIRST] - first_block * rows
        pad = SPAN // rows
        for part in range(2):
            before = span_ref[part].astype(jnp.float32)

            @pl.when(start < 0)
            def _():
                around_ref[:SPAN, :] = before
                for n in range(2):
                    around_ref[SPAN + n * rows : SPAN + (n + 1) * rows, :] = states_ref[
                        n, part
                    ].astype(jnp.float32)

            block = jnp.clip(lax.div(jnp.maximum(start, 0), rows), 0, blocks - pad - 1)

            @pl.when(start >= 0)
            def _():
                for n in range(pad + 1):
                    around_ref[n * rows : (n + 1) * rows, :] = states_ref[
                        block + n, part
                    ].astype(jnp.float32)
                around_ref[(pad + 1) * rows :, :] = jnp.zeros((SPAN, width), jnp.float32)

            offset = jnp.where(start < 0, jnp.maximum(start + SPAN, 0), start - block * rows)
            for n in range(pad):
                gathered_ref[part, n] = around_ref[pl.ds(offset + n * rows, rows), :].astype(
                    jnp.bfloat16
                )

    def ranks(row, count):
        shape = (count, rows)
        return (
            row
            + lax.broadcasted_iota(jnp.int32, shape, 0)
            - lax.broadcasted_iota(jnp.int32, shape, 1)
        )

    def in_order(head, row, count):
        return ranks(row, count) >= 0 if step == 0 else ranks(row, count) < 0

    def span_tiles():
        tiles = []
        for which, block in ((0, low), (1, high)):
            for n in range(SPAN // rows):
                nearest = scalars[SPAN_FIRST] + n * rows + WINDOW - (plane * blocks + block) * rows
                least = [jnp.where(flag == 1, nearest, 2 * rows) for flag in flags]

                def visible(head, row, count, least=least):
                    return ranks(row, count) >= least[head]

                tiles.append((which, ~n, 1, visible))
        return tiles

    def triangle(own):
        tiles = []
        for n in range(blocks - 1):
            if own:
                is_low = n < low
                tiles.append((jnp.where(is_low, 0, 1), jnp.where(is_low, n, n - low), 1, None))
            else:
                is_high = n < low
                tiles.append(
                    (jnp.where(is_high, 1, 0), jnp.where(is_high, high + 1 + n, n + 1), 1, None)
                )
        return tiles + [(0, low, 1, in_order), (1, high, 1, in_order)]

    def compute():
        if step == 1:
            tiles = [(which, n, 2, None) for which in range(2) for n in range(0, blocks, 2)]
            if not joined:
                add(tiles)
                return
            far = [(which, (n,), count, seen) for which, n, count, seen in triangle(False)]
            pl.when(plane == step)(lambda: add(tiles))
            pl.when(plane > step)(lambda: add(tiles + far))
            return
        tiles = triangle(step == 0)
        if not (steerable and last):
            add(tiles)
            return
        wanted = flags[0] + flags[1] > 0
        wanted = wanted & (scalars[SPAN_FIRST] < (first_block + blocks) * rows)
        pl.when(wanted & (low == 0))(gather_span)
        pl.when(wanted)(lambda: add(tiles + span_tiles()))
        pl.when(jnp.logical_not(wanted))(lambda: add(tiles))

    if step:
        pl.when(plane >= step)(compute)
    else:
        compute()
    if last:
        write_result(out_ref, weighted_ref, sums_ref, low, high)


def write_result(out_ref, weighted_ref, sums_ref, low, high):
    for which, block in ((0, low), (1, high)):
        total = jnp.sum(sums_ref[0, which], axis=-1, keepdims=True)
        result = (weighted_ref[0, which] / total).astype(out_ref.dtype)
        out_ref[block] = result.reshape(out_ref.shape[1:])


def query_specs(queries):
    blocks, parts, rows, width = queries.shape
    one, at = (1, 2, rows, width), parts // 2 - 1
    return [
        pl.BlockSpec(one, lambda n: (n, at, 0, 0)),
        pl.BlockSpec(one, lambda n: (blocks - 1 - n, at, 0, 0)),
    ]


def held_spec(queries):
    _, _, rows, width = queries.shape
    return pl.BlockSpec((1, 2, 2 * rows, width), lambda n: (n, 0, 0, 0))


def attend(
    step, scalars, bias, queries, states, carried=None, far_states=None, span_states=None,
    last=False, states_at=0,
):
    blocks, _, rows, width = queries.shape
    pair = 2
    assert blocks % 2 == 0
    held = pltpu.HBM((blocks // 2, 2, pair * rows, width), jnp.float32)
    whole = pl.BlockSpec((blocks, 2, rows, width), lambda n: (0, states_at, 0, 0))
    operands, in_specs = [scalars], [smem()]
    if bias is not None:
        operands.append(bias)
        in_specs.append(pl.BlockSpec(bias.shape, lambda n: (0, 0)))
    operands += [queries, queries, states]
    in_specs += query_specs(queries) + [whole]
    if far_states is not None:
        operands.append(far_states)
        in_specs.append(pl.BlockSpec(far_states.shape, lambda n: (0, 0, 0, 0)))
    if span_states is not None:
        operands.append(span_states)
        in_specs.append(pl.BlockSpec(span_states.shape, lambda n: (0, 0, 0)))
    if carried is not None:
        operands += [in_hbm(sums) for sums in carried]
        in_specs += [held_spec(queries)] * 2
    scratch = [pltpu.VMEM((2, pair * rows, width), queries.dtype)]
    if span_states is not None:
        scratch.append(pltpu.VMEM((2 * SPAN + rows, width), jnp.float32))
        scratch.append(pltpu.VMEM((2, SPAN // rows, rows, width), queries.dtype))
    if last:
        out_shape = jax.ShapeDtypeStruct((blocks, pair, rows, width), queries.dtype)
        out_specs = pl.BlockSpec(out_shape.shape, lambda n: (0, 0, 0, 0))
        scratch = [pltpu.VMEM((1, 2, pair * rows, width), jnp.float32)] * 2 + scratch
    else:
        out_shape, out_specs = [held, held], [held_spec(queries)] * 2
    return pl.pallas_call(
        functools.partial(
            attend_kernel,
            step=step,
            steerable=bias is not None,
            last=last,
            joined=far_states is not None,
        ),
        grid=(blocks // 2,),
        in_specs=in_specs,
        out_specs=out_specs,
        out_shape=out_shape,
        scratch_shapes=scratch,
        compiler_params=params(),
        cost_estimate=cost(
            pair * (blocks * rows) ** 2 * (16 if step == 1 and bias is not None else 1) / 2,
            8 * queries.size + 8 * pair * blocks * rows * width,
        ),
    )(*operands)


def unpack_kernel(scalars, out_a, out_b, attention, heads_ref):
    for n in range(GROUP):
        for group_head in range(2):
            heads_ref[2 * scalars[n] + group_head] = out_a[n, group_head]
            heads_ref[2 * scalars[GROUP + n] + group_head] = out_b[n, group_head]
    attention[...] = jnp.transpose(heads_ref[...], (1, 0, 2))


def unpack(scalars, out_a, out_b):
    blocks, pair, rows, width = out_a.shape
    heads = 2 * blocks * pair
    return pl.pallas_call(
        unpack_kernel,
        in_specs=[smem(), vmem(), vmem()],
        out_specs=vmem(),
        out_shape=jax.ShapeDtypeStruct((rows, heads, width), out_a.dtype),
        scratch_shapes=[pltpu.VMEM((heads, rows, width), out_a.dtype)],
        compiler_params=params(),
        cost_estimate=cost(0, 8 * out_a.size),
    )(scalars, out_a, out_b)


def per_device(queries, key_value, damping, span_start, steered_heads):
    rows = queries.shape[0]
    device_count = lax.axis_size("seq")
    assert WINDOW == 2 * GROUP * rows and device_count == 4 * GROUP
    assert key_value.shape[2] == 2 * GROUP and queries.shape[1] == 4 * GROUP
    assert steered_heads.shape[0] <= GROUP
    groups = [
        list(range(first, first + GROUP)) for first in range(0, device_count, GROUP)
    ]

    def exchange(blocks):
        return lax.all_to_all(
            blocks, "seq", split_axis=0, concat_axis=0, axis_index_groups=groups, tiled=True
        )

    def onward(blocks, planes=1):
        shift = planes * GROUP
        pairs = [(n, n + shift) for n in range(device_count - shift)]
        return lax.ppermute(blocks, "seq", pairs)

    def after(value, earlier):
        return lax.optimization_barrier((value, earlier))[0]

    index = lax.axis_index("seq").astype(jnp.int32).reshape(1)
    both_a, states_b, all_b, scalars = pack(
        index, span_start, steered_heads, queries, key_value
    )
    position = jnp.arange(damping.shape[0], dtype=jnp.int32)
    emphasized = (position >= span_start[0]) & (position < span_start[0] + SPAN)
    bias = jnp.where(emphasized, 0.0, jnp.log2(damping.astype(jnp.float32)))
    bias = bias.reshape(-1, rows)

    raw_b = onward(states_b)
    both_a = exchange(both_a)
    states_a = both_a[:, :2]
    back_a = onward(after(states_a, raw_b))
    held_a = attend(0, scalars, bias, after(both_a, raw_b), both_a)
    all_b = lax.dynamic_update_slice(all_b, after(raw_b, states_a), (0, 0, 0, 0))
    all_b = exchange(all_b)
    far_a = onward(after(back_a, held_a))
    length = GROUP * rows
    span_states = lax.dynamic_slice_in_dim(
        after(both_a, (back_a, held_a))[:, :2].transpose(1, 0, 2, 3).reshape(2, length, -1),
        jnp.minimum(span_start[0], length - SPAN),
        SPAN,
        1,
    )
    span_states = onward(span_states, 3)
    held_a = attend(1, scalars, bias, both_a, back_a, held_a)
    all_b = after(all_b, held_a)
    far_b = onward(all_b[:, :2])
    held_b = attend(0, scalars, None, all_b, all_b, states_at=1)
    out_a = attend(
        2, scalars, bias, both_a, far_a, after(held_a, held_b), span_states=span_states, last=True
    )
    held_b = after(held_b, out_a)
    out_a = exchange(out_a)
    out_b = attend(1, scalars, None, all_b, all_b, held_b, far_states=far_b, last=True)
    out_b = exchange(out_b)
    return unpack(scalars, out_a, out_b)


def solution(mesh):
    in_specs = (
        P(("prompt", "seq"), None, None),
        P(None, ("prompt", "seq"), None, None),
        P("prompt"),
        P("prompt"),
        P(),
    )
    out_specs = P(("prompt", "seq"), None, None)
    return jax.shard_map(
        per_device, mesh=mesh, in_specs=in_specs, out_specs=out_specs, check_vma=False
    )
```

```python
import functools
import math

import jax
import jax.numpy as jnp
from jax import lax
from jax.experimental import pallas as pl
from jax.experimental.pallas import tpu as pltpu
from jax.sharding import PartitionSpec as P

WINDOW = 4096
SPAN = 512

SCORE_SCALE = 144.0 ** (-0.5)
SOFTCAP = 50.0
LOG2_E = math.log2(math.e)

GROUP = 8
CHUNK = 64
TOKEN_STEPS = 4
PAIR_FLOPS = 256
VMEM_BYTES = 48 * 1024 * 1024

FIRST_SCALAR = 32
PLANE, SPAN_FIRST, STEERED_0, STEERED_1 = range(FIRST_SCALAR, FIRST_SCALAR + 4)
SCALARS = FIRST_SCALAR + 4


def smem():
    return pl.BlockSpec(memory_space=pltpu.SMEM)


def vmem():
    return pl.BlockSpec(memory_space=pltpu.VMEM)


def in_hbm(operand):
    return pltpu.with_memory_space_constraint(operand, pltpu.HBM)


def params():
    return pltpu.CompilerParams(vmem_limit_bytes=VMEM_BYTES)


def cost(pairs, moved):
    return pl.CostEstimate(
        flops=int(pairs * PAIR_FLOPS), bytes_accessed=int(moved), transcendentals=int(2 * pairs)
    )


def pack_kernel(
    index_ref, span_ref, steered_ref, queries_ref, states_ref,
    both_a, states_b, all_b, scalars, query_heads, state_heads,
):
    key_heads = states_ref.shape[2]
    steered_count = steered_ref.shape[0]

    @pl.when(pl.program_id(0) == 0)
    def _():
        steered_keys = [lax.div(steered_ref[n], 2) for n in range(steered_count)]
        flags = []
        for head in range(key_heads):
            hit = steered_keys[0] == head
            for n in range(1, steered_count):
                hit = hit | (steered_keys[n] == head)
            flags.append(hit.astype(jnp.int32))
        total = sum(flags[1:], flags[0])
        before = jnp.int32(0)
        for head in range(key_heads):
            rank = jnp.where(flags[head] == 1, before, total + head - before)
            scalars[rank] = jnp.int32(head)
            before = before + flags[head]
        place = lax.rem(index_ref[0], GROUP)
        scalars[PLANE] = lax.div(index_ref[0], GROUP)
        scalars[SPAN_FIRST] = span_ref[0]
        own_head = scalars[place]
        for group_head in range(2):
            hit = steered_ref[0] == 2 * own_head + group_head
            for n in range(1, steered_count):
                hit = hit | (steered_ref[n] == 2 * own_head + group_head)
            scalars[STEERED_0 + group_head] = hit.astype(jnp.int32)

    for part in range(2):
        state_heads[part] = jnp.transpose(states_ref[part], (1, 0, 2))
        for n in range(GROUP):
            both_a[n, part] = state_heads[part, scalars[n]]
            state = state_heads[part, scalars[GROUP + n]]
            states_b[n, part] = state
            all_b[n, 2 + part] = state
    query_heads[...] = jnp.transpose(queries_ref[...], (1, 0, 2))
    for n in range(GROUP):
        for group_head in range(2):
            both_a[n, 2 + group_head] = query_heads[2 * scalars[n] + group_head]
            all_b[n, 4 + group_head] = query_heads[2 * scalars[GROUP + n] + group_head]


def pack(index, span_start, steered_heads, queries, states):
    rows, heads, width = queries.shape
    key_heads = states.shape[2]
    some = rows // TOKEN_STEPS


    def sent(parts):
        shape = pltpu.HBM((GROUP, parts, rows, width), queries.dtype)
        return shape, pl.BlockSpec((GROUP, parts, some, width), lambda n: (0, 0, n, 0))

    shapes, specs = zip(sent(4), sent(2), sent(6))
    return pl.pallas_call(
        pack_kernel,
        grid=(TOKEN_STEPS,),
        in_specs=[smem()] * 3
        + [
            pl.BlockSpec((some, heads, width), lambda n: (n, 0, 0)),
            pl.BlockSpec((2, some, key_heads, width), lambda n: (0, n, 0, 0)),
        ],
        out_specs=list(specs) + [smem()],
        out_shape=list(shapes) + [jax.ShapeDtypeStruct((SCALARS,), jnp.int32)],
        scratch_shapes=[
            pltpu.VMEM((heads, some, width), queries.dtype),
            pltpu.VMEM((2, key_heads, some, width), queries.dtype),
        ],
        compiler_params=params(),
        cost_estimate=cost(0, 4 * (queries.size + states.size)),
    )(index, span_start, steered_heads, in_hbm(queries), in_hbm(states))


def raw_scores(query, key):
    return lax.dot_general(
        query, key, (((1,), (1,)), ((), ())), preferred_element_type=jnp.float32
    )


def weights(raw_score, bias, visible):
    score = jnp.tanh(raw_score * (SCORE_SCALE / SOFTCAP)) * (SOFTCAP * LOG2_E)
    weight = jnp.exp2(score if bias is None else score + bias)
    return weight if visible is None else jnp.where(visible, weight, 0.0)


def lane_sums(weight, lanes):
    sums = weight[:, :lanes]
    for first in range(lanes, weight.shape[1], lanes):
        sums = sums + weight[:, first : first + lanes]
    return sums


def attend_kernel(*refs, step, steerable, last, joined):
    refs = list(refs)
    scalars = refs.pop(0)
    bias_ref = refs.pop(0) if steerable else None
    low_ref, high_ref, states_ref = refs.pop(0), refs.pop(0), refs.pop(0)
    far_ref = refs.pop(0) if joined else None
    span_ref = refs.pop(0) if steerable and last else None
    if step:
        old_weighted, old_sums = refs.pop(0), refs.pop(0)
    if last:
        out_ref = refs.pop(0)
    weighted_ref, sums_ref, query_ref = refs[:3]
    around_ref, gathered_ref = refs[3:] if steerable and last else (None, None)
    low = pl.program_id(0)
    blocks, _, rows, width = states_ref.shape
    high = blocks - 1 - low
    plane = scalars[PLANE]
    first_block = (plane - step) * blocks
    query_ref[0] = low_ref[0].reshape(2 * rows, width)
    query_ref[1] = high_ref[0].reshape(2 * rows, width)
    if step:
        weighted_ref[...] = old_weighted[...]
        sums_ref[...] = old_sums[...]
    else:
        weighted_ref[...] = jnp.zeros(weighted_ref.shape, jnp.float32)
        sums_ref[...] = jnp.zeros(sums_ref.shape, jnp.float32)
    flags = [scalars[STEERED_0 + n] for n in range(2)]
    flag_values = [flag.astype(jnp.float32) for flag in flags]

    def states(part, key_block, count):
        if isinstance(key_block, tuple):
            return far_ref[key_block[0], part]
        if count == 1:
            return states_ref[key_block, part]
        return states_ref[pl.ds(key_block, count), part].reshape(count * rows, width)

    def bias(key_block, count):
        if not steerable:
            return None
        parts = [bias_ref[pl.ds(first_block + key_block + n, 1), :] for n in range(count)]
        row = parts[0] if count == 1 else jnp.concatenate(parts, axis=1)
        return [row * value for value in flag_values]

    def add(tiles):
        def of_span(key_block):
            return isinstance(key_block, int) and key_block < 0

        def part_of(part, key_block, count):
            if of_span(key_block):
                return gathered_ref[part, ~key_block]
            return states(part, key_block, count)

        def score(tile):
            which, key_block, count, _ = tile
            return raw_scores(query_ref[which], part_of(0, key_block, count))

        ahead = score(tiles[0])
        for n, (which, key_block, count, visible) in enumerate(tiles):
            raw_score = ahead
            if n + 1 < len(tiles):
                ahead = score(tiles[n + 1])
            added = None if of_span(key_block) else bias(key_block, count)
            chunk = CHUNK // count
            rounded = []
            for first in range(0, 2 * rows, chunk):
                head, row = first // rows, first % rows
                columns = slice(0, count * rows)
                if visible is in_order:
                    columns = slice(0, -(-(row + chunk) // width) * width)
                    if step:
                        columns = slice(row // width * width, rows)
                weight = weights(
                    raw_score[first : first + chunk, columns],
                    None if added is None else added[head][:, columns],
                    None if visible is None else visible(head, row, chunk)[:, columns],
                )
                some = pl.ds(first, chunk)
                sums_ref[0, which, some, :] += lane_sums(weight, width)
                weight = weight.astype(jnp.bfloat16)
                sides = [
                    jnp.zeros((chunk, size), jnp.bfloat16)
                    for size in (columns.start, count * rows - columns.stop)
                ]
                parts = [part for part in (sides[0], weight, sides[1]) if part.shape[1]]
                rounded.append(parts[0] if len(parts) == 1 else jnp.concatenate(parts, axis=1))
            weighted_ref[0, which] += jnp.dot(
                jnp.concatenate(rounded, axis=0),
                part_of(1, key_block, count),
                preferred_element_type=jnp.float32,
            )

    def gather_span():
        start = scalars[SPAN_FIRST] - first_block * rows
        pad = SPAN // rows
        for part in range(2):
            before = span_ref[part].astype(jnp.float32)

            @pl.when(start < 0)
            def _():
                around_ref[:SPAN, :] = before
                for n in range(2):
                    around_ref[SPAN + n * rows : SPAN + (n + 1) * rows, :] = states_ref[
                        n, part
                    ].astype(jnp.float32)

            block = jnp.clip(lax.div(jnp.maximum(start, 0), rows), 0, blocks - pad - 1)

            @pl.when(start >= 0)
            def _():
                for n in range(pad + 1):
                    around_ref[n * rows : (n + 1) * rows, :] = states_ref[
                        block + n, part
                    ].astype(jnp.float32)
                around_ref[(pad + 1) * rows :, :] = jnp.zeros((SPAN, width), jnp.float32)

            offset = jnp.where(start < 0, jnp.maximum(start + SPAN, 0), start - block * rows)
            for n in range(pad):
                gathered_ref[part, n] = around_ref[pl.ds(offset + n * rows, rows), :].astype(
                    jnp.bfloat16
                )

    def ranks(row, count):
        shape = (count, rows)
        return (
            row
            + lax.broadcasted_iota(jnp.int32, shape, 0)
            - lax.broadcasted_iota(jnp.int32, shape, 1)
        )

    def in_order(head, row, count):
        return ranks(row, count) >= 0 if step == 0 else ranks(row, count) < 0

    def span_tiles():
        tiles = []
        for which, block in ((0, low), (1, high)):
            for n in range(SPAN // rows):
                nearest = scalars[SPAN_FIRST] + n * rows + WINDOW - (plane * blocks + block) * rows
                least = [jnp.where(flag == 1, nearest, 2 * rows) for flag in flags]

                def visible(head, row, count, least=least):
                    return ranks(row, count) >= least[head]

                tiles.append((which, ~n, 1, visible))
        return tiles

    def triangle(own):
        tiles = []
        for n in range(blocks - 1):
            if own:
                is_low = n < low
                tiles.append((jnp.where(is_low, 0, 1), jnp.where(is_low, n, n - low), 1, None))
            else:
                is_high = n < low
                tiles.append(
                    (jnp.where(is_high, 1, 0), jnp.where(is_high, high + 1 + n, n + 1), 1, None)
                )
        return tiles + [(0, low, 1, in_order), (1, high, 1, in_order)]

    def compute():
        if step == 1:
            tiles = [(which, n, 2, None) for which in range(2) for n in range(0, blocks, 2)]
            if not joined:
                add(tiles)
                return
            far = [(which, (n,), count, seen) for which, n, count, seen in triangle(False)]
            pl.when(plane == step)(lambda: add(tiles))
            pl.when(plane > step)(lambda: add(tiles + far))
            return
        tiles = triangle(step == 0)
        if not (steerable and last):
            add(tiles)
            return
        wanted = flags[0] + flags[1] > 0
        wanted = wanted & (scalars[SPAN_FIRST] < (first_block + blocks) * rows)
        pl.when(wanted & (low == 0))(gather_span)
        pl.when(wanted)(lambda: add(tiles + span_tiles()))
        pl.when(jnp.logical_not(wanted))(lambda: add(tiles))

    if step:
        pl.when(plane >= step)(compute)
    else:
        compute()
    if last:
        write_result(out_ref, weighted_ref, sums_ref, low, high)


def write_result(out_ref, weighted_ref, sums_ref, low, high):
    for which, block in ((0, low), (1, high)):
        total = jnp.sum(sums_ref[0, which], axis=-1, keepdims=True)
        result = (weighted_ref[0, which] / total).astype(out_ref.dtype)
        out_ref[block] = result.reshape(out_ref.shape[1:])


def query_specs(queries):
    blocks, parts, rows, width = queries.shape
    one, at = (1, 2, rows, width), parts // 2 - 1
    return [
        pl.BlockSpec(one, lambda n: (n, at, 0, 0)),
        pl.BlockSpec(one, lambda n: (blocks - 1 - n, at, 0, 0)),
    ]


def held_spec(queries):
    _, _, rows, width = queries.shape
    return pl.BlockSpec((1, 2, 2 * rows, width), lambda n: (n, 0, 0, 0))


def attend(
    step, scalars, bias, queries, states, carried=None, far_states=None, span_states=None,
    last=False, states_at=0,
):
    blocks, _, rows, width = queries.shape
    pair = 2
    assert blocks % 2 == 0
    held = pltpu.HBM((blocks // 2, 2, pair * rows, width), jnp.float32)
    whole = pl.BlockSpec((blocks, 2, rows, width), lambda n: (0, states_at, 0, 0))
    operands, in_specs = [scalars], [smem()]
    if bias is not None:
        operands.append(bias)
        in_specs.append(pl.BlockSpec(bias.shape, lambda n: (0, 0)))
    operands += [queries, queries, states]
    in_specs += query_specs(queries) + [whole]
    if far_states is not None:
        operands.append(far_states)
        in_specs.append(pl.BlockSpec(far_states.shape, lambda n: (0, 0, 0, 0)))
    if span_states is not None:
        operands.append(span_states)
        in_specs.append(pl.BlockSpec(span_states.shape, lambda n: (0, 0, 0)))
    if carried is not None:
        operands += [in_hbm(sums) for sums in carried]
        in_specs += [held_spec(queries)] * 2
    scratch = [pltpu.VMEM((2, pair * rows, width), queries.dtype)]
    if span_states is not None:
        scratch.append(pltpu.VMEM((2 * SPAN + rows, width), jnp.float32))
        scratch.append(pltpu.VMEM((2, SPAN // rows, rows, width), queries.dtype))
    if last:
        out_shape = jax.ShapeDtypeStruct((blocks, pair, rows, width), queries.dtype)
        out_specs = pl.BlockSpec(out_shape.shape, lambda n: (0, 0, 0, 0))
        scratch = [pltpu.VMEM((1, 2, pair * rows, width), jnp.float32)] * 2 + scratch
    else:
        out_shape, out_specs = [held, held], [held_spec(queries)] * 2
    return pl.pallas_call(
        functools.partial(
            attend_kernel,
            step=step,
            steerable=bias is not None,
            last=last,
            joined=far_states is not None,
        ),
        grid=(blocks // 2,),
        in_specs=in_specs,
        out_specs=out_specs,
        out_shape=out_shape,
        scratch_shapes=scratch,
        compiler_params=params(),
        cost_estimate=cost(
            pair * (blocks * rows) ** 2 * (16 if step == 1 and bias is not None else 1) / 2,
            8 * queries.size + 8 * pair * blocks * rows * width,
        ),
    )(*operands)


def copy_parts(source_of, target_of, sems):
    copies = [
        pltpu.make_async_copy(source_of(n), target_of(n), sems.at[n]) for n in range(GROUP)
    ]
    for copy in copies:
        copy.start()
    for copy in copies:
        copy.wait()


def insert_kernel(parts_ref, whole_ref, result_ref, sems):
    del whole_ref
    copy_parts(lambda n: parts_ref.at[n], lambda n: result_ref.at[n, pl.ds(0, 2)], sems)


def insert_parts(parts, whole):
    return pl.pallas_call(
        insert_kernel,
        in_specs=[pl.BlockSpec(memory_space=pltpu.HBM)] * 2,
        out_specs=pl.BlockSpec(memory_space=pltpu.HBM),
        out_shape=pltpu.HBM(whole.shape, whole.dtype),
        input_output_aliases={1: 0},
        scratch_shapes=[pltpu.SemaphoreType.DMA((GROUP,))],
        compiler_params=params(),
        cost_estimate=cost(0, 2 * parts.size),
    )(parts, whole)


def take_kernel(whole_ref, parts_ref, sems):
    copy_parts(lambda n: whole_ref.at[n, pl.ds(0, 2)], lambda n: parts_ref.at[n], sems)


def take_parts(whole):
    blocks, _, rows, width = whole.shape
    return pl.pallas_call(
        take_kernel,
        in_specs=[pl.BlockSpec(memory_space=pltpu.HBM)],
        out_specs=pl.BlockSpec(memory_space=pltpu.HBM),
        out_shape=pltpu.HBM((blocks, 2, rows, width), whole.dtype),
        scratch_shapes=[pltpu.SemaphoreType.DMA((GROUP,))],
        compiler_params=params(),
        cost_estimate=cost(0, 2 * blocks * 2 * rows * width),
    )(whole)


def unpack_kernel(scalars, out_a, out_b, attention, heads_ref):
    for n in range(GROUP):
        for group_head in range(2):
            heads_ref[2 * scalars[n] + group_head] = out_a[n, group_head]
            heads_ref[2 * scalars[GROUP + n] + group_head] = out_b[n, group_head]
    attention[...] = jnp.transpose(heads_ref[...], (1, 0, 2))


def unpack(scalars, out_a, out_b):
    blocks, pair, rows, width = out_a.shape
    heads = 2 * blocks * pair
    return pl.pallas_call(
        unpack_kernel,
        in_specs=[smem(), vmem(), vmem()],
        out_specs=vmem(),
        out_shape=jax.ShapeDtypeStruct((rows, heads, width), out_a.dtype),
        scratch_shapes=[pltpu.VMEM((heads, rows, width), out_a.dtype)],
        compiler_params=params(),
        cost_estimate=cost(0, 8 * out_a.size),
    )(scalars, out_a, out_b)


def per_device(queries, key_value, damping, span_start, steered_heads):
    rows = queries.shape[0]
    device_count = lax.axis_size("seq")
    assert WINDOW == 2 * GROUP * rows and device_count == 4 * GROUP
    assert key_value.shape[2] == 2 * GROUP and queries.shape[1] == 4 * GROUP
    assert steered_heads.shape[0] <= GROUP
    groups = [
        list(range(first, first + GROUP)) for first in range(0, device_count, GROUP)
    ]

    def exchange(blocks):
        return lax.all_to_all(
            blocks, "seq", split_axis=0, concat_axis=0, axis_index_groups=groups, tiled=True
        )

    def onward(blocks, planes=1):
        shift = planes * GROUP
        pairs = [(n, n + shift) for n in range(device_count - shift)]
        return lax.ppermute(blocks, "seq", pairs)

    def after(value, earlier):
        return lax.optimization_barrier((value, earlier))[0]

    index = lax.axis_index("seq").astype(jnp.int32).reshape(1)
    both_a, states_b, all_b, scalars = pack(
        index, span_start, steered_heads, queries, key_value
    )
    position = jnp.arange(damping.shape[0], dtype=jnp.int32)
    emphasized = (position >= span_start[0]) & (position < span_start[0] + SPAN)
    bias = jnp.where(emphasized, 0.0, jnp.log2(damping.astype(jnp.float32)))
    bias = bias.reshape(-1, rows)

    raw_b = onward(states_b)
    both_a = exchange(both_a)
    states_a = both_a[:, :2]
    back_a = onward(after(states_a, raw_b))
    held_a = attend(0, scalars, bias, after(both_a, raw_b), both_a)
    all_b = insert_parts(after(raw_b, states_a), all_b)
    all_b = exchange(all_b)
    far_a = onward(after(back_a, held_a))
    length = GROUP * rows
    span_states = lax.dynamic_slice_in_dim(
        after(both_a, (back_a, held_a))[:, :2].transpose(1, 0, 2, 3).reshape(2, length, -1),
        jnp.minimum(span_start[0], length - SPAN),
        SPAN,
        1,
    )
    span_states = onward(span_states, 3)
    held_a = attend(1, scalars, bias, both_a, back_a, held_a)
    all_b = after(all_b, held_a)
    far_b = onward(take_parts(all_b))
    held_b = attend(0, scalars, None, all_b, all_b, states_at=1)
    out_a = attend(
        2, scalars, bias, both_a, far_a, after(held_a, held_b), span_states=span_states, last=True
    )
    held_b = after(held_b, out_a)
    out_a = exchange(out_a)
    out_b = attend(1, scalars, None, all_b, all_b, held_b, far_states=far_b, last=True)
    out_b = exchange(out_b)
    return unpack(scalars, out_a, out_b)


def solution(mesh):
    in_specs = (
        P(("prompt", "seq"), None, None),
        P(None, ("prompt", "seq"), None, None),
        P("prompt"),
        P("prompt"),
        P(),
    )
    out_specs = P(("prompt", "seq"), None, None)
    return jax.shard_map(
        per_device, mesh=mesh, in_specs=in_specs, out_specs=out_specs, check_vma=False
    )
```
